128 devices in a mesh: fsdp: 16 (over y, z), ctx: 4 (over x_lo, core), tp: 2 (over x_hi).
Axes of the slice: x: 4 (x_hi: 2, x_lo: 2; x = x_hi * 2 + x_lo), y: 4, z: 4, core: 2. Of those that a mesh axis runs over, the one named last changes fastest.
Arguments:
- tokens: bfloat16 [16384, 1536], P(('fsdp', 'ctx')), may hold values from -16 to 16
- segments: int32 [4, 4096], replicated, may hold values from 0 to 3, as said below
- w_query: bfloat16 [1536, 1536], P('fsdp', 'tp'), may hold values from -0.15625 to 0.15625
- key_matrix: bfloat16 [1536, 256], P('fsdp', 'tp'), may hold values from -0.15625 to 0.15625
- value_matrix: bfloat16 [1536, 256], P('fsdp', 'tp'), may hold values from -0.15625 to 0.15625
- b_query: bfloat16 [1536], P('tp'), may hold values from -3 to 3
- key_bias_vector: bfloat16 [256], P('tp'), may hold values from -3 to 3
- value_bias_vector: bfloat16 [256], P('tp'), may hold values from -3 to 3
- w_out: bfloat16 [1536, 1536], P('tp', 'fsdp'), may hold values from -0.875 to 0.875
- norm_attn: bfloat16 [1536], replicated, may hold values from 0.5 to 1.5
- norm_ffn: bfloat16 [1536], replicated, may hold values from 0.5 to 1.5
- w_gate: bfloat16 [1536, 8960], P('fsdp', 'tp'), may hold values from -0.15625 to 0.15625
- w_up: bfloat16 [1536, 8960], P('fsdp', 'tp'), may hold values from -0.15625 to 0.15625
- w_down: bfloat16 [8960, 1536], P('tp', 'fsdp'), may hold values from -0.0625 to 0.0625
- cotangent: bfloat16 [16384, 1536], P(('fsdp', 'ctx')), may hold values from -16 to 16
Outputs:
- output: bfloat16 [16384, 1536], P(('fsdp', 'ctx'))
- grad_tokens: float32 [16384, 1536], P(('fsdp', 'ctx'))
- grad_query: float32 [1536, 1536], P(('fsdp', 'ctx'), 'tp')
- grad_key: float32 [1536, 256], P(('fsdp', 'ctx'), 'tp')
- grad_value: float32 [1536, 256], P(('fsdp', 'ctx'), 'tp')
- grad_query_bias: float32 [12, 128], P('tp', ('fsdp', 'ctx'))
- grad_key_bias: float32 [2, 128], P('tp', ('fsdp', 'ctx'))
- grad_value_bias: float32 [2, 128], P('tp', ('fsdp', 'ctx'))
- grad_out_proj: float32 [1536, 1536], P('tp', ('fsdp', 'ctx'))
- grad_norm_attn: float32 [1536], P(('fsdp', 'ctx'))
- grad_norm_ffn: float32 [1536], P(('fsdp', 'ctx'))
- grad_gate: float32 [1536, 8960], P(('fsdp', 'ctx'), 'tp')
- grad_up: float32 [1536, 8960], P(('fsdp', 'ctx'), 'tp')
- grad_down: float32 [8960, 1536], P('tp', ('fsdp', 'ctx'))
The draws below stay inside these ranges and needn't reach their ends.
Inputs may be any that keep to these rules, and one draw needn't show every extreme that they name: `segments`: in each of the 4 sequences segment numbers start at 0 and rise by at most one from one token to the next. In every draw one sequence, chosen by the seed, has three documents, the first ending and the last beginning within 256 tokens of the sequence's ends; where there are several sequences, another has four documents.
All inputs are finite; a program needn't handle non-finite values.
Results may differ from the reference program's by a relative error of at most 0.025.
Values may be sent and summed in bfloat16 or wider, within the bound.
A program may use at most 256 MiB of HBM per device.

```python
import math
import jax
import jax.numpy as jnp
from jax import lax

MODEL_WIDTH = 1536
QUERY_HEADS = 12
KEY_VALUE_HEADS = 2
HEAD_SIZE = 128
FF = 8960
TOK_DEV = 256
SEQUENCE_LENGTH = 4096
SEQUENCE_COUNT = 4
TOKENS = 16384


doc_breaks = 3


def draw_segments(key, part):
    key = jax.random.fold_in(key, 11)
    count_key, pick_key, full_key, place_key, head_key, tail_key = jax.random.split(key, 6)
    rows = jnp.arange(SEQUENCE_COUNT, dtype=jnp.int32)
    chosen = jax.random.randint(pick_key, (), 0, SEQUENCE_COUNT)
    other = (chosen + 1 + jax.random.randint(full_key, (), 0, max(SEQUENCE_COUNT - 1, 1))) % SEQUENCE_COUNT
    counts = jax.random.randint(count_key, (SEQUENCE_COUNT,), 0, doc_breaks + 1)
    counts = jnp.where(rows == other, doc_breaks, counts)
    counts = jnp.where(rows == chosen, 2, counts)
    row_keys = jax.random.split(place_key, SEQUENCE_COUNT)

    def pick_places(row_key):
        return jax.random.permutation(row_key, SEQUENCE_LENGTH - 1)[:doc_breaks] + 1
    places = jax.vmap(pick_places)(row_keys)
    head_break = jax.random.randint(head_key, (), 1, TOK_DEV)
    tail_break = jax.random.randint(tail_key, (), SEQUENCE_LENGTH - TOK_DEV + 1, SEQUENCE_LENGTH)
    chosen_places = jnp.stack([head_break, tail_break, head_break]).astype(jnp.int32)
    places = jnp.where((rows == chosen)[:, None], chosen_places[None, :], places.astype(jnp.int32))
    marks = (jnp.arange(doc_breaks)[None, :] < counts[:, None]).astype(jnp.int32)
    breaks = jnp.zeros((SEQUENCE_COUNT, SEQUENCE_LENGTH), jnp.int32).at[rows[:, None], places].max(marks)
    return jnp.cumsum(breaks, axis=1).astype(jnp.int32)


def with_spikes(entries, own_key, source, target, blocks, factor):
    owner, partner = [(jnp.arange(entries.shape[position]) // (entries.shape[position] // blocks)).reshape([-1 if axis == position else 1 for axis in range(entries.ndim)]) for position in (source, target)]
    chosen = jax.random.permutation(own_key, blocks)[partner]
    strong = (owner == chosen) | (owner == (partner + blocks // 2) % blocks)
    return jnp.where(strong, factor * entries, entries)


def block_scale(rng, shape, shards, smallest, largest):
    def one(axis_at, shards_of):
        heights = jax.random.uniform(jax.random.fold_in(jax.random.fold_in(rng, 6), axis_at), (shards_of,), jnp.float32, smallest / len(shards), largest / len(shards))
        return jnp.repeat(jnp.exp(heights), shape[axis_at] // shards_of).reshape((-1,) + (1,) * (len(shape) - axis_at - 1))

    loudness = one(*shards[0])
    for cut in shards[1:]:
        loudness = loudness * one(*cut)
    return loudness


def bell_draw(rng, shape, deviation, most, cuts=(), kind=jnp.bfloat16):
    factor_of = block_scale(rng, shape, cuts, -0.22, 0.18) if cuts else 1.0
    array = jax.random.normal(rng, shape, jnp.float32) * deviation * factor_of
    return jnp.minimum(jnp.maximum(array, -most), most).astype(kind)


def noise_with(stream_key, shape, spread, limit, shards, heavy, kind=jnp.bfloat16):
    array = spread * jax.random.normal(stream_key, shape, jnp.float32)
    if shards:
        array = array * block_scale(stream_key, shape, shards, -0.22, 0.18)
    return jnp.clip(with_spikes(array, jax.random.fold_in(stream_key, 3), *heavy), -limit, limit).astype(kind)


def setup_inputs(seed: int = 0) -> dict:
    seeds = jax.random.split(jax.random.key(seed), 16)
    return {
        "tokens": noise_with(seeds[0], (TOKENS, MODEL_WIDTH), 1.0, 16.0, ((0, 64),), (0, 1, 64, 4.0)),
        "segments": draw_segments(jax.random.fold_in(seeds[15], 71), 0),
        "w_query": bell_draw(seeds[2], (MODEL_WIDTH, QUERY_HEADS * HEAD_SIZE), MODEL_WIDTH ** -0.5, 0.15625, ((0, 16), (1, 2))),
        "key_matrix": bell_draw(seeds[3], (MODEL_WIDTH, KEY_VALUE_HEADS * HEAD_SIZE), MODEL_WIDTH ** -0.5, 0.15625, ((0, 16), (1, 2))),
        "value_matrix": bell_draw(seeds[4], (MODEL_WIDTH, KEY_VALUE_HEADS * HEAD_SIZE), MODEL_WIDTH ** -0.5, 0.15625, ((0, 16), (1, 2))),
        "b_query": bell_draw(seeds[5], (QUERY_HEADS * HEAD_SIZE,), 0.5, 3.0, ((0, 2),)),
        "key_bias_vector": bell_draw(seeds[6], (KEY_VALUE_HEADS * HEAD_SIZE,), 0.5, 3.0, ((0, 2),)),
        "value_bias_vector": bell_draw(seeds[7], (KEY_VALUE_HEADS * HEAD_SIZE,), 0.5, 3.0, ((0, 2),)),
        "w_out": bell_draw(seeds[8], (QUERY_HEADS * HEAD_SIZE, MODEL_WIDTH), (QUERY_HEADS * HEAD_SIZE // 32) ** -0.5, 0.875, ((0, 2), (1, 16))),
        "norm_attn": jnp.clip(1.0 + 0.1 * jax.random.normal(seeds[9], (MODEL_WIDTH,), jnp.float32), 0.5, 1.5).astype(jnp.bfloat16),
        "norm_ffn": jnp.clip(1.0 + 0.1 * jax.random.normal(seeds[10], (MODEL_WIDTH,), jnp.float32), 0.5, 1.5).astype(jnp.bfloat16),
        "w_gate": bell_draw(seeds[11], (MODEL_WIDTH, FF), MODEL_WIDTH ** -0.5, 0.15625, ((0, 16), (1, 2))),
        "w_up": bell_draw(seeds[12], (MODEL_WIDTH, FF), MODEL_WIDTH ** -0.5, 0.15625, ((0, 16), (1, 2))),
        "w_down": bell_draw(seeds[13], (FF, MODEL_WIDTH), FF ** -0.5, 0.0625, ((0, 2), (1, 16))),
        "cotangent": noise_with(seeds[14], (TOKENS, MODEL_WIDTH), 1.0, 16.0, ((0, 64),), (0, 1, 64, 4.0)),
    }


@jax.custom_vjp
def reduced_precision(v):
    return lax.optimization_barrier(v.astype(jnp.bfloat16)).astype(jnp.float32)

@jax.custom_vjp
def low_back(v):
    return v

def low_keep(v):
    return (reduced_precision(v), None)

def low_pass(kept, grad):
    return (grad,)

def back_keep(v):
    return (v, None)

def back_low(kept, grad):
    return (reduced_precision(grad),)
reduced_precision.defvjp(low_keep, low_pass)
low_back.defvjp(back_keep, back_low)
epsilon = 1e-06
rope_base = 1000000.0
masked_score = -1e+30

def doc_positions(seg_row):
    length_total = seg_row.shape[0]
    places = jnp.arange(length_total, dtype=jnp.int32)
    starts = jnp.concatenate([jnp.ones((1,), dtype=jnp.bool_), seg_row[1:] != seg_row[:-1]])
    begins = lax.cummax(jnp.where(starts, places, jnp.zeros_like(places)), axis=0)
    return (places - begins).astype(jnp.int32)

def apply_rotary(values_in, angle_pos, turning):
    half_size = values_in.shape[-1] // 2
    frequency = jnp.exp(jnp.arange(half_size, dtype=jnp.float32) * (-2.0 * math.log(rope_base) / values_in.shape[-1]))
    angles = angle_pos[:, None, None] * frequency
    cosine = jnp.cos(angles)
    sine_part = jnp.sin(angles) * turning
    front_half = values_in[..., :half_size]
    back_half = values_in[..., half_size:]
    return jnp.concatenate([front_half * cosine - back_half * sine_part, back_half * cosine + front_half * sine_part], axis=-1)

def product(left_side, right_side):
    return jnp.dot(left_side, right_side, precision=lax.Precision.HIGHEST, preferred_element_type=jnp.float32)

def normalize(tok_field, gains):
    factor = lax.rsqrt(lax.optimization_barrier(jnp.mean(tok_field * tok_field, axis=-1, keepdims=True)) + epsilon)
    return tok_field * factor * gains

def layer_sequence(weights, tok_field, seg_row):
    w_query, key_matrix, value_matrix, b_query, key_bias_vector, value_bias_vector, w_out, norm_attn, norm_ffn, w_gate, w_up, w_down = weights
    length_total = tok_field.shape[0]
    token_positions = doc_positions(seg_row).astype(jnp.float32)
    places = jnp.arange(length_total, dtype=jnp.int32)
    hidden_one = reduced_precision(normalize(tok_field, norm_attn))
    query_lin = low_back(product(hidden_one, w_query)) + b_query
    key_linear = low_back(product(hidden_one, key_matrix)) + key_bias_vector
    value_linear = low_back(product(hidden_one, value_matrix)) + value_bias_vector
    query_rotary = reduced_precision(apply_rotary(query_lin.reshape(length_total, QUERY_HEADS, HEAD_SIZE), token_positions, 1.0) * (1.0 / math.sqrt(HEAD_SIZE)))
    key_rotary = reduced_precision(apply_rotary(key_linear.reshape(length_total, KEY_VALUE_HEADS, HEAD_SIZE), token_positions, 1.0))
    value_rotary = reduced_precision(value_linear.reshape(length_total, KEY_VALUE_HEADS, HEAD_SIZE))
    block_rows = min(512, length_total)
    block_total = length_total // block_rows
    query_grouping = query_rotary.reshape(block_total, block_rows, KEY_VALUE_HEADS, QUERY_HEADS // KEY_VALUE_HEADS, HEAD_SIZE)

    def attend(block_pack):
        query_part, seg_part, place_part = block_pack
        visible = (seg_part[:, None] == seg_row[None, :]) & (places[None, :] <= place_part[:, None])
        scores = low_back(jnp.einsum('tgjd,sgd->gjts', query_part, key_rotary, precision=lax.Precision.HIGHEST))
        scores = jnp.where(visible[None, None], scores, masked_score)
        top_score = lax.optimization_barrier(jnp.max(scores, axis=-1, keepdims=True))
        raw_weights = jnp.exp(scores - top_score)
        probs = reduced_precision(raw_weights / lax.optimization_barrier(jnp.sum(raw_weights, axis=-1, keepdims=True)))
        return jnp.einsum('gjts,sgd->tgjd', probs, value_rotary, precision=lax.Precision.HIGHEST)
    attended = lax.map(jax.checkpoint(attend), (query_grouping, seg_row.reshape(block_total, block_rows), places.reshape(block_total, block_rows)))
    attended = reduced_precision(low_back(attended.reshape(length_total, QUERY_HEADS * HEAD_SIZE)))
    residual = tok_field + low_back(product(attended, w_out))
    hidden_two = reduced_precision(normalize(residual, norm_ffn))
    gate_val = low_back(product(hidden_two, w_gate))
    up_val = low_back(product(hidden_two, w_up))
    inner = reduced_precision(jax.nn.silu(gate_val) * up_val)
    return residual + low_back(product(inner, w_down))

def forward(weights, fields, segments):
    saved_layer = jax.checkpoint(layer_sequence)

    def one_sequence(seq_pair):
        return saved_layer(weights, seq_pair[0], seq_pair[1])
    return lax.map(one_sequence, (fields, segments))

def reference(tokens, segments, w_query, key_matrix, value_matrix, b_query, key_bias_vector, value_bias_vector, w_out, norm_attn, norm_ffn, w_gate, w_up, w_down, cotangent):
    weights = tuple((item.astype(jnp.float32) for item in (w_query, key_matrix, value_matrix, b_query, key_bias_vector, value_bias_vector, w_out, norm_attn, norm_ffn, w_gate, w_up, w_down)))
    fields = tokens.astype(jnp.float32).reshape(SEQUENCE_COUNT, SEQUENCE_LENGTH, MODEL_WIDTH)

    def apply_layer(weight_set, field_set):
        return forward(weight_set, field_set, segments)
    layer_result, pull_back = jax.vjp(apply_layer, weights, fields)
    weight_grads, gradient_entries = pull_back(cotangent.astype(jnp.float32).reshape(SEQUENCE_COUNT, SEQUENCE_LENGTH, MODEL_WIDTH))
    query_weight_gradient, key_weight_gradient, value_weight_gradient, query_bias_gradient, key_bias_gradient, value_bias_gradient, output_weight_gradient, attention_norm_gradient, feedforward_norm_gradient, gate_weight_gradient, up_weight_gradient, down_weight_gradient = weight_grads
    return (layer_result.reshape(SEQUENCE_COUNT * SEQUENCE_LENGTH, MODEL_WIDTH).astype(jnp.bfloat16), gradient_entries.reshape(SEQUENCE_COUNT * SEQUENCE_LENGTH, MODEL_WIDTH), query_weight_gradient, key_weight_gradient, value_weight_gradient, query_bias_gradient.reshape(QUERY_HEADS, HEAD_SIZE), key_bias_gradient.reshape(KEY_VALUE_HEADS, HEAD_SIZE), value_bias_gradient.reshape(KEY_VALUE_HEADS, HEAD_SIZE), output_weight_gradient, attention_norm_gradient, feedforward_norm_gradient, gate_weight_gradient, up_weight_gradient, down_weight_gradient)
```

```python
import functools
import math

import jax
import jax.numpy as jnp
from jax import lax
from jax.experimental import pallas as pl
from jax.experimental.pallas import tpu as pltpu
from jax.sharding import PartitionSpec as P

MESH = pl.DeviceIdType.MESH
VM = pl.BlockSpec(memory_space=pltpu.VMEM)
DMA = pltpu.SemaphoreType.DMA
BF = jnp.bfloat16
F32 = jnp.float32

epsilon = 1e-06
rope_base = 1000000.0
masked_score = -1e30
KEYS = 512


class Place:
    def __init__(self):
        f = lax.axis_index("fsdp")
        c = lax.axis_index("ctx")
        self.y, self.z = f // 4, f % 4
        self.lo, self.k = c // 2, c % 2
        self.t = lax.axis_index("tp")

    def along_y(self, j):
        return {"fsdp": lax.rem(self.y + j, 4) * 4 + self.z}

    def along_z(self, j):
        return {"fsdp": self.y * 4 + lax.rem(self.z + j, 4)}

    @property
    def sibling(self):
        return {"ctx": self.lo * 2 + 1 - self.k}

    def in_ring(self, lo, t):
        return {"ctx": lo * 2 + self.k, "tp": t}

    @property
    def others(self):
        return [(self.lo, 1 - self.t), (1 - self.lo, self.t), (1 - self.lo, 1 - self.t)]


def greet(devices):
    barrier = pltpu.get_barrier_semaphore()
    for device in devices:
        pl.semaphore_signal(barrier, inc=1, device_id=device, device_id_type=MESH)
    pl.semaphore_wait(barrier, len(devices))


def send(source, target, send_sem, recv_sem, device):
    copy = pltpu.make_async_remote_copy(
        src_ref=source,
        dst_ref=target,
        send_sem=send_sem,
        recv_sem=recv_sem,
        device_id=device,
        device_id_type=MESH,
    )
    copy.start()
    return copy


def comm_call(body, outs, scratch, collective_id, mib, *args):
    return pl.pallas_call(
        body,
        out_shape=outs,
        in_specs=[VM] * len(args),
        out_specs=[VM] * len(outs),
        scratch_shapes=scratch,
        compiler_params=pltpu.CompilerParams(
            collective_id=collective_id, has_side_effects=True, vmem_limit_bytes=mib << 20
        ),
    )(*args)


def shape(dims, kind):
    return jax.ShapeDtypeStruct(dims, kind)


def opening_kernel(w, tok, dy, w_all, tok2, dy_all, s1, r1, s2, r2, ts, tr, ds, dr, fs, fr):
    me = Place()
    y, z, lo, k, t = me.y, me.z, me.lo, me.k, me.t
    rows = w.shape[0] // 2
    halves = (pl.ds(0, rows), pl.ds(rows, rows))
    near = [me.in_ring(1 - lo, t), me.in_ring(1 - lo, 1 - t)]
    greet(
        [me.along_z(j) for j in (1, 2, 3)]
        + [me.along_y(j) for j in (1, 2, 3)]
        + [me.sibling]
        + near
    )
    first = []
    for half, along in ((0, me.along_z), (1, me.along_y)):
        part = halves[half]
        first.append(
            [
                send(
                    w.at[part],
                    w_all.at[y, z, part],
                    s1.at[half, j - 1],
                    r1.at[half, j - 1],
                    along(j),
                )
                for j in (2, 1, 3)
            ]
        )
    rest = []
    mine = dy.shape[0] // 2
    near_copies = [
        send(dy.at[pl.ds(t * mine, mine)], dy_all.at[lo, k, t], ds.at[i], dr.at[i], near[i])
        for i in (0, 1)
    ]
    rest.append(send(tok, tok2.at[k], ts, tr, me.sibling))
    own = [
        send(
            dy.at[pl.ds(h * mine, mine)], dy_all.at[lo, k, h], fs.at[2 + h], fr.at[2 + h], me.sibling
        )
        for h in (0, 1)
    ]
    rest += own
    for half, along in ((0, me.along_y), (1, me.along_z)):
        part = halves[half]
        for j in (2, 1, 3):
            rest.append(
                send(
                    w.at[part],
                    w_all.at[y, z, part],
                    s2.at[half, 0, j - 1],
                    r2.at[half, 0, j - 1],
                    along(j),
                )
            )
    w_all[y, z] = w[...]
    tok2[k] = tok[...]
    for h in (0, 1):
        dy_all[lo, k, h] = dy[pl.ds(h * mine, mine)]
    for order in range(3):
        for half, along in ((0, me.along_y), (1, me.along_z)):
            part = halves[half]
            offset = (2, 1, 3)[order]
            first[half][order].wait()
            if half == 0:
                block = w_all.at[y, lax.rem(z - offset + 4, 4), part]
            else:
                block = w_all.at[lax.rem(y - offset + 4, 4), z, part]
            for j in (2, 1, 3):
                rest.append(
                    send(
                        block,
                        block,
                        s2.at[half, offset, j - 1],
                        r2.at[half, offset, j - 1],
                        along(j),
                    )
                )
    for i, half in ((0, t), (1, 1 - t)):
        near_copies[i].wait()
        block = dy_all.at[1 - lo, k, half]
        rest.append(send(block, block, fs.at[i], fr.at[i], me.sibling))
    for copy in rest:
        copy.wait()


def opening(w, tok, dy):
    rows, width = w.shape
    count, model = tok.shape
    return comm_call(
        opening_kernel,
        [
            shape((4, 4, rows, width), BF),
            shape((2, count, model), BF),
            shape((2, 2, 2, count // 2, model), BF),
        ],
        [
            DMA((2, 3)),
            DMA((2, 3)),
            DMA((2, 4, 3)),
            DMA((2, 4, 3)),
            DMA,
            DMA,
            DMA((2,)),
            DMA((2,)),
            DMA((4,)),
            DMA((4,)),
        ],
        1,
        32,
        w,
        tok,
        dy,
    )


def keys_kernel(mine, kv, s1, r1, s2, r2):
    me = Place()
    k = me.k
    own = me.z * 2 + me.lo
    steps = [(dz, dl) for dz in (2, 1, 3, 0) for dl in (0, 1) if dz or dl]

    def partner(dz, dl):
        return {
            "fsdp": me.y * 4 + lax.rem(me.z + dz, 4),
            "ctx": lax.rem(me.lo + dl, 2) * 2 + k,
        }

    greet([partner(dz, dl) for dz, dl in steps] + [me.sibling])
    copies = [
        send(mine, kv.at[k, own], s1.at[i], r1.at[i], partner(dz, dl))
        for i, (dz, dl) in enumerate(steps)
    ]
    rest = [send(mine, kv.at[k, own], s2.at[7], r2.at[7], me.sibling)]
    kv[k, own] = mine[...]
    for i in (6, 2, 4, 3, 5, 0, 1):
        dz, dl = steps[i]
        copies[i].wait()
        block = kv.at[k, lax.rem(me.z - dz + 4, 4) * 2 + lax.rem(me.lo + dl, 2)]
        rest.append(send(block, block, s2.at[i], r2.at[i], me.sibling))
    for copy in rest:
        copy.wait()


def share_keys(mine):
    rows, width = mine.shape
    return comm_call(
        keys_kernel,
        [shape((2, 8, rows, width), BF)],
        [DMA((7,)), DMA((7,)), DMA((8,)), DMA((8,))],
        2,
        16,
        mine,
    )[0]


def over_rows(a, b):
    return lax.dot_general(a, b, (((0,), (0,)), ((), ())), preferred_element_type=F32)


def by_columns(a, b):
    return lax.dot_general(a, b, (((1,), (1,)), ((), ())), preferred_element_type=F32)


def plain(a, b):
    return lax.dot_general(a, b, (((1,), (0,)), ((), ())), preferred_element_type=F32)


def visible_pairs(block, first, start, rows):
    key = block * KEYS + lax.broadcasted_iota(jnp.int32, (KEYS, rows), 0)
    row = first + lax.broadcasted_iota(jnp.int32, (1, rows), 1)
    return (key >= start) & (key <= row)


def attend_kernel(heads, start_ref, q, kv, o, exact, lse, top, total, acc):
    me = Place()
    rows = q.shape[0]
    size = q.shape[1] // heads
    index = me.z * 2 + me.lo
    first = index * rows
    start = start_ref[...]
    top[...] = jnp.full_like(top, masked_score)
    total[...] = jnp.zeros_like(total)
    acc[...] = jnp.zeros_like(acc)

    def step(block, _):
        keys = kv[0, block]
        values = kv[1, block]
        seen = visible_pairs(block, first, start, rows)
        for h in range(heads):
            s = by_columns(keys, q[:, h * size : (h + 1) * size])
            s = jnp.where(seen, s, masked_score)
            before = top[h : h + 1]
            now = jnp.maximum(before, jnp.max(s, axis=0, keepdims=True))
            p = jnp.exp(s - now)
            shrink = jnp.exp(before - now)
            top[h : h + 1] = now
            total[h : h + 1] = total[h : h + 1] * shrink + jnp.sum(p, axis=0, keepdims=True)
            acc[h] = acc[h] * shrink + over_rows(values, p.astype(BF))
        return 0

    lax.fori_loop(0, index + 1, step, 0)
    lse[...] = jnp.zeros_like(lse)
    for h in range(heads):
        sums = total[h : h + 1]
        lse[h : h + 1] = top[h : h + 1] + jnp.log(sums)
        out = acc[h] / sums
        exact[h] = out
        o[:, h * size : (h + 1) * size] = out.T.astype(BF)


def attend(start, q, kv, heads):
    rows, width = q.shape
    return pl.pallas_call(
        functools.partial(attend_kernel, heads),
        out_shape=[
            shape((rows, width), BF),
            shape((heads, width // heads, rows), F32),
            shape((8, rows), F32),
        ],
        in_specs=[VM] * 3,
        out_specs=[VM] * 3,
        scratch_shapes=[
            pltpu.VMEM((8, rows), F32),
            pltpu.VMEM((8, rows), F32),
            pltpu.VMEM((heads, width // heads, rows), F32),
        ],
        compiler_params=pltpu.CompilerParams(vmem_limit_bytes=32 << 20),
    )(start, q, kv)


def attend_back_kernel(heads, start_ref, lse, q, kv, exact, do, dq, dkv, dots, acc):
    me = Place()
    rows = q.shape[0]
    size = q.shape[1] // heads
    index = me.z * 2 + me.lo
    first = index * rows
    start = start_ref[...]
    for h in range(heads):
        part = slice(h * size, (h + 1) * size)
        product = exact[h] * do[:, part].astype(F32).T
        dots[h : h + 1] = jnp.sum(product, axis=0, keepdims=True)
    acc[...] = jnp.zeros_like(acc)

    def step(block, _):
        keys = kv[0, block]
        values = kv[1, block]
        seen = visible_pairs(block, first, start, rows)
        dk = jnp.zeros((KEYS, size), F32)
        dv = jnp.zeros((KEYS, size), F32)
        for h in range(heads):
            q_h = q[:, h * size : (h + 1) * size]
            do_h = do[:, h * size : (h + 1) * size]
            s = jnp.where(seen, by_columns(keys, q_h), masked_score)
            p = jnp.exp(s - lse[h : h + 1])
            dv = dv + plain(p.astype(BF), do_h)
            dp = by_columns(values, do_h)
            ds = (p * (dp - dots[h : h + 1])).astype(BF)
            dk = dk + plain(ds, q_h)
            acc[h] = acc[h] + over_rows(keys, ds)
        dkv[0, block] = dk
        dkv[1, block] = dv
        return 0

    lax.fori_loop(0, index + 1, step, 0)

    def blank(block, _):
        dkv[0, block] = jnp.zeros((KEYS, size), F32)
        dkv[1, block] = jnp.zeros((KEYS, size), F32)
        return 0

    lax.fori_loop(index + 1, kv.shape[1], blank, 0)
    for h in range(heads):
        dq[:, h * size : (h + 1) * size] = acc[h].T


def attend_back(start, lse, q, kv, exact, do, heads):
    rows, width = q.shape
    return pl.pallas_call(
        functools.partial(attend_back_kernel, heads),
        out_shape=[shape((rows, width), F32), shape(kv.shape, F32)],
        in_specs=[VM] * 6,
        out_specs=[VM] * 2,
        scratch_shapes=[
            pltpu.VMEM((8, rows), F32),
            pltpu.VMEM((heads, width // heads, rows), F32),
        ],
        compiler_params=pltpu.CompilerParams(vmem_limit_bytes=40 << 20),
    )(start, lse, q, kv, exact, do)


def pair_sum(me, part, r1, s1, r2, sems):
    k, t = me.k, me.t
    copy = send(part.at[1 - k], r1, sems.at[0], sems.at[1], me.sibling)
    copy.wait()
    s1[...] = (part[k, 1 - t].astype(F32) + r1[1 - t].astype(F32)).astype(BF)
    copy = send(s1, r2, sems.at[2], sems.at[3], me.in_ring(me.lo, 1 - t))
    here = part[k, t].astype(F32) + r1[t].astype(F32)
    copy.wait()
    return here + r2[...].astype(F32)


def middle_kernel(part, tok, gain, x1, h2, r1, s1, r2, sems, hs, hr, fs, fr):
    me = Place()
    lo, k, t = me.lo, me.k, me.t
    greet([me.in_ring(*other) for other in me.others] + [me.sibling])
    x = tok[...].astype(F32) + pair_sum(me, part, r1, s1, r2, sems)
    x1[...] = x
    factor = lax.rsqrt(jnp.mean(x * x, axis=-1, keepdims=True) + epsilon)
    h2[lo, k, t] = (x * factor * gain[...]).astype(BF)
    block = h2.at[lo, k, t]
    copies = [
        send(block, block, hs.at[i], hr.at[i], me.in_ring(*other))
        for i, other in enumerate(me.others)
    ]
    rest = [send(block, block, fs.at[3], fr.at[3], me.sibling)]
    for i in (1, 2, 0):
        there, half = me.others[i]
        copies[i].wait()
        block = h2.at[there, k, half]
        rest.append(send(block, block, fs.at[i], fr.at[i], me.sibling))
    for copy in rest:
        copy.wait()


def middle(part, tok, gain):
    rows, model = tok.shape
    return comm_call(
        middle_kernel,
        [shape((rows, model), F32), shape((2, 2, 2, rows, model), BF)],
        [
            pltpu.VMEM((2, rows, model), BF),
            pltpu.VMEM((rows, model), BF),
            pltpu.VMEM((rows, model), BF),
            DMA((4,)),
            DMA((3,)),
            DMA((3,)),
            DMA((4,)),
            DMA((4,)),
        ],
        3,
        32,
        part,
        tok,
        gain,
    )


def norm_back(grad_normed, normed, factor):
    return factor * (grad_normed - normed * jnp.mean(grad_normed * normed, axis=-1, keepdims=True))


def turn_kernel(
    dh2, yp, x1, dy, gain, dx1, dxl, gnf, out, r1, s1, r2, as1, ar1, as2, ar2, gs, gr, os, orr
):
    me = Place()
    lo, k, t = me.lo, me.k, me.t
    greet([me.in_ring(*other) for other in me.others] + [me.sibling])
    cores = [
        [
            send(
                part.at[there, 1 - k], r1.at[a, there], as1.at[a, there], ar1.at[a, there], me.sibling
            )
            for there in (0, 1)
        ]
        for a, part in enumerate((dh2, yp))
    ]
    spread = []
    for a, part in enumerate((dh2, yp)):
        for there in (0, 1):
            cores[a][there].wait()
            s1[a, there] = (part[there, k].astype(F32) + r1[a, there].astype(F32)).astype(BF)
        spread.append(
            [
                send(s1.at[a, there, half], r2.at[a, i], as2.at[a, i], ar2.at[a, i], me.in_ring(there, half))
                for i, (there, half) in enumerate(me.others)
            ]
        )
    for copy in spread[0]:
        copy.wait()
    grad = s1[0, lo, t].astype(F32)
    for i in range(3):
        grad = grad + r2[0, i].astype(F32)
    x = x1[...]
    factor = lax.rsqrt(jnp.mean(x * x, axis=-1, keepdims=True) + epsilon)
    normed = x * factor
    gnf[...] = jnp.sum(grad * normed, axis=0, keepdims=True)
    back = dy[...].astype(F32) + norm_back(grad * gain[...], normed, factor)
    dx1[...] = back
    dxl[k, t] = back.astype(BF)
    block = dxl.at[k, t]
    across = send(block, block, gs.at[0], gr.at[0], me.in_ring(lo, 1 - t))
    rest = [send(block, block, gs.at[1], gr.at[1], me.sibling)]
    across.wait()
    block = dxl.at[k, 1 - t]
    rest.append(send(block, block, gs.at[2], gr.at[2], me.sibling))
    for copy in spread[1]:
        copy.wait()
    y = s1[1, lo, t].astype(F32)
    for i in range(3):
        y = y + r2[1, i].astype(F32)
    out[t] = (x1[...] + y).astype(BF)
    block = out.at[t]
    rest.append(send(block, block, os, orr, me.in_ring(lo, 1 - t)))
    for copy in rest:
        copy.wait()


def turn(dh2, yp, x1, dy, gain):
    rows, model = x1.shape
    return comm_call(
        turn_kernel,
        [
            shape((rows, model), F32),
            shape((2, 2, rows, model), BF),
            shape((1, model), F32),
            shape((2, rows, model), BF),
        ],
        [
            pltpu.VMEM((2, 2, 2, rows, model), BF),
            pltpu.VMEM((2, 2, 2, rows, model), BF),
            pltpu.VMEM((2, 3, rows, model), BF),
            DMA((2, 2)),
            DMA((2, 2)),
            DMA((2, 3)),
            DMA((2, 3)),
            DMA((3,)),
            DMA((3,)),
            DMA,
            DMA,
        ],
        4,
        48,
        dh2,
        yp,
        x1,
        dy,
        gain,
    )


def keys_back_kernel(dkv, mine, r1, s1, r2, as1, ar1, as2, ar2):
    me = Place()
    k = me.k
    own = me.z * 2 + me.lo
    steps = [(dz, dl) for dz in (2, 1, 3, 0) for dl in (0, 1) if dz or dl]

    def block(dz, dl):
        return lax.rem(me.z + dz, 4) * 2 + lax.rem(me.lo + dl, 2)

    def partner(dz, dl):
        return {
            "fsdp": me.y * 4 + lax.rem(me.z + dz, 4),
            "ctx": lax.rem(me.lo + dl, 2) * 2 + k,
        }

    greet([partner(dz, dl) for dz, dl in steps] + [me.sibling])
    cores = send(dkv.at[1 - k], r1, as1, ar1, me.sibling)
    cores.wait()
    s1[...] = (dkv[k] + r1[...]).astype(BF)
    copies = [
        send(s1.at[block(dz, dl)], r2.at[i], as2.at[i], ar2.at[i], partner(dz, dl))
        for i, (dz, dl) in enumerate(steps)
    ]
    total = s1[own].astype(F32)
    for i, copy in enumerate(copies):
        copy.wait()
        total = total + r2[i].astype(F32)
    mine[...] = total


def return_keys(dkv):
    _, count, rows, width = dkv.shape
    return comm_call(
        keys_back_kernel,
        [shape((rows, width), F32)],
        [
            pltpu.VMEM((count, rows, width), F32),
            pltpu.VMEM((count, rows, width), BF),
            pltpu.VMEM((count - 1, rows, width), BF),
            DMA,
            DMA,
            DMA((count - 1,)),
            DMA((count - 1,)),
        ],
        5,
        24,
        dkv,
    )[0]


def tokens_kernel(part, tok, dx1, gain, grad, gna, r1, s1, r2, sems, gs, gr):
    me = Place()
    t = me.t
    greet([me.in_ring(me.lo, 1 - t), me.sibling])
    dh1 = pair_sum(me, part, r1, s1, r2, sems)
    x = tok[...].astype(F32)
    factor = lax.rsqrt(jnp.mean(x * x, axis=-1, keepdims=True) + epsilon)
    normed = x * factor
    gna[...] = jnp.sum(dh1 * normed, axis=0, keepdims=True)
    grad[t] = (dx1[...] + norm_back(dh1 * gain[...], normed, factor)).astype(BF)
    block = grad.at[t]
    send(block, block, gs, gr, me.in_ring(me.lo, 1 - t)).wait()


def tokens_back(part, tok, dx1, gain):
    rows, model = tok.shape
    return comm_call(
        tokens_kernel,
        [shape((2, rows, model), BF), shape((1, model), F32)],
        [
            pltpu.VMEM((2, rows, model), BF),
            pltpu.VMEM((rows, model), BF),
            pltpu.VMEM((rows, model), BF),
            DMA((4,)),
            DMA,
            DMA,
        ],
        6,
        24,
        part,
        tok,
        dx1,
        gain,
    )


def closing_kernel(
    ga, ext, ffn, a_all, ext_all, ffn_all,
    r1, sm, r2, fin, e1, esm, e2, as1, ar1, as2, ar2, as3, ar3, es, er, fs, fr, xs, xr,
):
    me = Place()
    y, z, lo, k, t = me.y, me.z, me.lo, me.k, me.t
    c = lo * 2 + k

    def in_ctx(j):
        return {"ctx": lax.rem(c + j, 4)}

    ring = [(dt, dc) for dt in (0, 1) for dc in range(4) if dt or dc]

    def in_x(dt, dc):
        return {"ctx": lax.rem(c + dc, 4), "tp": lax.rem(t + dt, 2)}

    greet(
        [me.along_z(j) for j in (1, 2, 3)]
        + [me.along_y(j) for j in (1, 2, 3)]
        + [in_x(dt, dc) for dt, dc in ring]
    )
    small = [
        send(ext.at[:, lax.rem(z + j, 4)], e1.at[j - 1], es.at[0, j - 1], er.at[0, j - 1], me.along_z(j))
        for j in (2, 1, 3)
    ]
    large = [
        [
            send(
                ga.at[:, lax.rem(z + j, 4), 0], r1.at[0, j - 1], as1.at[0, j - 1], ar1.at[0, j - 1], me.along_z(j)
            )
            for j in (2, 1, 3)
        ],
        [
            send(
                ga.at[lax.rem(y + j, 4), :, 1], r1.at[1, j - 1], as1.at[1, j - 1], ar1.at[1, j - 1], me.along_y(j)
            )
            for j in (2, 1, 3)
        ],
    ]
    rest = [
        send(ffn.at[lax.rem(c + j, 4)], ffn_all.at[c], fs.at[j - 1], fr.at[j - 1], in_ctx(j))
        for j in (1, 2, 3)
    ]
    ffn_all[c] = ffn[c]
    for copy in small:
        copy.wait()
    esm[...] = (ext[:, z] + e1[0]) + (e1[1] + e1[2])
    small = [
        send(esm.at[lax.rem(y + j, 4)], e2.at[j - 1], es.at[1, j - 1], er.at[1, j - 1], me.along_y(j))
        for j in (2, 1, 3)
    ]
    for copy in small:
        copy.wait()
    ext_all[t, c] = (esm[y] + e2[0]) + (e2[1] + e2[2])
    block = ext_all.at[t, c]
    rest += [
        send(block, block, xs.at[i], xr.at[i], in_x(dt, dc)) for i, (dt, dc) in enumerate(ring)
    ]
    for half in (0, 1):
        for copy in large[half]:
            copy.wait()
        here = ga[:, z, 0] if half == 0 else ga[y, :, 1]
        total = here.astype(F32)
        for j in range(3):
            total = total + r1[half, j].astype(F32)
        sm[half] = total.astype(BF)
    last = [
        [
            send(
                sm.at[0, lax.rem(y + j, 4)], r2.at[0, j - 1], as2.at[0, j - 1], ar2.at[0, j - 1], me.along_y(j)
            )
            for j in (2, 1, 3)
        ],
        [
            send(
                sm.at[1, lax.rem(z + j, 4)], r2.at[1, j - 1], as2.at[1, j - 1], ar2.at[1, j - 1], me.along_z(j)
            )
            for j in (2, 1, 3)
        ],
    ]
    half_rows = sm.shape[2]
    quarter = half_rows // 2
    for half in (0, 1):
        for copy in last[half]:
            copy.wait()
        here = sm[0, y] if half == 0 else sm[1, z]
        total = here.astype(F32)
        for j in range(3):
            total = total + r2[half, j].astype(F32)
        fin[2 * half] = total[:quarter]
        fin[2 * half + 1] = total[quarter:]
    a_all[c] = fin[c]
    rest += [
        send(fin.at[lax.rem(c + j, 4)], a_all.at[c], as3.at[j - 1], ar3.at[j - 1], in_ctx(j))
        for j in (1, 2, 3)
    ]
    for copy in rest:
        copy.wait()


def closing(ga, ext, ffn):
    _, _, _, rows, width = ga.shape
    return comm_call(
        closing_kernel,
        [
            shape((4, rows // 2, width), F32),
            shape((2, 4) + ext.shape[2:], F32),
            shape(ffn.shape, BF),
        ],
        [
            pltpu.VMEM((2, 3, 4, rows, width), BF),
            pltpu.VMEM((2, 4, rows, width), BF),
            pltpu.VMEM((2, 3, rows, width), BF),
            pltpu.VMEM((4, rows // 2, width), F32),
            pltpu.VMEM((3, 4) + ext.shape[2:], F32),
            pltpu.VMEM((4,) + ext.shape[2:], F32),
            pltpu.VMEM((3,) + ext.shape[2:], F32),
            DMA((2, 3)),
            DMA((2, 3)),
            DMA((2, 3)),
            DMA((2, 3)),
            DMA((3,)),
            DMA((3,)),
            DMA((2, 3)),
            DMA((2, 3)),
            DMA((3,)),
            DMA((3,)),
            DMA((7,)),
            DMA((7,)),
        ],
        7,
        40,
        ga,
        ext,
        ffn,
    )


def rotate(values_in, cosine, sine):
    half_size = values_in.shape[-1] // 2
    front, back = values_in[..., :half_size], values_in[..., half_size:]
    return jnp.concatenate([front * cosine - back * sine, back * cosine + front * sine], axis=-1)


def shards(
    tokens,
    segments,
    w_query,
    key_matrix,
    value_matrix,
    b_query,
    key_bias_vector,
    value_bias_vector,
    w_out,
    norm_attn,
    norm_ffn,
    w_gate,
    w_up,
    w_down,
    cotangent,
):
    f = lax.axis_index("fsdp")
    c = lax.axis_index("ctx")
    t = lax.axis_index("tp")
    seq, quarter = f // 4, f % 4
    lo, k = c // 2, c % 2
    is_key = k == 0
    size = key_matrix.shape[1]
    query_width = w_query.shape[1] // 2
    heads = query_width // size
    own_width = query_width + size
    model = tokens.shape[1]
    count = tokens.shape[0]
    slice_rows = count // 2
    shard_rows = w_query.shape[0]
    hidden = w_gate.shape[1] // 4
    padded = -(-hidden // 128) * 128

    def hidden_slice(w, axis):
        return lax.dynamic_slice_in_dim(w, c * hidden, hidden, axis)

    own_ffn = jnp.stack(
        [hidden_slice(w_gate, 1), hidden_slice(w_up, 1), hidden_slice(w_down, 0).T]
    )
    own_ffn = jnp.pad(own_ffn, ((0, 0), (0, 0), (0, padded - hidden)))
    ffn_weights = lax.all_gather(own_ffn, "fsdp", axis=1, tiled=True)
    gate_all, up_all, down_all = ffn_weights[0], ffn_weights[1], ffn_weights[2]

    own_attn = jnp.concatenate(
        [
            lax.dynamic_slice_in_dim(w_query, k * query_width, query_width, 1),
            jnp.where(is_key, key_matrix, value_matrix),
            lax.dynamic_slice_in_dim(w_out, k * query_width, query_width, 0).T,
        ],
        axis=1,
    )
    attn_all, tok2, dy_all = opening(own_attn, tokens, cotangent)
    attn_all = attn_all.reshape(model, own_width + query_width)
    in_all, out_all = attn_all[:, :own_width], attn_all[:, own_width:]
    dy_all = dy_all.reshape(4 * count, model)
    own_tokens = lax.dynamic_slice_in_dim(tokens, t * slice_rows, slice_rows, 0)
    own_dy = lax.dynamic_slice_in_dim(cotangent, t * slice_rows, slice_rows, 0)

    seg_row = lax.dynamic_index_in_dim(segments, seq, 0, keepdims=False)
    rows = 2 * count
    first = (quarter * 2 + lo) * rows
    seg_mine = lax.dynamic_slice_in_dim(seg_row, first, rows)
    starts = jnp.zeros((rows,), jnp.int32)
    for number in range(1, 4):
        begin = jnp.sum((seg_row < number).astype(jnp.int32))
        starts = jnp.where(seg_mine == number, begin, starts)
    pos = (first + jnp.arange(rows, dtype=jnp.int32) - starts).astype(F32)
    frequency = jnp.exp(
        jnp.arange(size // 2, dtype=F32) * (-2.0 * math.log(rope_base) / size)
    )
    angles = pos[:, None, None] * frequency
    cosine, sine = jnp.cos(angles), jnp.sin(angles)
    kv_cosine = jnp.where(is_key, cosine[:, 0], 1.0)
    kv_sine = jnp.where(is_key, sine[:, 0], 0.0)
    starts = starts[None, :]
    query_scale = 1.0 / math.sqrt(size)

    gain_attn = norm_attn.astype(F32)
    gain_ffn = norm_ffn.astype(F32)
    x = tok2.reshape(rows, model).astype(F32)
    h1 = (x * lax.rsqrt(jnp.mean(x * x, axis=-1, keepdims=True) + epsilon) * gain_attn).astype(BF)
    bias = jnp.concatenate(
        [
            lax.dynamic_slice_in_dim(b_query, k * query_width, query_width, 0),
            jnp.where(is_key, key_bias_vector, value_bias_vector),
        ]
    ).astype(F32)
    linear = plain(h1, in_all) + bias
    q_lin = linear[:, :query_width].reshape(rows, heads, size)
    q = (rotate(q_lin, cosine, sine) * query_scale).astype(BF).reshape(rows, query_width)
    kv = share_keys(rotate(linear[:, query_width:], kv_cosine, kv_sine).astype(BF))
    ob, exact, lse = attend(starts, q, kv, heads)
    part = by_columns(ob, out_all).astype(BF).reshape(2, 2, slice_rows, model)
    x1, h2 = middle(part, own_tokens, gain_ffn[None])
    h2 = h2.reshape(4 * count, model)

    gate_val = plain(h2, gate_all)
    up_val = plain(h2, up_all)
    sigmoid_gate = jax.nn.sigmoid(gate_val)
    silu_gate = gate_val * sigmoid_gate
    inner = (silu_gate * up_val).astype(BF)
    grad_down = over_rows(dy_all, inner).astype(BF)
    grad_inner = plain(dy_all, down_all)
    gate_slope = sigmoid_gate * (1.0 + gate_val * (1.0 - sigmoid_gate))
    gate_back = (grad_inner * up_val * gate_slope).astype(BF)
    up_back = (grad_inner * silu_gate).astype(BF)
    part_two = by_columns(gate_back, gate_all) + by_columns(up_back, up_all)
    grad_gate = over_rows(h2, gate_back).astype(BF)
    grad_up = over_rows(h2, up_back).astype(BF)
    ffn_part = by_columns(inner, down_all).astype(BF)
    ffn_grads = lax.psum_scatter(
        jnp.stack([grad_gate, grad_up, grad_down]), "fsdp", scatter_dimension=1, tiled=True
    )
    ring_shape = (2, 2, 2, slice_rows, model)
    dx1, dxl, grad_norm_two, output = turn(
        part_two.astype(BF).reshape(ring_shape),
        ffn_part.reshape(ring_shape),
        x1,
        own_dy,
        gain_ffn[None],
    )
    dxl = dxl.reshape(rows, model)

    grad_out = over_rows(dxl, ob)
    do = plain(dxl, out_all).astype(BF)
    dq, dkv = attend_back(starts, lse, q, kv, exact, do, heads)
    dkv = return_keys(dkv)
    dq = rotate(dq.reshape(rows, heads, size) * query_scale, cosine, -sine).reshape(
        rows, query_width
    )
    dkv = rotate(dkv, kv_cosine, -kv_sine)
    back = jnp.concatenate([dq, dkv], axis=1)
    grad_bias = jnp.sum(back, axis=0)
    back = back.astype(BF)
    grad_in = over_rows(h1, back)
    part_one = by_columns(back, in_all).astype(BF).reshape(2, 2, slice_rows, model)
    grad_tokens, grad_norm_one = tokens_back(part_one, own_tokens, dx1, gain_attn[None])

    grad_attn = jnp.concatenate([grad_in, grad_out], axis=1).astype(BF)
    owner_rows = shard_rows // 4
    ext = jnp.concatenate(
        [
            grad_norm_one.reshape(16, 4, owner_rows),
            grad_norm_two.reshape(16, 4, owner_rows),
            grad_bias.reshape(heads + 1, 16, 4, 2).transpose(1, 2, 0, 3).reshape(16, 4, -1),
        ],
        axis=2,
    )
    ext = jnp.pad(ext, ((0, 0), (0, 4), (0, 128 - ext.shape[2]))).reshape(4, 4, 8, 128)
    ffn_blocks = ffn_grads.reshape(3, 4, owner_rows, padded).transpose(1, 0, 2, 3)
    ffn_blocks = jnp.pad(
        ffn_blocks.reshape(4, 3 * owner_rows, padded), ((0, 0), (0, -3 * owner_rows % 16), (0, 0))
    )
    a_all, ext_all, ffn_all = closing(
        grad_attn.reshape(4, 4, 2, shard_rows // 2, own_width + query_width), ext, ffn_blocks
    )
    a_all = a_all[:2] + a_all[2:]
    ffn_all = ffn_all[:, : 3 * owner_rows, :hidden].astype(F32)
    ffn_all = ffn_all.reshape(4, 3, owner_rows, hidden).transpose(1, 2, 0, 3)
    ffn_all = ffn_all.reshape(3, owner_rows, 4 * hidden)
    own_ext = lax.dynamic_index_in_dim(ext_all, c, 2, keepdims=False)
    norms = jnp.sum(own_ext.reshape(8, 128), axis=0)
    biases = lax.dynamic_index_in_dim(own_ext, t, 0, keepdims=False)
    biases = biases[:2] + biases[2:]
    biases = biases[:, 2 * owner_rows : 2 * owner_rows + 2 * (heads + 1)].reshape(2, heads + 1, 2)
    return (
        output.reshape(count, model),
        grad_tokens.reshape(count, model).astype(F32),
        jnp.concatenate([a_all[0, :, :query_width], a_all[1, :, :query_width]], axis=1),
        a_all[0, :, query_width:own_width],
        a_all[1, :, query_width:own_width],
        biases[:, :heads].reshape(2 * heads, 2),
        biases[0, heads:],
        biases[1, heads:],
        jnp.concatenate([a_all[0, :, own_width:], a_all[1, :, own_width:]], axis=1).T,
        norms[:owner_rows],
        norms[owner_rows : 2 * owner_rows],
        ffn_all[0],
        ffn_all[1],
        ffn_all[2].T,
    )


def solution(mesh):
    both = ("fsdp", "ctx")
    in_specs = (
        P(both, None),
        P(),
        P("fsdp", "tp"),
        P("fsdp", "tp"),
        P("fsdp", "tp"),
        P("tp"),
        P("tp"),
        P("tp"),
        P("tp", "fsdp"),
        P(),
        P(),
        P("fsdp", "tp"),
        P("fsdp", "tp"),
        P("tp", "fsdp"),
        P(both, None),
    )
    out_specs = (
        P(both, None),
        P(both, None),
        P(both, "tp"),
        P(both, "tp"),
        P(both, "tp"),
        P("tp", both),
        P("tp", both),
        P("tp", both),
        P("tp", both),
        P(both),
        P(both),
        P(both, "tp"),
        P(both, "tp"),
        P("tp", both),
    )
    return jax.shard_map(shards, mesh=mesh, in_specs=in_specs, out_specs=out_specs, check_vma=False)
```

```python
import functools
import math

import jax
import jax.numpy as jnp
from jax import lax
from jax.experimental import pallas as pl
from jax.experimental.pallas import tpu as pltpu
from jax.sharding import PartitionSpec as P

MESH = pl.DeviceIdType.MESH
VM = pl.BlockSpec(memory_space=pltpu.VMEM)
DMA = pltpu.SemaphoreType.DMA
BF = jnp.bfloat16
F32 = jnp.float32

epsilon = 1e-06
rope_base = 1000000.0
masked_score = -1e30
KEYS = 512


class Place:
    def __init__(self):
        f = lax.axis_index("fsdp")
        c = lax.axis_index("ctx")
        self.y, self.z = f // 4, f % 4
        self.lo, self.k = c // 2, c % 2
        self.t = lax.axis_index("tp")

    def along_y(self, j):
        return {"fsdp": lax.rem(self.y + j, 4) * 4 + self.z}

    def along_z(self, j):
        return {"fsdp": self.y * 4 + lax.rem(self.z + j, 4)}

    @property
    def sibling(self):
        return {"ctx": self.lo * 2 + 1 - self.k}

    def in_ring(self, lo, t):
        return {"ctx": lo * 2 + self.k, "tp": t}

    @property
    def others(self):
        return [(self.lo, 1 - self.t), (1 - self.lo, self.t), (1 - self.lo, 1 - self.t)]


def greet(devices):
    barrier = pltpu.get_barrier_semaphore()
    for device in devices:
        pl.semaphore_signal(barrier, inc=1, device_id=device, device_id_type=MESH)
    pl.semaphore_wait(barrier, len(devices))


def describe(source, target, send_sem, recv_sem, device):
    return pltpu.make_async_remote_copy(
        src_ref=source,
        dst_ref=target,
        send_sem=send_sem,
        recv_sem=recv_sem,
        device_id=device,
        device_id_type=MESH,
    )


def send(source, target, send_sem, recv_sem, device):
    copy = describe(source, target, send_sem, recv_sem, device)
    copy.start()
    return copy


def comm_call(body, outs, scratch, collective_id, mib, *args):
    return pl.pallas_call(
        body,
        out_shape=outs,
        in_specs=[VM] * len(args),
        out_specs=[VM] * len(outs),
        scratch_shapes=scratch,
        compiler_params=pltpu.CompilerParams(
            collective_id=collective_id, has_side_effects=True, vmem_limit_bytes=mib << 20
        ),
    )(*args)


def shape(dims, kind):
    return jax.ShapeDtypeStruct(dims, kind)


def opening_kernel(w, tok, dy, w_all, tok2, dy_all, s1, r1, s2, r2, ts, tr, ds, dr, fs, fr):
    me = Place()
    y, z, lo, k, t = me.y, me.z, me.lo, me.k, me.t
    rows = w.shape[0] // 2
    halves = (pl.ds(0, rows), pl.ds(rows, rows))
    near = [me.in_ring(1 - lo, t), me.in_ring(1 - lo, 1 - t)]
    greet(
        [me.along_z(j) for j in (1, 2, 3)]
        + [me.along_y(j) for j in (1, 2, 3)]
        + [me.sibling]
        + near
    )
    first = []
    for half, along in ((0, me.along_z), (1, me.along_y)):
        part = halves[half]
        first.append(
            [
                send(
                    w.at[part],
                    w_all.at[y, z, part],
                    s1.at[half, j - 1],
                    r1.at[half, j - 1],
                    along(j),
                )
                for j in (2, 1, 3)
            ]
        )
    rest = []
    mine = dy.shape[0] // 2
    near_copies = [
        send(dy.at[pl.ds(t * mine, mine)], dy_all.at[lo, t, k], ds.at[i], dr.at[i], near[i])
        for i in (0, 1)
    ]
    rest.append(send(tok, tok2.at[k], ts, tr, me.sibling))
    own = [
        send(
            dy.at[pl.ds(h * mine, mine)], dy_all.at[lo, h, k], fs.at[2 + h], fr.at[2 + h], me.sibling
        )
        for h in (0, 1)
    ]
    rest += own
    for half, along in ((0, me.along_y), (1, me.along_z)):
        part = halves[half]
        for j in (2, 1, 3):
            rest.append(
                send(
                    w.at[part],
                    w_all.at[y, z, part],
                    s2.at[half, 0, j - 1],
                    r2.at[half, 0, j - 1],
                    along(j),
                )
            )
    w_all[y, z] = w[...]
    tok2[k] = tok[...]
    for h in (0, 1):
        dy_all[lo, h, k] = dy[pl.ds(h * mine, mine)]
    for order in range(3):
        for half, along in ((0, me.along_y), (1, me.along_z)):
            part = halves[half]
            offset = (2, 1, 3)[order]
            first[half][order].wait()
            if half == 0:
                block = w_all.at[y, lax.rem(z - offset + 4, 4), part]
            else:
                block = w_all.at[lax.rem(y - offset + 4, 4), z, part]
            for j in (2, 1, 3):
                rest.append(
                    send(
                        block,
                        block,
                        s2.at[half, offset, j - 1],
                        r2.at[half, offset, j - 1],
                        along(j),
                    )
                )
    for i, half in ((0, t), (1, 1 - t)):
        near_copies[i].wait()
        block = dy_all.at[1 - lo, half, k]
        rest.append(send(block, block, fs.at[i], fr.at[i], me.sibling))
    for copy in rest:
        copy.wait()


def opening(w, tok, dy):
    rows, width = w.shape
    count, model = tok.shape
    return comm_call(
        opening_kernel,
        [
            shape((4, 4, rows, width), BF),
            shape((2, count, model), BF),
            shape((2, 2, 2, count // 2, model), BF),
        ],
        [
            DMA((2, 3)),
            DMA((2, 3)),
            DMA((2, 4, 3)),
            DMA((2, 4, 3)),
            DMA,
            DMA,
            DMA((2,)),
            DMA((2,)),
            DMA((4,)),
            DMA((4,)),
        ],
        1,
        32,
        w,
        tok,
        dy,
    )


def keys_kernel(mine, kv, s1, r1, s2, r2):
    me = Place()
    k = me.k
    own = me.z * 2 + me.lo
    steps = [(dz, dl) for dz in (2, 1, 3, 0) for dl in (0, 1) if dz or dl]

    def partner(dz, dl):
        return {
            "fsdp": me.y * 4 + lax.rem(me.z + dz, 4),
            "ctx": lax.rem(me.lo + dl, 2) * 2 + k,
        }

    greet([partner(dz, dl) for dz, dl in steps] + [me.sibling])
    copies = [
        send(mine, kv.at[k, own], s1.at[i], r1.at[i], partner(dz, dl))
        for i, (dz, dl) in enumerate(steps)
    ]
    rest = [send(mine, kv.at[k, own], s2.at[7], r2.at[7], me.sibling)]
    kv[k, own] = mine[...]
    for i in (6, 2, 4, 3, 5, 0, 1):
        dz, dl = steps[i]
        copies[i].wait()
        block = kv.at[k, lax.rem(me.z - dz + 4, 4) * 2 + lax.rem(me.lo + dl, 2)]
        rest.append(send(block, block, s2.at[i], r2.at[i], me.sibling))
    for copy in rest:
        copy.wait()


def share_keys(mine):
    rows, width = mine.shape
    return comm_call(
        keys_kernel,
        [shape((2, 8, rows, width), BF)],
        [DMA((7,)), DMA((7,)), DMA((8,)), DMA((8,))],
        2,
        16,
        mine,
    )[0]


def over_rows(a, b):
    return lax.dot_general(a, b, (((0,), (0,)), ((), ())), preferred_element_type=F32)


def by_columns(a, b):
    return lax.dot_general(a, b, (((1,), (1,)), ((), ())), preferred_element_type=F32)


def plain(a, b):
    return lax.dot_general(a, b, (((1,), (0,)), ((), ())), preferred_element_type=F32)


def visible_pairs(block, first, start, rows):
    key = block * KEYS + lax.broadcasted_iota(jnp.int32, (KEYS, rows), 0)
    row = first + lax.broadcasted_iota(jnp.int32, (1, rows), 1)
    return (key >= start) & (key <= row)


def attend_kernel(heads, start_ref, q, kv, o, exact, lse, top, total, acc):
    me = Place()
    rows = q.shape[0]
    size = q.shape[1] // heads
    index = me.z * 2 + me.lo
    first = index * rows
    start = start_ref[...]
    top[...] = jnp.full_like(top, masked_score)
    total[...] = jnp.zeros_like(total)
    acc[...] = jnp.zeros_like(acc)

    def step(block, _):
        keys = kv[0, block]
        values = kv[1, block]
        seen = visible_pairs(block, first, start, rows)
        for h in range(heads):
            s = by_columns(keys, q[:, h * size : (h + 1) * size])
            s = jnp.where(seen, s, masked_score)
            before = top[h : h + 1]
            now = jnp.maximum(before, jnp.max(s, axis=0, keepdims=True))
            p = jnp.exp(s - now)
            shrink = jnp.exp(before - now)
            top[h : h + 1] = now
            total[h : h + 1] = total[h : h + 1] * shrink + jnp.sum(p, axis=0, keepdims=True)
            acc[h] = acc[h] * shrink + over_rows(values, p.astype(BF))
        return 0

    lax.fori_loop(0, index + 1, step, 0)
    lse[...] = jnp.zeros_like(lse)
    for h in range(heads):
        sums = total[h : h + 1]
        lse[h : h + 1] = top[h : h + 1] + jnp.log(sums)
        out = acc[h] / sums
        exact[h] = out
        o[:, h * size : (h + 1) * size] = out.T.astype(BF)


def attend(start, q, kv, heads):
    rows, width = q.shape
    return pl.pallas_call(
        functools.partial(attend_kernel, heads),
        out_shape=[
            shape((rows, width), BF),
            shape((heads, width // heads, rows), F32),
            shape((8, rows), F32),
        ],
        in_specs=[VM] * 3,
        out_specs=[VM] * 3,
        scratch_shapes=[
            pltpu.VMEM((8, rows), F32),
            pltpu.VMEM((8, rows), F32),
            pltpu.VMEM((heads, width // heads, rows), F32),
        ],
        compiler_params=pltpu.CompilerParams(vmem_limit_bytes=32 << 20),
    )(start, q, kv)


def attend_back_kernel(heads, start_ref, lse, q, kv, exact, do, dq, dkv, dots, acc):
    me = Place()
    rows = q.shape[0]
    size = q.shape[1] // heads
    index = me.z * 2 + me.lo
    first = index * rows
    start = start_ref[...]
    for h in range(heads):
        part = slice(h * size, (h + 1) * size)
        product = exact[h] * do[:, part].astype(F32).T
        dots[h : h + 1] = jnp.sum(product, axis=0, keepdims=True)
    acc[...] = jnp.zeros_like(acc)

    def step(block, _):
        keys = kv[0, block]
        values = kv[1, block]
        seen = visible_pairs(block, first, start, rows)
        dk = jnp.zeros((KEYS, size), F32)
        dv = jnp.zeros((KEYS, size), F32)
        for h in range(heads):
            q_h = q[:, h * size : (h + 1) * size]
            do_h = do[:, h * size : (h + 1) * size]
            s = jnp.where(seen, by_columns(keys, q_h), masked_score)
            p = jnp.exp(s - lse[h : h + 1])
            dv = dv + plain(p.astype(BF), do_h)
            dp = by_columns(values, do_h)
            ds = (p * (dp - dots[h : h + 1])).astype(BF)
            dk = dk + plain(ds, q_h)
            acc[h] = acc[h] + over_rows(keys, ds)
        dkv[0, block] = dk
        dkv[1, block] = dv
        return 0

    lax.fori_loop(0, index + 1, step, 0)

    def blank(block, _):
        dkv[0, block] = jnp.zeros((KEYS, size), F32)
        dkv[1, block] = jnp.zeros((KEYS, size), F32)
        return 0

    lax.fori_loop(index + 1, kv.shape[1], blank, 0)
    for h in range(heads):
        dq[:, h * size : (h + 1) * size] = acc[h].T


def attend_back(start, lse, q, kv, exact, do, heads):
    rows, width = q.shape
    return pl.pallas_call(
        functools.partial(attend_back_kernel, heads),
        out_shape=[shape((rows, width), F32), shape(kv.shape, F32)],
        in_specs=[VM] * 6,
        out_specs=[VM] * 2,
        scratch_shapes=[
            pltpu.VMEM((8, rows), F32),
            pltpu.VMEM((heads, width // heads, rows), F32),
        ],
        compiler_params=pltpu.CompilerParams(vmem_limit_bytes=40 << 20),
    )(start, lse, q, kv, exact, do)


def pair_sum(me, part, r1, s1, r2, sems):
    k, t = me.k, me.t
    copy = send(part.at[1 - k], r1, sems.at[0], sems.at[1], me.sibling)
    copy.wait()
    s1[...] = (part[k, 1 - t].astype(F32) + r1[1 - t].astype(F32)).astype(BF)
    copy = send(s1, r2, sems.at[2], sems.at[3], me.in_ring(me.lo, 1 - t))
    here = part[k, t].astype(F32) + r1[t].astype(F32)
    copy.wait()
    return here + r2[...].astype(F32)


def norm_back(grad_normed, normed, factor):
    return factor * (grad_normed - normed * jnp.mean(grad_normed * normed, axis=-1, keepdims=True))


def block_kernel(
    part, tok, gain, dy_hbm, w_hbm,
    x1, dx1, dxl, gnf, ysum, g_hbm,
    w, dy, dy_t, h2, h2_t, hid, gate_back, up_back, whole, m1, m2, m3, pb, s1, r1, r2, yb, ry,
    ls, ms, hs, hr, fs, fr, ps, pr, xs, xr, ys, yr, gs, gr, os,
):
    me = Place()
    lo, k, t = me.lo, me.k, me.t
    rows, model = tok.shape
    both = 2 * rows

    def chip(i):
        return lax.rem(lo + lax.rem((i + 1) // 2, 2), 2), lax.rem(t + i // 2, 2)

    def columns(i):
        return pl.ds(pl.multiple_of(i * both, both), both)

    loads = [pltpu.make_async_copy(dy_hbm, dy, ls.at[3])]
    loads += [pltpu.make_async_copy(w_hbm.at[i], w.at[i], ls.at[i]) for i in range(3)]
    for copy in loads:
        copy.start()
    greet([me.in_ring(*chip(i)) for i in (1, 2, 3)] + [me.sibling])
    cores = send(part.at[1 - k], m1, ms.at[0], ms.at[1], me.sibling)
    loads[0].wait()

    def turn_dy(i, _):
        lo_i, t_i = chip(i)
        dy_t[:, columns(i)] = dy[lo_i, t_i].reshape(both, model).T
        return 0

    cores.wait()
    m2[...] = (part[k, 1 - t].astype(F32) + m1[1 - t].astype(F32)).astype(BF)
    across = send(m2, m3, ms.at[2], ms.at[3], me.in_ring(lo, 1 - t))
    lax.fori_loop(0, 4, turn_dy, 0)
    x = tok[...].astype(F32) + part[k, t].astype(F32) + m1[t].astype(F32)
    across.wait()
    x = x + m3[...].astype(F32)
    x1[...] = x
    factor = lax.rsqrt(jnp.mean(x * x, axis=-1, keepdims=True) + epsilon)
    h2[lo, t, k] = (x * factor * gain[...]).astype(BF)

    def hidden_copy(i):
        block = h2.at[lo, t, k]
        return describe(block, block, hs.at[i - 1], hr.at[i - 1], me.in_ring(*chip(i)))

    def hidden_share(i):
        lo_i, t_i = chip(i)
        block = h2.at[lo_i, t_i, k]
        return describe(block, block, fs.at[i], fr.at[i], me.sibling)

    def part_share(i):
        return describe(pb.at[i], r1.at[i], ps.at[i], pr.at[i], me.sibling)

    def part_copy(i):
        return describe(
            s1.at[i], r2.at[i - 1], xs.at[i - 1], xr.at[i - 1], me.in_ring(*chip(i))
        )

    def result_share(i):
        return describe(yb.at[i], ry.at[i], ys.at[i], yr.at[i], me.sibling)

    for i in (1, 2, 3):
        hidden_copy(i).start()
    hidden_share(0).start()
    for copy in loads[1:]:
        copy.wait()

    def finish(i):
        part_share(i).wait_recv()
        s1[i] = (s1[i].astype(F32) + r1[i].astype(F32)).astype(BF)

        @pl.when(i > 0)
        def _():
            part_copy(i).start()

        whole[...] = by_columns(hid[i], w[2]).reshape(2, rows, model)
        yb[i] = whole[1 - k].astype(BF)
        ysum[i] = whole[k].astype(BF)
        result_share(i).start()
        lo_i, t_i = chip(i)
        h2_t[:, columns(i)] = h2[lo_i, t_i].reshape(both, model).T

    def step(i, _):
        lo_i, t_i = chip(i)

        @pl.when(i > 0)
        def _():
            hidden_copy(i).wait_recv()
            hidden_share(i).start()
            finish(i - 1)

        hidden_share(i).wait_recv()
        h = h2[lo_i, t_i].reshape(both, model)
        d = dy[lo_i, t_i].reshape(both, model)
        gate = plain(h, w[0])
        up = plain(h, w[1])
        sigmoid_gate = jax.nn.sigmoid(gate)
        silu_gate = gate * sigmoid_gate
        hid[i] = (silu_gate * up).astype(BF)
        grad_inner = plain(d, w[2])
        slope = sigmoid_gate * (1.0 + gate * (1.0 - sigmoid_gate))
        gate_back[i] = (grad_inner * up * slope).astype(BF)
        up_back[i] = (grad_inner * silu_gate).astype(BF)
        whole[...] = (by_columns(gate_back[i], w[0]) + by_columns(up_back[i], w[1])).reshape(
            2, rows, model
        )
        pb[i] = whole[1 - k].astype(BF)
        s1[i] = whole[k].astype(BF)
        part_share(i).start()
        return 0

    lax.fori_loop(0, 4, step, 0)
    finish(3)

    def gradient(i, left_t, right):
        flat = right.shape[0] * right.shape[1]
        step_rows = model // 3

        def some(m, _):
            r = pl.ds(pl.multiple_of(m * step_rows, step_rows), step_rows)
            w[i, r] = plain(left_t[r, :], right[...].reshape(flat, right.shape[2])).astype(BF)
            return 0

        lax.fori_loop(0, 3, some, 0)
        copy = pltpu.make_async_copy(w.at[i], g_hbm.at[i], os.at[i])
        copy.start()
        return copy

    outs = [gradient(2, dy_t, hid)]

    grad = s1[0].astype(F32)
    for i in (1, 2, 3):
        part_copy(i).wait_recv()
        grad = grad + r2[i - 1].astype(F32)
    x = x1[...]
    factor = lax.rsqrt(jnp.mean(x * x, axis=-1, keepdims=True) + epsilon)
    normed = x * factor
    gnf[...] = jnp.sum(grad * normed, axis=0, keepdims=True)
    back = dy[lo, t, k].astype(F32) + norm_back(grad * gain[...], normed, factor)
    dx1[...] = back
    dxl[k, t] = back.astype(BF)
    block = dxl.at[k, t]
    across = send(block, block, gs.at[0], gr.at[0], me.in_ring(lo, 1 - t))
    rest = [send(block, block, gs.at[1], gr.at[1], me.sibling)]
    outs.append(gradient(0, h2_t, gate_back))
    across.wait()
    block = dxl.at[k, 1 - t]
    rest.append(send(block, block, gs.at[2], gr.at[2], me.sibling))
    outs.append(gradient(1, h2_t, up_back))
    for i in range(4):
        result_share(i).wait()
        ysum[i] = (ysum[i].astype(F32) + ry[i].astype(F32)).astype(BF)
        hidden_share(i).wait_send()
        part_share(i).wait_send()
    for i in (1, 2, 3):
        hidden_copy(i).wait_send()
        part_copy(i).wait_send()
    for copy in rest + outs:
        copy.wait()


def block(part, tok, gain, dy, w):
    rows, model = tok.shape
    hidden = w.shape[2]
    any_place = pl.BlockSpec(memory_space=pl.ANY)
    quarter = pltpu.VMEM((4, rows, model), BF)
    inner = pltpu.VMEM((4, 2 * rows, hidden), BF)
    turned = pltpu.VMEM((model, 8 * rows), BF)
    return pl.pallas_call(
        block_kernel,
        out_shape=[
            shape((rows, model), F32),
            shape((rows, model), F32),
            shape((2, 2, rows, model), BF),
            shape((1, model), F32),
            shape((4, rows, model), BF),
            shape(w.shape, BF),
        ],
        in_specs=[VM] * 3 + [any_place] * 2,
        out_specs=[VM] * 5 + [any_place],
        scratch_shapes=[
            pltpu.VMEM(w.shape, BF),
            pltpu.VMEM(dy.shape, BF),
            turned,
            pltpu.VMEM(dy.shape, BF),
            turned,
            inner,
            inner,
            inner,
            pltpu.VMEM((2, rows, model), F32),
            pltpu.VMEM((2, rows, model), BF),
            pltpu.VMEM((rows, model), BF),
            pltpu.VMEM((rows, model), BF),
            quarter,
            quarter,
            quarter,
            pltpu.VMEM((3, rows, model), BF),
            quarter,
            quarter,
            DMA((4,)),
            DMA((4,)),
            DMA((3,)),
            DMA((3,)),
            DMA((4,)),
            DMA((4,)),
            DMA((4,)),
            DMA((4,)),
            DMA((3,)),
            DMA((3,)),
            DMA((4,)),
            DMA((4,)),
            DMA((3,)),
            DMA((3,)),
            DMA((3,)),
        ],
        compiler_params=pltpu.CompilerParams(
            collective_id=3, has_side_effects=True, vmem_limit_bytes=62 << 20
        ),
    )(part, tok, gain, dy, w)


def keys_back_kernel(dkv, mine, r1, s1, r2, as1, ar1, as2, ar2):
    me = Place()
    k = me.k
    own = me.z * 2 + me.lo
    steps = [(dz, dl) for dz in (2, 1, 3, 0) for dl in (0, 1) if dz or dl]

    def block(dz, dl):
        return lax.rem(me.z + dz, 4) * 2 + lax.rem(me.lo + dl, 2)

    def partner(dz, dl):
        return {
            "fsdp": me.y * 4 + lax.rem(me.z + dz, 4),
            "ctx": lax.rem(me.lo + dl, 2) * 2 + k,
        }

    greet([partner(dz, dl) for dz, dl in steps] + [me.sibling])
    cores = send(dkv.at[1 - k], r1, as1, ar1, me.sibling)
    cores.wait()
    s1[...] = (dkv[k] + r1[...]).astype(BF)
    copies = [
        send(s1.at[block(dz, dl)], r2.at[i], as2.at[i], ar2.at[i], partner(dz, dl))
        for i, (dz, dl) in enumerate(steps)
    ]
    total = s1[own].astype(F32)
    for i, copy in enumerate(copies):
        copy.wait()
        total = total + r2[i].astype(F32)
    mine[...] = total


def return_keys(dkv):
    _, count, rows, width = dkv.shape
    return comm_call(
        keys_back_kernel,
        [shape((rows, width), F32)],
        [
            pltpu.VMEM((count, rows, width), F32),
            pltpu.VMEM((count, rows, width), BF),
            pltpu.VMEM((count - 1, rows, width), BF),
            DMA,
            DMA,
            DMA((count - 1,)),
            DMA((count - 1,)),
        ],
        5,
        24,
        dkv,
    )[0]


def tokens_kernel(part, tok, dx1, gain, grad, gna, r1, s1, r2, sems, gs, gr):
    me = Place()
    t = me.t
    greet([me.in_ring(me.lo, 1 - t), me.sibling])
    dh1 = pair_sum(me, part, r1, s1, r2, sems)
    x = tok[...].astype(F32)
    factor = lax.rsqrt(jnp.mean(x * x, axis=-1, keepdims=True) + epsilon)
    normed = x * factor
    gna[...] = jnp.sum(dh1 * normed, axis=0, keepdims=True)
    grad[t] = (dx1[...] + norm_back(dh1 * gain[...], normed, factor)).astype(BF)
    block = grad.at[t]
    send(block, block, gs, gr, me.in_ring(me.lo, 1 - t)).wait()


def tokens_back(part, tok, dx1, gain):
    rows, model = tok.shape
    return comm_call(
        tokens_kernel,
        [shape((2, rows, model), BF), shape((1, model), F32)],
        [
            pltpu.VMEM((2, rows, model), BF),
            pltpu.VMEM((rows, model), BF),
            pltpu.VMEM((rows, model), BF),
            DMA((4,)),
            DMA,
            DMA,
        ],
        6,
        24,
        part,
        tok,
        dx1,
        gain,
    )


def closing_kernel(
    ga, ext, ffn, ysum, x1, a_all, ext_all, ffn_all, out,
    r1, sm, r2, fin, e1, esm, e2, yr2,
    as1, ar1, as2, ar2, as3, ar3, es, er, fs, fr, xs, xr, ys, yr,
):
    me = Place()
    y, z, lo, k, t = me.y, me.z, me.lo, me.k, me.t
    c = lo * 2 + k

    def in_ctx(j):
        return {"ctx": lax.rem(c + j, 4)}

    ring = [(dt, dc) for dt in (0, 1) for dc in range(4) if dt or dc]

    def in_x(dt, dc):
        return {"ctx": lax.rem(c + dc, 4), "tp": lax.rem(t + dt, 2)}

    greet(
        [me.along_z(j) for j in (1, 2, 3)]
        + [me.along_y(j) for j in (1, 2, 3)]
        + [in_x(dt, dc) for dt, dc in ring]
    )
    small = [
        send(ext.at[:, lax.rem(z + j, 4)], e1.at[j - 1], es.at[0, j - 1], er.at[0, j - 1], me.along_z(j))
        for j in (2, 1, 3)
    ]
    large = [
        [
            send(
                ga.at[:, lax.rem(z + j, 4), 0], r1.at[0, j - 1], as1.at[0, j - 1], ar1.at[0, j - 1], me.along_z(j)
            )
            for j in (2, 1, 3)
        ],
        [
            send(
                ga.at[lax.rem(y + j, 4), :, 1], r1.at[1, j - 1], as1.at[1, j - 1], ar1.at[1, j - 1], me.along_y(j)
            )
            for j in (2, 1, 3)
        ],
    ]
    rest = [
        send(ffn.at[lax.rem(c + j, 4)], ffn_all.at[c], fs.at[j - 1], fr.at[j - 1], in_ctx(j))
        for j in (1, 2, 3)
    ]
    ffn_all[c] = ffn[c]
    near = [(1 - lo, t), (1 - lo, 1 - t), (lo, 1 - t)]
    results = [
        send(ysum.at[i + 1], yr2.at[i], ys.at[i], yr.at[i], me.in_ring(*near[i])) for i in range(3)
    ]
    for copy in small:
        copy.wait()
    esm[...] = (ext[:, z] + e1[0]) + (e1[1] + e1[2])
    small = [
        send(esm.at[lax.rem(y + j, 4)], e2.at[j - 1], es.at[1, j - 1], er.at[1, j - 1], me.along_y(j))
        for j in (2, 1, 3)
    ]
    for copy in small:
        copy.wait()
    ext_all[t, c] = (esm[y] + e2[0]) + (e2[1] + e2[2])
    block = ext_all.at[t, c]
    rest += [
        send(block, block, xs.at[i], xr.at[i], in_x(dt, dc)) for i, (dt, dc) in enumerate(ring)
    ]
    for half in (0, 1):
        for copy in large[half]:
            copy.wait()
        here = ga[:, z, 0] if half == 0 else ga[y, :, 1]
        total = here.astype(F32)
        for j in range(3):
            total = total + r1[half, j].astype(F32)
        sm[half] = total.astype(BF)
    last = [
        [
            send(
                sm.at[0, lax.rem(y + j, 4)], r2.at[0, j - 1], as2.at[0, j - 1], ar2.at[0, j - 1], me.along_y(j)
            )
            for j in (2, 1, 3)
        ],
        [
            send(
                sm.at[1, lax.rem(z + j, 4)], r2.at[1, j - 1], as2.at[1, j - 1], ar2.at[1, j - 1], me.along_z(j)
            )
            for j in (2, 1, 3)
        ],
    ]
    result = x1[...] + ysum[0].astype(F32)
    for i in range(3):
        results[i].wait()
        result = result + yr2[i].astype(F32)
    out[t] = result.astype(BF)
    block = out.at[t]
    rest.append(send(block, block, ys.at[3], yr.at[3], me.in_ring(lo, 1 - t)))
    half_rows = sm.shape[2]
    quarter = half_rows // 2
    for half in (0, 1):
        for copy in last[half]:
            copy.wait()
        here = sm[0, y] if half == 0 else sm[1, z]
        total = here.astype(F32)
        for j in range(3):
            total = total + r2[half, j].astype(F32)
        fin[2 * half] = total[:quarter]
        fin[2 * half + 1] = total[quarter:]
    a_all[c] = fin[c]
    rest += [
        send(fin.at[lax.rem(c + j, 4)], a_all.at[c], as3.at[j - 1], ar3.at[j - 1], in_ctx(j))
        for j in (1, 2, 3)
    ]
    for copy in rest:
        copy.wait()


def closing(ga, ext, ffn, ysum, x1):
    _, _, _, rows, width = ga.shape
    slice_rows, model = x1.shape
    return comm_call(
        closing_kernel,
        [
            shape((4, rows // 2, width), F32),
            shape((2, 4) + ext.shape[2:], F32),
            shape(ffn.shape, BF),
            shape((2, slice_rows, model), BF),
        ],
        [
            pltpu.VMEM((2, 3, 4, rows, width), BF),
            pltpu.VMEM((2, 4, rows, width), BF),
            pltpu.VMEM((2, 3, rows, width), BF),
            pltpu.VMEM((4, rows // 2, width), F32),
            pltpu.VMEM((3, 4) + ext.shape[2:], F32),
            pltpu.VMEM((4,) + ext.shape[2:], F32),
            pltpu.VMEM((3,) + ext.shape[2:], F32),
            pltpu.VMEM((3, slice_rows, model), BF),
            DMA((2, 3)),
            DMA((2, 3)),
            DMA((2, 3)),
            DMA((2, 3)),
            DMA((3,)),
            DMA((3,)),
            DMA((2, 3)),
            DMA((2, 3)),
            DMA((3,)),
            DMA((3,)),
            DMA((7,)),
            DMA((7,)),
            DMA((4,)),
            DMA((4,)),
        ],
        7,
        40,
        ga,
        ext,
        ffn,
        ysum,
        x1,
    )


def rotate(values_in, cosine, sine):
    half_size = values_in.shape[-1] // 2
    front, back = values_in[..., :half_size], values_in[..., half_size:]
    return jnp.concatenate([front * cosine - back * sine, back * cosine + front * sine], axis=-1)


def shards(
    tokens,
    segments,
    w_query,
    key_matrix,
    value_matrix,
    b_query,
    key_bias_vector,
    value_bias_vector,
    w_out,
    norm_attn,
    norm_ffn,
    w_gate,
    w_up,
    w_down,
    cotangent,
):
    f = lax.axis_index("fsdp")
    c = lax.axis_index("ctx")
    t = lax.axis_index("tp")
    seq, quarter = f // 4, f % 4
    lo, k = c // 2, c % 2
    is_key = k == 0
    size = key_matrix.shape[1]
    query_width = w_query.shape[1] // 2
    heads = query_width // size
    own_width = query_width + size
    model = tokens.shape[1]
    count = tokens.shape[0]
    slice_rows = count // 2
    shard_rows = w_query.shape[0]
    hidden = w_gate.shape[1] // 4
    padded = -(-hidden // 128) * 128

    def hidden_slice(w, axis):
        return lax.dynamic_slice_in_dim(w, c * hidden, hidden, axis)

    own_ffn = jnp.stack(
        [hidden_slice(w_gate, 1), hidden_slice(w_up, 1), hidden_slice(w_down, 0).T]
    )
    own_ffn = jnp.pad(own_ffn, ((0, 0), (0, 0), (0, padded - hidden)))
    ffn_weights = lax.all_gather(own_ffn, "fsdp", axis=1, tiled=True)

    own_attn = jnp.concatenate(
        [
            lax.dynamic_slice_in_dim(w_query, k * query_width, query_width, 1),
            jnp.where(is_key, key_matrix, value_matrix),
            lax.dynamic_slice_in_dim(w_out, k * query_width, query_width, 0).T,
        ],
        axis=1,
    )
    attn_all, tok2, dy_all = opening(own_attn, tokens, cotangent)
    attn_all = attn_all.reshape(model, own_width + query_width)
    in_all, out_all = attn_all[:, :own_width], attn_all[:, own_width:]
    own_tokens = lax.dynamic_slice_in_dim(tokens, t * slice_rows, slice_rows, 0)

    seg_row = lax.dynamic_index_in_dim(segments, seq, 0, keepdims=False)
    rows = 2 * count
    first = (quarter * 2 + lo) * rows
    seg_mine = lax.dynamic_slice_in_dim(seg_row, first, rows)
    starts = jnp.zeros((rows,), jnp.int32)
    for number in range(1, 4):
        begin = jnp.sum((seg_row < number).astype(jnp.int32))
        starts = jnp.where(seg_mine == number, begin, starts)
    pos = (first + jnp.arange(rows, dtype=jnp.int32) - starts).astype(F32)
    frequency = jnp.exp(
        jnp.arange(size // 2, dtype=F32) * (-2.0 * math.log(rope_base) / size)
    )
    angles = pos[:, None, None] * frequency
    cosine, sine = jnp.cos(angles), jnp.sin(angles)
    kv_cosine = jnp.where(is_key, cosine[:, 0], 1.0)
    kv_sine = jnp.where(is_key, sine[:, 0], 0.0)
    starts = starts[None, :]
    query_scale = 1.0 / math.sqrt(size)

    gain_attn = norm_attn.astype(F32)
    gain_ffn = norm_ffn.astype(F32)
    x = tok2.reshape(rows, model).astype(F32)
    h1 = (x * lax.rsqrt(jnp.mean(x * x, axis=-1, keepdims=True) + epsilon) * gain_attn).astype(BF)
    bias = jnp.concatenate(
        [
            lax.dynamic_slice_in_dim(b_query, k * query_width, query_width, 0),
            jnp.where(is_key, key_bias_vector, value_bias_vector),
        ]
    ).astype(F32)
    linear = plain(h1, in_all) + bias
    q_lin = linear[:, :query_width].reshape(rows, heads, size)
    q = (rotate(q_lin, cosine, sine) * query_scale).astype(BF).reshape(rows, query_width)
    kv = share_keys(rotate(linear[:, query_width:], kv_cosine, kv_sine).astype(BF))
    ob, exact, lse = attend(starts, q, kv, heads)
    part = by_columns(ob, out_all).astype(BF).reshape(2, 2, slice_rows, model)
    x1, dx1, dxl, grad_norm_two, ysum, ffn_grads = block(
        part, own_tokens, gain_ffn[None], dy_all, ffn_weights
    )
    ffn_grads = lax.psum_scatter(ffn_grads, "fsdp", scatter_dimension=1, tiled=True)
    dxl = dxl.reshape(rows, model)

    grad_out = over_rows(dxl, ob)
    do = plain(dxl, out_all).astype(BF)
    dq, dkv = attend_back(starts, lse, q, kv, exact, do, heads)
    dkv = return_keys(dkv)
    dq = rotate(dq.reshape(rows, heads, size) * query_scale, cosine, -sine).reshape(
        rows, query_width
    )
    dkv = rotate(dkv, kv_cosine, -kv_sine)
    back = jnp.concatenate([dq, dkv], axis=1)
    grad_bias = jnp.sum(back, axis=0)
    back = back.astype(BF)
    grad_in = over_rows(h1, back)
    part_one = by_columns(back, in_all).astype(BF).reshape(2, 2, slice_rows, model)
    grad_tokens, grad_norm_one = tokens_back(part_one, own_tokens, dx1, gain_attn[None])

    grad_attn = jnp.concatenate([grad_in, grad_out], axis=1).astype(BF)
    owner_rows = shard_rows // 4
    ext = jnp.concatenate(
        [
            grad_norm_one.reshape(16, 4, owner_rows),
            grad_norm_two.reshape(16, 4, owner_rows),
            grad_bias.reshape(heads + 1, 16, 4, 2).transpose(1, 2, 0, 3).reshape(16, 4, -1),
        ],
        axis=2,
    )
    ext = jnp.pad(ext, ((0, 0), (0, 4), (0, 128 - ext.shape[2]))).reshape(4, 4, 8, 128)
    ffn_blocks = ffn_grads.reshape(3, 4, owner_rows, padded).transpose(1, 0, 2, 3)
    ffn_blocks = jnp.pad(
        ffn_blocks.reshape(4, 3 * owner_rows, padded), ((0, 0), (0, -3 * owner_rows % 16), (0, 0))
    )
    a_all, ext_all, ffn_all, output = closing(
        grad_attn.reshape(4, 4, 2, shard_rows // 2, own_width + query_width),
        ext,
        ffn_blocks,
        ysum,
        x1,
    )
    a_all = a_all[:2] + a_all[2:]
    ffn_all = ffn_all[:, : 3 * owner_rows, :hidden].astype(F32)
    ffn_all = ffn_all.reshape(4, 3, owner_rows, hidden).transpose(1, 2, 0, 3)
    ffn_all = ffn_all.reshape(3, owner_rows, 4 * hidden)
    own_ext = lax.dynamic_index_in_dim(ext_all, c, 2, keepdims=False)
    norms = jnp.sum(own_ext.reshape(8, 128), axis=0)
    biases = lax.dynamic_index_in_dim(own_ext, t, 0, keepdims=False)
    biases = biases[:2] + biases[2:]
    biases = biases[:, 2 * owner_rows : 2 * owner_rows + 2 * (heads + 1)].reshape(2, heads + 1, 2)
    return (
        output.reshape(count, model),
        grad_tokens.reshape(count, model).astype(F32),
        jnp.concatenate([a_all[0, :, :query_width], a_all[1, :, :query_width]], axis=1),
        a_all[0, :, query_width:own_width],
        a_all[1, :, query_width:own_width],
        biases[:, :heads].reshape(2 * heads, 2),
        biases[0, heads:],
        biases[1, heads:],
        jnp.concatenate([a_all[0, :, own_width:], a_all[1, :, own_width:]], axis=1).T,
        norms[:owner_rows],
        norms[owner_rows : 2 * owner_rows],
        ffn_all[0],
        ffn_all[1],
        ffn_all[2].T,
    )


def solution(mesh):
    both = ("fsdp", "ctx")
    in_specs = (
        P(both, None),
        P(),
        P("fsdp", "tp"),
        P("fsdp", "tp"),
        P("fsdp", "tp"),
        P("tp"),
        P("tp"),
        P("tp"),
        P("tp", "fsdp"),
        P(),
        P(),
        P("fsdp", "tp"),
        P("fsdp", "tp"),
        P("tp", "fsdp"),
        P(both, None),
    )
    out_specs = (
        P(both, None),
        P(both, None),
        P(both, "tp"),
        P(both, "tp"),
        P(both, "tp"),
        P("tp", both),
        P("tp", both),
        P("tp", both),
        P("tp", both),
        P(both),
        P(both),
        P(both, "tp"),
        P(both, "tp"),
        P("tp", both),
    )
    return jax.shard_map(shards, mesh=mesh, in_specs=in_specs, out_specs=out_specs, check_vma=False)
```

```python
import functools
import math

import jax
import jax.numpy as jnp
from jax import lax
from jax.experimental import pallas as pl
from jax.experimental.pallas import tpu as pltpu
from jax.sharding import PartitionSpec as P

MESH = pl.DeviceIdType.MESH
VM = pl.BlockSpec(memory_space=pltpu.VMEM)
DMA = pltpu.SemaphoreType.DMA
BF = jnp.bfloat16
F32 = jnp.float32

epsilon = 1e-06
rope_base = 1000000.0
masked_score = -1e30
KEYS = 512


class Place:
    def __init__(self):
        f = lax.axis_index("fsdp")
        c = lax.axis_index("ctx")
        self.y, self.z = f // 4, f % 4
        self.lo, self.k = c // 2, c % 2
        self.t = lax.axis_index("tp")

    def along_y(self, j):
        return {"fsdp": lax.rem(self.y + j, 4) * 4 + self.z}

    def along_z(self, j):
        return {"fsdp": self.y * 4 + lax.rem(self.z + j, 4)}

    @property
    def sibling(self):
        return {"ctx": self.lo * 2 + 1 - self.k}

    def in_ring(self, lo, t):
        return {"ctx": lo * 2 + self.k, "tp": t}

    @property
    def others(self):
        return [(self.lo, 1 - self.t), (1 - self.lo, self.t), (1 - self.lo, 1 - self.t)]


def greet(devices):
    barrier = pltpu.get_barrier_semaphore()
    for device in devices:
        pl.semaphore_signal(barrier, inc=1, device_id=device, device_id_type=MESH)
    pl.semaphore_wait(barrier, len(devices))


def describe(source, target, send_sem, recv_sem, device):
    return pltpu.make_async_remote_copy(
        src_ref=source,
        dst_ref=target,
        send_sem=send_sem,
        recv_sem=recv_sem,
        device_id=device,
        device_id_type=MESH,
    )


def send(source, target, send_sem, recv_sem, device):
    copy = describe(source, target, send_sem, recv_sem, device)
    copy.start()
    return copy


def comm_call(body, outs, scratch, collective_id, mib, *args):
    return pl.pallas_call(
        body,
        out_shape=outs,
        in_specs=[VM] * len(args),
        out_specs=[VM] * len(outs),
        scratch_shapes=scratch,
        compiler_params=pltpu.CompilerParams(
            collective_id=collective_id, has_side_effects=True, vmem_limit_bytes=mib << 20
        ),
    )(*args)


def shape(dims, kind):
    return jax.ShapeDtypeStruct(dims, kind)


def opening_kernel(
    w, down, tok, dy, w_all, downs, tok2, dy_all, s1, r1, s2, r2, s3, r3, ts, tr, ds, dr, fs, fr
):
    me = Place()
    y, z, lo, k, t = me.y, me.z, me.lo, me.k, me.t
    rows = w.shape[0] // 2
    halves = (pl.ds(0, rows), pl.ds(rows, rows))
    near = [me.in_ring(1 - lo, t), me.in_ring(1 - lo, 1 - t)]
    greet(
        [me.along_z(j) for j in (1, 2, 3)]
        + [me.along_y(j) for j in (1, 2, 3)]
        + [me.sibling]
        + near
    )
    first = []
    for half, along in ((0, me.along_z), (1, me.along_y)):
        part = halves[half]
        first.append(
            [
                send(
                    w.at[part],
                    w_all.at[y, z, part],
                    s1.at[half, j - 1],
                    r1.at[half, j - 1],
                    along(j),
                )
                for j in (2, 1, 3)
            ]
        )
    rest = []
    mine = dy.shape[0] // 2
    near_copies = [
        send(dy.at[pl.ds(t * mine, mine)], dy_all.at[lo, t, k], ds.at[i], dr.at[i], near[i])
        for i in (0, 1)
    ]
    rest.append(send(tok, tok2.at[k], ts, tr, me.sibling))
    own = [
        send(
            dy.at[pl.ds(h * mine, mine)], dy_all.at[lo, h, k], fs.at[2 + h], fr.at[2 + h], me.sibling
        )
        for h in (0, 1)
    ]
    rest += own
    for half, along in ((0, me.along_y), (1, me.along_z)):
        part = halves[half]
        for j in (2, 1, 3):
            rest.append(
                send(
                    w.at[part],
                    w_all.at[y, z, part],
                    s2.at[half, 0, j - 1],
                    r2.at[half, 0, j - 1],
                    along(j),
                )
            )
    for half, along, here in ((0, me.along_z, z), (1, me.along_y, y)):
        for j in (2, 1, 3):
            rest.append(
                send(
                    down.at[halves[half]],
                    downs.at[half, here],
                    s3.at[half, j - 1],
                    r3.at[half, j - 1],
                    along(j),
                )
            )
        downs[half, here] = down[halves[half]]
    w_all[y, z] = w[...]
    tok2[k] = tok[...]
    for h in (0, 1):
        dy_all[lo, h, k] = dy[pl.ds(h * mine, mine)]
    for order in range(3):
        for half, along in ((0, me.along_y), (1, me.along_z)):
            part = halves[half]
            offset = (2, 1, 3)[order]
            first[half][order].wait()
            if half == 0:
                block = w_all.at[y, lax.rem(z - offset + 4, 4), part]
            else:
                block = w_all.at[lax.rem(y - offset + 4, 4), z, part]
            for j in (2, 1, 3):
                rest.append(
                    send(
                        block,
                        block,
                        s2.at[half, offset, j - 1],
                        r2.at[half, offset, j - 1],
                        along(j),
                    )
                )
    for i, half in ((0, t), (1, 1 - t)):
        near_copies[i].wait()
        block = dy_all.at[1 - lo, half, k]
        rest.append(send(block, block, fs.at[i], fr.at[i], me.sibling))
    for copy in rest:
        copy.wait()


def opening(w, down, tok, dy):
    rows, width = w.shape
    count, model = tok.shape
    return comm_call(
        opening_kernel,
        [
            shape((4, 4, rows, width), BF),
            shape((2, 4, rows // 2, down.shape[1]), BF),
            shape((2, count, model), BF),
            shape((2, 2, 2, count // 2, model), BF),
        ],
        [
            DMA((2, 3)),
            DMA((2, 3)),
            DMA((2, 4, 3)),
            DMA((2, 4, 3)),
            DMA((2, 3)),
            DMA((2, 3)),
            DMA,
            DMA,
            DMA((2,)),
            DMA((2,)),
            DMA((4,)),
            DMA((4,)),
        ],
        1,
        32,
        w,
        down,
        tok,
        dy,
    )


def keys_kernel(mine, kv, s1, r1, s2, r2):
    me = Place()
    k = me.k
    own = me.z * 2 + me.lo
    steps = [(dz, dl) for dz in (2, 1, 3, 0) for dl in (0, 1) if dz or dl]

    def partner(dz, dl):
        return {
            "fsdp": me.y * 4 + lax.rem(me.z + dz, 4),
            "ctx": lax.rem(me.lo + dl, 2) * 2 + k,
        }

    greet([partner(dz, dl) for dz, dl in steps] + [me.sibling])
    copies = [
        send(mine, kv.at[k, own], s1.at[i], r1.at[i], partner(dz, dl))
        for i, (dz, dl) in enumerate(steps)
    ]
    rest = [send(mine, kv.at[k, own], s2.at[7], r2.at[7], me.sibling)]
    kv[k, own] = mine[...]
    for i in (6, 2, 4, 3, 5, 0, 1):
        dz, dl = steps[i]
        copies[i].wait()
        block = kv.at[k, lax.rem(me.z - dz + 4, 4) * 2 + lax.rem(me.lo + dl, 2)]
        rest.append(send(block, block, s2.at[i], r2.at[i], me.sibling))
    for copy in rest:
        copy.wait()


def share_keys(mine):
    rows, width = mine.shape
    return comm_call(
        keys_kernel,
        [shape((2, 8, rows, width), BF)],
        [DMA((7,)), DMA((7,)), DMA((8,)), DMA((8,))],
        2,
        16,
        mine,
    )[0]


def over_rows(a, b):
    return lax.dot_general(a, b, (((0,), (0,)), ((), ())), preferred_element_type=F32)


def by_columns(a, b):
    return lax.dot_general(a, b, (((1,), (1,)), ((), ())), preferred_element_type=F32)


def plain(a, b):
    return lax.dot_general(a, b, (((1,), (0,)), ((), ())), preferred_element_type=F32)


def visible_pairs(block, first, start, rows):
    key = block * KEYS + lax.broadcasted_iota(jnp.int32, (KEYS, rows), 0)
    row = first + lax.broadcasted_iota(jnp.int32, (1, rows), 1)
    return (key >= start) & (key <= row)


def attend_kernel(heads, start_ref, q, kv, o, exact, lse, top, total, acc):
    me = Place()
    rows = q.shape[0]
    size = q.shape[1] // heads
    index = me.z * 2 + me.lo
    first = index * rows
    start = start_ref[...]
    top[...] = jnp.full_like(top, masked_score)
    total[...] = jnp.zeros_like(total)
    acc[...] = jnp.zeros_like(acc)

    def step(block, _):
        keys = kv[0, block]
        values = kv[1, block]
        seen = visible_pairs(block, first, start, rows)
        for h in range(heads):
            s = by_columns(keys, q[:, h * size : (h + 1) * size])
            s = jnp.where(seen, s, masked_score)
            before = top[h : h + 1]
            now = jnp.maximum(before, jnp.max(s, axis=0, keepdims=True))
            p = jnp.exp(s - now)
            shrink = jnp.exp(before - now)
            top[h : h + 1] = now
            total[h : h + 1] = total[h : h + 1] * shrink + jnp.sum(p, axis=0, keepdims=True)
            acc[h] = acc[h] * shrink + over_rows(values, p.astype(BF))
        return 0

    lax.fori_loop(0, index + 1, step, 0)
    lse[...] = jnp.zeros_like(lse)
    for h in range(heads):
        sums = total[h : h + 1]
        lse[h : h + 1] = top[h : h + 1] + jnp.log(sums)
        out = acc[h] / sums
        exact[h] = out
        o[:, h * size : (h + 1) * size] = out.T.astype(BF)


def attend(start, q, kv, heads):
    rows, width = q.shape
    return pl.pallas_call(
        functools.partial(attend_kernel, heads),
        out_shape=[
            shape((rows, width), BF),
            shape((heads, width // heads, rows), F32),
            shape((8, rows), F32),
        ],
        in_specs=[VM] * 3,
        out_specs=[VM] * 3,
        scratch_shapes=[
            pltpu.VMEM((8, rows), F32),
            pltpu.VMEM((8, rows), F32),
            pltpu.VMEM((heads, width // heads, rows), F32),
        ],
        compiler_params=pltpu.CompilerParams(vmem_limit_bytes=32 << 20),
    )(start, q, kv)


def norm_back(grad_normed, normed, factor):
    return factor * (grad_normed - normed * jnp.mean(grad_normed * normed, axis=-1, keepdims=True))


def block_kernel(
    part, tok, gain, downs, dy_hbm, w_hbm,
    x1, dx1, dxl, gnf, ysum, down_sum, g_hbm,
    w, dy, dy_t, h2, h2_t, hid, gate_back, up_back, whole, m1, m2, m3, pb, s1, r1, r2, yb, ry, pd,
    bs, br, cs, cr, ls, ms, hs, hr, fs, fr, ps, pr, xs, xr, ys, yr, gs, gr,
):
    me = Place()
    y, z, lo, k, t = me.y, me.z, me.lo, me.k, me.t
    rows, model = tok.shape
    both = 2 * rows
    inner = w.shape[-1]
    offsets = (2, 1, 3)

    def chip(i):
        return lax.rem(lo + lax.rem((i + 1) // 2, 2), 2), lax.rem(t + i // 2, 2)

    def columns(i):
        return pl.ds(pl.multiple_of(i * both, both), both)

    loads = [pltpu.make_async_copy(dy_hbm, dy, ls.at[3])]
    loads += [pltpu.make_async_copy(w_hbm.at[i], w.at[i], ls.at[i]) for i in range(2)]
    for copy in loads:
        copy.start()
    greet(
        [me.in_ring(*chip(i)) for i in (1, 2, 3)]
        + [me.sibling]
        + [me.along_z(j) for j in (1, 2, 3)]
        + [me.along_y(j) for j in (1, 2, 3)]
    )
    cores = send(part.at[1 - k], m1, ms.at[0], ms.at[1], me.sibling)
    here = w.at[2]
    downs_out = []
    for j in offsets:
        downs_out.append(
            send(downs.at[0], here.at[y, :, 0], bs.at[0, j - 1], br.at[0, j - 1], me.along_y(j))
        )
        downs_out.append(
            send(downs.at[1], here.at[:, z, 1], bs.at[1, j - 1], br.at[1, j - 1], me.along_z(j))
        )
    w[2, y, :, 0] = downs[0]
    w[2, :, z, 1] = downs[1]
    loads[0].wait()

    def weight(i):
        return w[i].reshape(model, inner)


    def turn_dy(i, _):
        lo_i, t_i = chip(i)
        dy_t[:, columns(i)] = dy[lo_i, t_i].reshape(both, model).T
        return 0

    cores.wait()
    m2[...] = (part[k, 1 - t].astype(F32) + m1[1 - t].astype(F32)).astype(BF)
    across = send(m2, m3, ms.at[2], ms.at[3], me.in_ring(lo, 1 - t))
    lax.fori_loop(0, 4, turn_dy, 0)
    x = tok[...].astype(F32) + part[k, t].astype(F32) + m1[t].astype(F32)
    across.wait()
    x = x + m3[...].astype(F32)
    x1[...] = x
    factor = lax.rsqrt(jnp.mean(x * x, axis=-1, keepdims=True) + epsilon)
    h2[lo, t, k] = (x * factor * gain[...]).astype(BF)

    def hidden_copy(i):
        block = h2.at[lo, t, k]
        return describe(block, block, hs.at[i - 1], hr.at[i - 1], me.in_ring(*chip(i)))

    def hidden_share(i):
        lo_i, t_i = chip(i)
        block = h2.at[lo_i, t_i, k]
        return describe(block, block, fs.at[i], fr.at[i], me.sibling)

    def part_share(i):
        return describe(pb.at[i], r1.at[i], ps.at[i], pr.at[i], me.sibling)

    def part_copy(i):
        return describe(
            s1.at[i], r2.at[i - 1], xs.at[i - 1], xr.at[i - 1], me.in_ring(*chip(i))
        )

    def result_share(i):
        return describe(yb.at[i], ry.at[i], ys.at[i], yr.at[i], me.sibling)

    for i in (1, 2, 3):
        hidden_copy(i).start()
    hidden_share(0).start()
    for copy in loads[1:] + downs_out:
        copy.wait()

    def finish(i):
        part_share(i).wait_recv()
        s1[i] = (s1[i].astype(F32) + r1[i].astype(F32)).astype(BF)

        @pl.when(i > 0)
        def _():
            part_copy(i).start()

        whole[...] = by_columns(hid[i], weight(2)).reshape(2, rows, model)
        yb[i] = whole[1 - k].astype(BF)
        ysum[i] = whole[k].astype(BF)
        result_share(i).start()
        lo_i, t_i = chip(i)
        h2_t[:, columns(i)] = h2[lo_i, t_i].reshape(both, model).T

    def step(i, _):
        lo_i, t_i = chip(i)

        @pl.when(i > 0)
        def _():
            hidden_copy(i).wait_recv()
            hidden_share(i).start()
            finish(i - 1)

        hidden_share(i).wait_recv()
        h = h2[lo_i, t_i].reshape(both, model)
        d = dy[lo_i, t_i].reshape(both, model)
        gate = plain(h, weight(0))
        up = plain(h, weight(1))
        sigmoid_gate = jax.nn.sigmoid(gate)
        silu_gate = gate * sigmoid_gate
        hid[i] = (silu_gate * up).astype(BF)
        grad_inner = plain(d, weight(2))
        slope = sigmoid_gate * (1.0 + gate * (1.0 - sigmoid_gate))
        gate_back[i] = (grad_inner * up * slope).astype(BF)
        up_back[i] = (grad_inner * silu_gate).astype(BF)
        whole[...] = (
            by_columns(gate_back[i], weight(0)) + by_columns(up_back[i], weight(1))
        ).reshape(2, rows, model)
        pb[i] = whole[1 - k].astype(BF)
        s1[i] = whole[k].astype(BF)
        part_share(i).start()
        return 0

    lax.fori_loop(0, 4, step, 0)
    finish(3)

    def gradient(i, left_t, right):
        flat = right.shape[0] * right.shape[1]
        step_rows = model // 4

        def some(m, _):
            r = pl.ds(pl.multiple_of(m * step_rows, step_rows), step_rows)
            value = plain(left_t[r, :], right[...].reshape(flat, inner))
            w[i, m] = value.astype(BF).reshape(w.shape[2:])
            return 0

        lax.fori_loop(0, 4, some, 0)

    def gradient_out(i):
        copy = pltpu.make_async_copy(w.at[i], g_hbm.at[i], ls.at[i])
        copy.start()
        return copy

    gradient(2, dy_t, hid)
    downs_back = []
    for j in offsets:
        downs_back.append(
            send(
                here.at[:, lax.rem(z + j, 4), 0], pd.at[0, j - 1], cs.at[0, j - 1], cr.at[0, j - 1], me.along_z(j)
            )
        )
        downs_back.append(
            send(
                here.at[lax.rem(y + j, 4), :, 1], pd.at[1, j - 1], cs.at[1, j - 1], cr.at[1, j - 1], me.along_y(j)
            )
        )

    grad = s1[0].astype(F32)
    for i in (1, 2, 3):
        part_copy(i).wait_recv()
        grad = grad + r2[i - 1].astype(F32)
    x = x1[...]
    factor = lax.rsqrt(jnp.mean(x * x, axis=-1, keepdims=True) + epsilon)
    normed = x * factor
    gnf[...] = jnp.sum(grad * normed, axis=0, keepdims=True)
    back = dy[lo, t, k].astype(F32) + norm_back(grad * gain[...], normed, factor)
    dx1[...] = back
    dxl[k, t] = back.astype(BF)
    block = dxl.at[k, t]
    across = send(block, block, gs.at[0], gr.at[0], me.in_ring(lo, 1 - t))
    rest = [send(block, block, gs.at[1], gr.at[1], me.sibling)]
    gradient(0, h2_t, gate_back)
    outs = [gradient_out(0)]
    across.wait()
    block = dxl.at[k, 1 - t]
    rest.append(send(block, block, gs.at[2], gr.at[2], me.sibling))
    gradient(1, h2_t, up_back)
    outs.append(gradient_out(1))
    for i in range(4):
        result_share(i).wait()
        ysum[i] = (ysum[i].astype(F32) + ry[i].astype(F32)).astype(BF)
        hidden_share(i).wait_send()
        part_share(i).wait_send()
    for i in (1, 2, 3):
        hidden_copy(i).wait_send()
        part_copy(i).wait_send()
    for copy in downs_back:
        copy.wait()
    for half in (0, 1):
        mine = w[2, :, z, 0] if half == 0 else w[2, y, :, 1]
        total = mine.astype(F32)
        for j in range(3):
            total = total + pd[half, j].astype(F32)
        down_sum[half] = total.astype(BF)
    for copy in rest + outs:
        copy.wait()


def block(part, tok, gain, downs, dy, w):
    rows, model = tok.shape
    hidden = w.shape[2]
    half_rows = model // 32
    w = w.reshape(2, 4, 4, 2, half_rows, hidden)
    any_place = pl.BlockSpec(memory_space=pl.ANY)
    quarter = pltpu.VMEM((4, rows, model), BF)
    inner = pltpu.VMEM((4, 2 * rows, hidden), BF)
    turned = pltpu.VMEM((model, 8 * rows), BF)
    return pl.pallas_call(
        block_kernel,
        out_shape=[
            shape((rows, model), F32),
            shape((rows, model), F32),
            shape((2, 2, rows, model), BF),
            shape((1, model), F32),
            shape((4, rows, model), BF),
            shape(downs.shape, BF),
            shape(w.shape, BF),
        ],
        in_specs=[VM] * 4 + [any_place] * 2,
        out_specs=[VM] * 6 + [any_place],
        scratch_shapes=[
            pltpu.VMEM((3,) + w.shape[1:], BF),
            pltpu.VMEM(dy.shape, BF),
            turned,
            pltpu.VMEM(dy.shape, BF),
            turned,
            inner,
            inner,
            inner,
            pltpu.VMEM((2, rows, model), F32),
            pltpu.VMEM((2, rows, model), BF),
            pltpu.VMEM((rows, model), BF),
            pltpu.VMEM((rows, model), BF),
            quarter,
            quarter,
            quarter,
            pltpu.VMEM((3, rows, model), BF),
            quarter,
            quarter,
            pltpu.VMEM((2, 3) + downs.shape[1:], BF),
            DMA((2, 3)),
            DMA((2, 3)),
            DMA((2, 3)),
            DMA((2, 3)),
            DMA((4,)),
            DMA((4,)),
            DMA((3,)),
            DMA((3,)),
            DMA((4,)),
            DMA((4,)),
            DMA((4,)),
            DMA((4,)),
            DMA((3,)),
            DMA((3,)),
            DMA((4,)),
            DMA((4,)),
            DMA((3,)),
            DMA((3,)),
        ],
        compiler_params=pltpu.CompilerParams(
            collective_id=3, has_side_effects=True, vmem_limit_bytes=62 << 20
        ),
    )(part, tok, gain, downs, dy, w)


def turned(values, cosines, sines):
    return values * cosines - pltpu.roll(values, values.shape[-1] // 2, 1) * sines


def rear_kernel(
    heads,
    g_hbm, down_sum, dxl, attn, q, kv, exact, lse, start_ref, ob, h1, cosines, sines, ysum, x1, dx1, tok, gain, gnf,
    a_all, ext_all, ffn_all, down_all, out, grad,
    do, dots, acc, keep, give, arrived, sums, landed, back, part, m1, m2, m3, left_t, ga,
    own, p1, p2, q1, sm, q2, fin, fin_d, wide, narrow, e0, e1, es, e2, y2,
    ls, d1, d2, d3, d4, ms, fs1, fr1, fs2, fr2, as1, ar1, as2, ar2, as3, ar3, xs, xr, ss, sr, ts, tr, us, ur, ys, yr,
    gs, gr,
):
    me = Place()
    y, z, lo, k, t = me.y, me.z, me.lo, me.k, me.t
    c = lo * 2 + k
    index = z * 2 + lo
    rows, width = q.shape
    size = width // heads
    slice_rows, model = tok.shape
    rowed = width + size
    offsets = (2, 1, 3)

    def in_x(dt, dc):
        return {"ctx": lax.rem(c + dc, 4), "tp": lax.rem(t + dt, 2)}

    def owner(b):
        return {"fsdp": y * 4 + b // 2, "ctx": lax.rem(b, 2) * 2 + k}

    ring = [(dt, dc) for dt in (0, 1) for dc in range(4) if dt or dc]

    def first_hop(w, half, j):
        if half == 0:
            source, device = g_hbm.at[w, :, lax.rem(z + j, 4), 0], me.along_z(j)
        else:
            source, device = g_hbm.at[w, lax.rem(y + j, 4), :, 1], me.along_y(j)
        return describe(
            source, p1.at[w, half, j - 1], fs1.at[w, half, j - 1], fr1.at[w, half, j - 1], device
        )

    def second_hop(w, half, j):
        if half == 0:
            source, device = own.at[w, 0, lax.rem(y + j, 4)], me.along_y(j)
        else:
            source, device = own.at[w, 1, lax.rem(z + j, 4)], me.along_z(j)
        return describe(
            source, p2.at[w, half, j - 1], fs2.at[w, half, j - 1], fr2.at[w, half, j - 1], device
        )

    def own_load(w, half):
        source = g_hbm.at[w, :, z, 0] if half == 0 else g_hbm.at[w, y, :, 1]
        return pltpu.make_async_copy(source, own.at[w, half], ls.at[w, half])

    def start_hop(half, *span):
        def some(w, _):
            for j in offsets:
                first_hop(w, half, j).start()
            own_load(w, half).start()
            return 0

        lax.fori_loop(*span, some, 0)

    greet(
        [me.along_z(j) for j in (1, 2, 3)]
        + [me.along_y(j) for j in (1, 2, 3)]
        + [in_x(dt, dc) for dt, dc in ring]
        + [{"fsdp": y * 4 + lax.rem(z + j, 4), "ctx": (1 - lo) * 2 + k} for j in (1, 2, 3)]
    )
    own[2] = down_sum[...]
    for half in (0, 1):
        for j in offsets:
            second_hop(2, half, j).start()
    start_hop(1, 0, 2)
    start_hop(0, 0, 1)
    near = [(1 - lo, t), (1 - lo, 1 - t), (lo, 1 - t)]
    results = [
        send(ysum.at[i + 1], y2.at[i], ys.at[i], yr.at[i], me.in_ring(*near[i])) for i in range(3)
    ]

    do[...] = plain(dxl[...], attn[:, rowed:]).astype(BF)
    for h in range(heads):
        product = exact[h] * do[:, h * size : (h + 1) * size].astype(F32).T
        dots[h : h + 1] = jnp.sum(product, axis=0, keepdims=True)
    acc[...] = jnp.zeros_like(acc)
    start = start_ref[...]
    first = index * rows

    def core_share(b):
        return describe(give.at[b], arrived.at[b], d1.at[b], d2.at[b], me.sibling)

    def home(b):
        return describe(sums.at[b], landed.at[index], d3.at[b], d4.at[index], owner(b))

    def step(b, _):
        keys = kv[0, b]
        values = kv[1, b]
        seen = visible_pairs(b, first, start, rows)
        dk = jnp.zeros((KEYS, size), F32)
        dv = jnp.zeros((KEYS, size), F32)
        for h in range(heads):
            q_h = q[:, h * size : (h + 1) * size]
            do_h = do[:, h * size : (h + 1) * size]
            s = jnp.where(seen, by_columns(keys, q_h), masked_score)
            p = jnp.exp(s - lse[h : h + 1])
            dv = dv + plain(p.astype(BF), do_h)
            dp = by_columns(values, do_h)
            ds = (p * (dp - dots[h : h + 1])).astype(BF)
            dk = dk + plain(ds, q_h)
            acc[h] = acc[h] + over_rows(keys, ds)
        keep[b] = jnp.where(k == 0, dk, dv)
        give[b] = jnp.where(k == 0, dv, dk)
        core_share(b).start()

        @pl.when(b > 0)
        def _():
            core_share(b - 1).wait_recv()
            sums[b - 1] = (keep[b - 1] + arrived[b - 1]).astype(BF)
            home(b - 1).start()

        return 0

    lax.fori_loop(0, index + 1, step, 0)
    start_hop(0, 1, 2)

    scale = 1.0 / math.sqrt(size)
    for h in range(heads):
        dq = turned(acc[h].T * scale, cosines[...], -sines[...])
        e0[2:3, h * size : (h + 1) * size] = jnp.sum(dq, axis=0, keepdims=True)
        back[:, h * size : (h + 1) * size] = dq.astype(BF)
    left_t[...] = dxl[...].T
    blocks = ga.shape[:4]

    def spread(value):
        return value.astype(BF).reshape(blocks + (value.shape[1],))

    ga[:, :, :, :, rowed:] = spread(plain(left_t[...], ob[...]))
    left_t[...] = h1[...].T
    ga[:, :, :, :, :width] = spread(plain(left_t[...], back[:, :width]))

    core_share(index).wait_recv()
    dkv = keep[index] + arrived[index]
    keep[index] = dkv
    for b in range(1, 8):

        @pl.when(b > index)
        def _():
            describe(sums.at[0], landed.at[b], d3.at[0], d4.at[b], owner(0)).wait_recv()
            keep[index] = keep[index] + landed[b].astype(F32)

    is_key = k == 0
    dkv = turned(
        keep[index], jnp.where(is_key, cosines[...], 1.0), jnp.where(is_key, -sines[...], 0.0)
    )
    e0[2:3, width:rowed] = jnp.sum(dkv, axis=0, keepdims=True)
    back[:, width:] = dkv.astype(BF)
    part[...] = (
        by_columns(back[...], attn[:, :rowed]).astype(BF).reshape(2, 2, slice_rows, model)
    )
    cores = send(part.at[1 - k], m1, ms.at[0], ms.at[1], me.sibling)
    ga[:, :, :, :, width:rowed] = spread(plain(left_t[...], back[:, width:]))

    large = []
    for j in offsets:
        large.append(
            send(
                ga.at[:, lax.rem(z + j, 4), 0], q1.at[0, j - 1], as1.at[0, j - 1], ar1.at[0, j - 1], me.along_z(j)
            )
        )
        large.append(
            send(
                ga.at[lax.rem(y + j, 4), :, 1], q1.at[1, j - 1], as1.at[1, j - 1], ar1.at[1, j - 1], me.along_y(j)
            )
        )

    cores.wait()
    m2[...] = (part[k, 1 - t].astype(F32) + m1[1 - t].astype(F32)).astype(BF)
    across = send(m2, m3, ms.at[2], ms.at[3], me.in_ring(lo, 1 - t))
    x = tok[...].astype(F32)
    factor = lax.rsqrt(jnp.mean(x * x, axis=-1, keepdims=True) + epsilon)
    normed = x * factor
    dh1 = part[k, t].astype(F32) + m1[t].astype(F32)
    across.wait()
    dh1 = dh1 + m3[...].astype(F32)
    e0[0:1] = jnp.sum(dh1 * normed, axis=0, keepdims=True)
    e0[1:2] = gnf[...]
    e0[2:3, rowed:] = jnp.zeros((1, model - rowed), F32)
    e0[3:] = jnp.zeros((5, model), F32)
    small = [
        send(e0, e1.at[j - 1], ss.at[0, j - 1], sr.at[0, j - 1], me.along_z(j)) for j in offsets
    ]
    grad[t] = (dx1[...] + norm_back(dh1 * gain[...], normed, factor)).astype(BF)
    mine = grad.at[t]
    rest = [send(mine, mine, gs.at[0], gr.at[0], me.in_ring(lo, 1 - t))]

    quarter = sm.shape[2] // 2

    def summed(w, half):
        for j in offsets:
            second_hop(w, half, j).wait()
        here = own[w, 0, y] if half == 0 else own[w, 1, z]
        total = here.astype(F32)
        for j in range(3):
            total = total + p2[w, half, j].astype(F32)
        return total

    for half in (0, 1):
        total = summed(2, half)
        fin_d[2 * half] = total[:quarter]
        fin_d[2 * half + 1] = total[quarter:]
    down_all[c] = fin_d[c]
    rest += [
        send(fin_d.at[lax.rem(c + j, 4)], down_all.at[c], us.at[j - 1], ur.at[j - 1], in_x(0, j))
        for j in (2, 1, 3)
    ]

    result = x1[...] + ysum[0].astype(F32)
    for i in range(3):
        results[i].wait()
        result = result + y2[i].astype(F32)
    out[t] = result.astype(BF)
    mine = out.at[t]
    rest.append(send(mine, mine, gs.at[1], gr.at[1], me.in_ring(lo, 1 - t)))

    for copy in small:
        copy.wait()
    es[...] = (e0[...] + e1[0]) + (e1[1] + e1[2])
    small = [
        send(es, e2.at[j - 1], ss.at[1, j - 1], sr.at[1, j - 1], me.along_y(j)) for j in offsets
    ]

    def first_sum(w, _):
        for half in (0, 1):
            own_load(w, half).wait()
            for j in offsets:
                first_hop(w, half, j).wait()
            total = own[w, half].astype(F32)
            for j in range(3):
                total = total + p1[w, half, j].astype(F32)
            own[w, half] = total.astype(BF)
            for j in offsets:
                second_hop(w, half, j).start()
        return 0

    lax.fori_loop(0, 2, first_sum, 0)

    for copy in small:
        copy.wait()
    ext_all[t, c] = (es[...] + e2[0]) + (e2[1] + e2[2])
    mine = ext_all.at[t, c]
    rest += [
        send(mine, mine, xs.at[i], xr.at[i], in_x(dt, dc)) for i, (dt, dc) in enumerate(ring)
    ]
    for copy in large:
        copy.wait()
    for half in (0, 1):
        here = ga[:, z, 0] if half == 0 else ga[y, :, 1]
        total = here.astype(F32)
        for j in range(3):
            total = total + q1[half, j].astype(F32)
        sm[half] = total.astype(BF)
    last = []
    for j in offsets:
        last.append(
            send(
                sm.at[0, lax.rem(y + j, 4)], q2.at[0, j - 1], as2.at[0, j - 1], ar2.at[0, j - 1], me.along_y(j)
            )
        )
        last.append(
            send(
                sm.at[1, lax.rem(z + j, 4)], q2.at[1, j - 1], as2.at[1, j - 1], ar2.at[1, j - 1], me.along_z(j)
            )
        )

    def second_sum(w, _):
        for half in (0, 1):
            total = summed(w, half)
            place = pl.ds(pl.multiple_of(w * quarter, 8), quarter)
            wide[2 * half, place] = total[:quarter]
            wide[2 * half + 1, place] = total[quarter:]
        return 0

    lax.fori_loop(0, 2, second_sum, 0)
    narrow[...] = wide[...].astype(BF)
    ffn_all[c] = narrow[c]
    rest += [
        send(narrow.at[lax.rem(c + j, 4)], ffn_all.at[c], ts.at[j - 1], tr.at[j - 1], in_x(0, j))
        for j in (2, 1, 3)
    ]
    for copy in last:
        copy.wait()
    for half in (0, 1):
        here = sm[0, y] if half == 0 else sm[1, z]
        total = here.astype(F32)
        for j in range(3):
            total = total + q2[half, j].astype(F32)
        fin[2 * half] = total[:quarter]
        fin[2 * half + 1] = total[quarter:]
    a_all[c] = fin[c]
    rest += [
        send(fin.at[lax.rem(c + j, 4)], a_all.at[c], as3.at[j - 1], ar3.at[j - 1], in_x(0, j))
        for j in (2, 1, 3)
    ]

    def sent(b, _):
        core_share(b).wait_send()

        @pl.when(b < index)
        def _():
            home(b).wait_send()

        return 0

    lax.fori_loop(0, index + 1, sent, 0)
    for copy in rest:
        copy.wait()


def rear(heads, g, down_sum, dxl, attn, q, kv, exact, lse, start, ob, h1, cosines, sines, ysum, x1, dx1, tok, gain, gnf):
    rows, width = q.shape
    size = width // heads
    slice_rows, model = tok.shape
    hidden = g.shape[-1]
    total = attn.shape[1]
    half_rows = model // 32
    quarter = half_rows // 2
    packed = 2 * quarter
    shared = pltpu.VMEM(kv.shape[1:], F32)
    shared_low = pltpu.VMEM(kv.shape[1:], BF)
    slab = pltpu.VMEM((slice_rows, model), BF)
    args = (down_sum, dxl, attn, q, kv, exact, lse, start, ob, h1, cosines, sines, ysum, x1, dx1, tok, gain, gnf)
    outs = [
        shape((4, quarter, total), F32),
        shape((2, 4, 8, model), F32),
        shape((4, packed, hidden), BF),
        shape((4, quarter, hidden), F32),
        shape((2, slice_rows, model), BF),
        shape((2, slice_rows, model), BF),
    ]
    return pl.pallas_call(
        functools.partial(rear_kernel, heads),
        out_shape=outs,
        in_specs=[pl.BlockSpec(memory_space=pl.ANY)] + [VM] * len(args),
        out_specs=[VM] * len(outs),
        scratch_shapes=[
            pltpu.VMEM((rows, width), BF),
            pltpu.VMEM((8, rows), F32),
            pltpu.VMEM((heads, size, rows), F32),
            shared,
            shared,
            shared,
            shared_low,
            shared_low,
            pltpu.VMEM((rows, width + size), BF),
            pltpu.VMEM((2, 2, slice_rows, model), BF),
            pltpu.VMEM((2, slice_rows, model), BF),
            slab,
            slab,
            pltpu.VMEM((model, rows), BF),
            pltpu.VMEM((4, 4, 2, half_rows, total), BF),
            pltpu.VMEM((3, 2, 4, half_rows, hidden), BF),
            pltpu.VMEM((2, 2, 3, 4, half_rows, hidden), BF),
            pltpu.VMEM((3, 2, 3, half_rows, hidden), BF),
            pltpu.VMEM((2, 3, 4, half_rows, total), BF),
            pltpu.VMEM((2, 4, half_rows, total), BF),
            pltpu.VMEM((2, 3, half_rows, total), BF),
            pltpu.VMEM((4, quarter, total), F32),
            pltpu.VMEM((4, quarter, hidden), F32),
            pltpu.VMEM((4, packed, hidden), F32),
            pltpu.VMEM((4, packed, hidden), BF),
            pltpu.VMEM((8, model), F32),
            pltpu.VMEM((3, 8, model), F32),
            pltpu.VMEM((8, model), F32),
            pltpu.VMEM((3, 8, model), F32),
            pltpu.VMEM((3, slice_rows, model), BF),
            DMA((2, 2)),
            DMA((8,)),
            DMA((8,)),
            DMA((8,)),
            DMA((8,)),
            DMA((4,)),
            DMA((2, 2, 3)),
            DMA((2, 2, 3)),
            DMA((3, 2, 3)),
            DMA((3, 2, 3)),
            DMA((2, 3)),
            DMA((2, 3)),
            DMA((2, 3)),
            DMA((2, 3)),
            DMA((3,)),
            DMA((3,)),
            DMA((7,)),
            DMA((7,)),
            DMA((2, 3)),
            DMA((2, 3)),
            DMA((3,)),
            DMA((3,)),
            DMA((3,)),
            DMA((3,)),
            DMA((3,)),
            DMA((3,)),
            DMA((2,)),
            DMA((2,)),
        ],
        compiler_params=pltpu.CompilerParams(
            collective_id=7, has_side_effects=True, vmem_limit_bytes=62 << 20
        ),
    )(g, *args)


def rotate(values_in, cosine, sine):
    half_size = values_in.shape[-1] // 2
    front, back = values_in[..., :half_size], values_in[..., half_size:]
    return jnp.concatenate([front * cosine - back * sine, back * cosine + front * sine], axis=-1)


def shards(
    tokens,
    segments,
    w_query,
    key_matrix,
    value_matrix,
    b_query,
    key_bias_vector,
    value_bias_vector,
    w_out,
    norm_attn,
    norm_ffn,
    w_gate,
    w_up,
    w_down,
    cotangent,
):
    f = lax.axis_index("fsdp")
    c = lax.axis_index("ctx")
    t = lax.axis_index("tp")
    seq, quarter = f // 4, f % 4
    lo, k = c // 2, c % 2
    is_key = k == 0
    size = key_matrix.shape[1]
    query_width = w_query.shape[1] // 2
    heads = query_width // size
    own_width = query_width + size
    model = tokens.shape[1]
    count = tokens.shape[0]
    slice_rows = count // 2
    shard_rows = w_query.shape[0]
    hidden = w_gate.shape[1] // 4
    padded = -(-hidden // 128) * 128

    def hidden_slice(w, axis):
        return lax.dynamic_slice_in_dim(w, c * hidden, hidden, axis)

    def widened(w):
        return jnp.pad(w, ((0, 0), (0, padded - hidden)))

    own_ffn = jnp.stack([widened(hidden_slice(w_gate, 1)), widened(hidden_slice(w_up, 1))])
    ffn_weights = lax.all_gather(own_ffn, "fsdp", axis=1, tiled=True)
    own_down = widened(hidden_slice(w_down, 0).T)

    own_attn = jnp.concatenate(
        [
            lax.dynamic_slice_in_dim(w_query, k * query_width, query_width, 1),
            jnp.where(is_key, key_matrix, value_matrix),
            lax.dynamic_slice_in_dim(w_out, k * query_width, query_width, 0).T,
        ],
        axis=1,
    )
    attn_all, downs, tok2, dy_all = opening(own_attn, own_down, tokens, cotangent)
    attn_all = attn_all.reshape(model, own_width + query_width)
    in_all, out_all = attn_all[:, :own_width], attn_all[:, own_width:]
    own_tokens = lax.dynamic_slice_in_dim(tokens, t * slice_rows, slice_rows, 0)

    seg_row = lax.dynamic_index_in_dim(segments, seq, 0, keepdims=False)
    rows = 2 * count
    first = (quarter * 2 + lo) * rows
    seg_mine = lax.dynamic_slice_in_dim(seg_row, first, rows)
    starts = jnp.zeros((rows,), jnp.int32)
    for number in range(1, 4):
        begin = jnp.sum((seg_row < number).astype(jnp.int32))
        starts = jnp.where(seg_mine == number, begin, starts)
    pos = (first + jnp.arange(rows, dtype=jnp.int32) - starts).astype(F32)
    frequency = jnp.exp(
        jnp.arange(size // 2, dtype=F32) * (-2.0 * math.log(rope_base) / size)
    )
    angles = pos[:, None, None] * frequency
    cosine, sine = jnp.cos(angles), jnp.sin(angles)
    kv_cosine = jnp.where(is_key, cosine[:, 0], 1.0)
    kv_sine = jnp.where(is_key, sine[:, 0], 0.0)
    starts = starts[None, :]
    query_scale = 1.0 / math.sqrt(size)

    gain_attn = norm_attn.astype(F32)
    gain_ffn = norm_ffn.astype(F32)
    x = tok2.reshape(rows, model).astype(F32)
    h1 = (x * lax.rsqrt(jnp.mean(x * x, axis=-1, keepdims=True) + epsilon) * gain_attn).astype(BF)
    bias = jnp.concatenate(
        [
            lax.dynamic_slice_in_dim(b_query, k * query_width, query_width, 0),
            jnp.where(is_key, key_bias_vector, value_bias_vector),
        ]
    ).astype(F32)
    linear = plain(h1, in_all) + bias
    q_lin = linear[:, :query_width].reshape(rows, heads, size)
    q = (rotate(q_lin, cosine, sine) * query_scale).astype(BF).reshape(rows, query_width)
    kv = share_keys(rotate(linear[:, query_width:], kv_cosine, kv_sine).astype(BF))
    ob, exact, lse = attend(starts, q, kv, heads)
    part = by_columns(ob, out_all).astype(BF).reshape(2, 2, slice_rows, model)
    x1, dx1, dxl, grad_norm_two, ysum, down_sum, ffn_grads = block(
        part, own_tokens, gain_ffn[None], downs, dy_all, ffn_weights
    )
    a_all, ext_all, ffn_all, down_all, output, grad_tokens = rear(
        heads,
        ffn_grads,
        down_sum,
        dxl.reshape(rows, model),
        attn_all,
        q,
        kv,
        exact,
        lse,
        starts,
        ob,
        h1,
        jnp.concatenate([cosine[:, 0], cosine[:, 0]], axis=1),
        jnp.concatenate([sine[:, 0], -sine[:, 0]], axis=1),
        ysum,
        x1,
        dx1,
        own_tokens,
        gain_attn[None],
        grad_norm_two,
    )
    owner_rows = shard_rows // 4
    a_all = a_all[:2] + a_all[2:]

    def side_by_side(pieces):
        return jnp.concatenate([pieces[i, :, :hidden].astype(F32) for i in range(4)], axis=1)

    owner = f * 4 + c
    norms = lax.dynamic_slice_in_dim(
        jnp.sum(ext_all[:, :, :2].reshape(8, 2, model), axis=0), owner * owner_rows, owner_rows, 1
    )
    biases = lax.dynamic_index_in_dim(ext_all[:, :, 2, :own_width], t, 0, keepdims=False)
    biases = (biases[:2] + biases[2:]).reshape(2, heads + 1, size)
    biases = lax.dynamic_slice_in_dim(biases, owner * 2, 2, 2)
    return (
        output.reshape(count, model),
        grad_tokens.reshape(count, model).astype(F32),
        jnp.concatenate([a_all[0, :, :query_width], a_all[1, :, :query_width]], axis=1),
        a_all[0, :, query_width:own_width],
        a_all[1, :, query_width:own_width],
        biases[:, :heads].reshape(2 * heads, 2),
        biases[0, heads:],
        biases[1, heads:],
        jnp.concatenate([a_all[0, :, own_width:], a_all[1, :, own_width:]], axis=1).T,
        norms[0],
        norms[1],
        side_by_side(ffn_all[:, :owner_rows]),
        side_by_side(ffn_all[:, owner_rows:]),
        side_by_side(down_all).T,
    )


def solution(mesh):
    both = ("fsdp", "ctx")
    in_specs = (
        P(both, None),
        P(),
        P("fsdp", "tp"),
        P("fsdp", "tp"),
        P("fsdp", "tp"),
        P("tp"),
        P("tp"),
        P("tp"),
        P("tp", "fsdp"),
        P(),
        P(),
        P("fsdp", "tp"),
        P("fsdp", "tp"),
        P("tp", "fsdp"),
        P(both, None),
    )
    out_specs = (
        P(both, None),
        P(both, None),
        P(both, "tp"),
        P(both, "tp"),
        P(both, "tp"),
        P("tp", both),
        P("tp", both),
        P("tp", both),
        P("tp", both),
        P(both),
        P(both),
        P(both, "tp"),
        P(both, "tp"),
        P("tp", both),
    )
    return jax.shard_map(shards, mesh=mesh, in_specs=in_specs, out_specs=out_specs, check_vma=False)
```

```python
import functools
import math

import jax
import jax.numpy as jnp
from jax import lax
from jax.experimental import pallas as pl
from jax.experimental.pallas import tpu as pltpu
from jax.sharding import PartitionSpec as P

MESH = pl.DeviceIdType.MESH
VM = pl.BlockSpec(memory_space=pltpu.VMEM)
DMA = pltpu.SemaphoreType.DMA
BF = jnp.bfloat16
F32 = jnp.float32

epsilon = 1e-06
rope_base = 1000000.0
masked_score = -1e30
KEYS = 512


class Place:
    def __init__(self):
        f = lax.axis_index("fsdp")
        c = lax.axis_index("ctx")
        self.y, self.z = f // 4, f % 4
        self.lo, self.k = c // 2, c % 2
        self.t = lax.axis_index("tp")

    def along_y(self, j):
        return {"fsdp": lax.rem(self.y + j, 4) * 4 + self.z}

    def along_z(self, j):
        return {"fsdp": self.y * 4 + lax.rem(self.z + j, 4)}

    @property
    def sibling(self):
        return {"ctx": self.lo * 2 + 1 - self.k}

    def in_ring(self, lo, t):
        return {"ctx": lo * 2 + self.k, "tp": t}

    @property
    def others(self):
        return [(self.lo, 1 - self.t), (1 - self.lo, self.t), (1 - self.lo, 1 - self.t)]


def greet(devices):
    barrier = pltpu.get_barrier_semaphore()
    for device in devices:
        pl.semaphore_signal(barrier, inc=1, device_id=device, device_id_type=MESH)
    pl.semaphore_wait(barrier, len(devices))


def describe(source, target, send_sem, recv_sem, device):
    return pltpu.make_async_remote_copy(
        src_ref=source,
        dst_ref=target,
        send_sem=send_sem,
        recv_sem=recv_sem,
        device_id=device,
        device_id_type=MESH,
    )


def send(source, target, send_sem, recv_sem, device):
    copy = describe(source, target, send_sem, recv_sem, device)
    copy.start()
    return copy


def comm_call(body, outs, scratch, collective_id, mib, *args):
    return pl.pallas_call(
        body,
        out_shape=outs,
        in_specs=[VM] * len(args),
        out_specs=[VM] * len(outs),
        scratch_shapes=scratch,
        compiler_params=pltpu.CompilerParams(
            collective_id=collective_id, has_side_effects=True, vmem_limit_bytes=mib << 20
        ),
    )(*args)


def shape(dims, kind):
    return jax.ShapeDtypeStruct(dims, kind)


def over_rows(a, b):
    return lax.dot_general(a, b, (((0,), (0,)), ((), ())), preferred_element_type=F32)


def by_columns(a, b):
    return lax.dot_general(a, b, (((1,), (1,)), ((), ())), preferred_element_type=F32)


def plain(a, b):
    return lax.dot_general(a, b, (((1,), (0,)), ((), ())), preferred_element_type=F32)


def visible_pairs(block, first, start, rows):
    key = block * KEYS + lax.broadcasted_iota(jnp.int32, (KEYS, rows), 0)
    row = first + lax.broadcasted_iota(jnp.int32, (1, rows), 1)
    return (key >= start) & (key <= row)


class RingGather:
    def __init__(self, along, position, pieces, target, source, sems):
        self.along, self.position, self.pieces = along, position, pieces
        self.target, self.source, self.sems = target, source, sems

    def hop(self, i, way):
        s, r = self.sems[:2]
        return describe(
            self.source(i),
            self.target(self.position, i),
            s.at[i, way],
            r.at[i, way],
            self.along(1 if way == 0 else 3),
        )

    def onward(self, i):
        s, r = self.sems[2:]
        way = i // 2
        block = self.target(lax.rem(self.position + (3 if way == 0 else 1), 4), i)
        return describe(block, block, s.at[i], r.at[i], self.along(1 if way == 0 else 3))

    def start(self, i):
        self.hop(i, 0).start()
        self.hop(i, 1).start()

    def forward(self, i):
        self.hop(i, i // 2).wait_recv()
        self.onward(i).start()

    def finish(self):
        for i in range(4):
            self.hop(i, 1 - i // 2).wait_recv()
            self.onward(i).wait()
            self.hop(i, 0).wait_send()
            self.hop(i, 1).wait_send()


def turned(values, cosines, sines):
    return values * cosines - pltpu.roll(values, values.shape[-1] // 2, 1) * sines


def front_kernel(
    heads,
    w, ffn, tok, dy, segments, gain, bias, frequency,
    w_all, gate_all, halves, dy_all, h1, q, kv, exact, ob, lse, starts, cosines, sines, part,
    tok2, top, total, acc,
    s1, r1, wa, wb, wc, wd, s3, r3, ga, gb, gc, gd, ts, tr, ds, dr, fs, fr, ks, kr, cs, cr,
):
    me = Place()
    y, z, lo, k, t = me.y, me.z, me.lo, me.k, me.t
    index = z * 2 + lo
    count, model = tok.shape
    rows = 2 * count
    width, size = q.shape[1], exact.shape[1]
    rowed = width + size
    shard = w.shape[0] // 2
    parts = (pl.ds(0, shard), pl.ds(shard, shard))
    near = [me.in_ring(1 - lo, t), me.in_ring(1 - lo, 1 - t)]
    offsets = (1, 3, 2)
    greet(
        [me.along_z(j) for j in (1, 2, 3)]
        + [me.along_y(j) for j in (1, 2, 3)]
        + [me.sibling]
        + near
        + [{"fsdp": y * 4 + lax.rem(z + j, 4), "ctx": (1 - lo) * 2 + k} for j in (1, 2, 3)]
    )

    def attn_place(half, position, i):
        if half == 0:
            return w_all.at[position, lax.rem(z + 4 - i, 4), parts[0]]
        return w_all.at[lax.rem(y + 4 - i, 4), position, parts[1]]

    def attn_source(half, i):
        if i == 0:
            return w.at[parts[half]]
        return attn_place(half, y if half == 0 else z, i)

    def first_hop(half, j):
        along = me.along_z if half == 0 else me.along_y
        return describe(
            w.at[parts[half]],
            w_all.at[y, z, parts[half]],
            s1.at[half, j - 1],
            r1.at[half, j - 1],
            along(j),
        )

    rings = [
        RingGather(
            me.along_y if half == 0 else me.along_z,
            y if half == 0 else z,
            4,
            functools.partial(attn_place, half),
            functools.partial(attn_source, half),
            [sem.at[half] for sem in (wa, wb, wc, wd)],
        )
        for half in (0, 1)
    ]
    for j in offsets:
        for half in (0, 1):
            first_hop(half, j).start()
    for ring in rings:
        ring.start(0)
    tokens_share = send(tok, tok2, ts, tr, me.sibling)
    slab = count // 2
    near_copies = [
        send(dy.at[pl.ds(t * slab, slab)], dy_all.at[lo, t, k], ds.at[i], dr.at[i], near[i])
        for i in (0, 1)
    ]
    rest = [
        send(dy.at[pl.ds(h * slab, slab)], dy_all.at[lo, h, k], fs.at[2 + h], fr.at[2 + h], me.sibling)
        for h in (0, 1)
    ]
    w_all[y, z] = w[...]
    for h in (0, 1):
        dy_all[lo, h, k] = dy[pl.ds(h * slab, slab)]

    first = pl.multiple_of(index * rows, rows)
    everyone = segments[pl.ds(y, 1), :]
    mine = segments[pl.ds(y, 1), pl.ds(first, rows)]
    start = jnp.zeros((1, rows), jnp.int32)
    for number in (1, 2, 3):
        begin = jnp.sum(jnp.where(everyone < number, 1.0, 0.0), axis=1, keepdims=True)
        start = jnp.where(mine == number, begin.astype(jnp.int32), start)
    starts[...] = start
    row = first + lax.broadcasted_iota(jnp.int32, (1, rows), 1)
    pos = jnp.broadcast_to((row - start).astype(F32), (8, rows)).T[:, :1]
    angles = pos * frequency[...]
    lane = lax.broadcasted_iota(jnp.int32, (1, size), 1)
    cosines[...] = jnp.cos(angles)
    sines[...] = jnp.sin(angles) * jnp.where(lane < size // 2, 1.0, -1.0)

    for j in offsets:
        for half in (0, 1):
            first_hop(half, j).wait()
            rings[half].start(j)

    def normed(x):
        x = x.astype(F32)
        factor = lax.rsqrt(jnp.mean(x * x, axis=-1, keepdims=True) + epsilon)
        return (x * factor * gain[...]).astype(BF)

    h1[pl.ds(pl.multiple_of(k * count, count), count)] = normed(tok[...])
    tokens_share.wait()
    h1[pl.ds(pl.multiple_of((1 - k) * count, count), count)] = normed(tok2[...])

    for i in (0, 1, 3, 2):
        for ring in rings:
            ring.forward(i)

    def ffn_hop(i, half, j):
        along, here = (me.along_z, z) if half == 0 else (me.along_y, y)
        return describe(
            ffn.at[i, parts[half]],
            halves.at[i, half, here],
            s3.at[i, half, j - 1],
            r3.at[i, half, j - 1],
            along(j),
        )

    for i in range(3):
        for half in (0, 1):
            for j in offsets:
                ffn_hop(i, half, j).start()
            halves[i, half, z if half == 0 else y] = ffn[i, parts[half]]
    for ring in rings:
        ring.finish()

    inward = w_all[:, :, :, :rowed].reshape(model, rowed)
    linear = plain(h1[...], inward) + bias[...]
    scale = 1.0 / math.sqrt(size)
    is_key = k == 0
    own = turned(
        linear[:, width:],
        jnp.where(is_key, cosines[...], 1.0),
        jnp.where(is_key, sines[...], 0.0),
    )
    kv[k, index] = own.astype(BF)
    block = kv.at[k, index]

    def keys_copy(i, device):
        return describe(block, block, ks.at[i], kr.at[index], device)

    targets = [(dz, to) for dz in (1, 2, 3) for to in (0, 1)]

    def target(dz, to):
        return {"fsdp": y * 4 + lax.rem(z + dz, 4), "ctx": to * 2 + k}

    for i, (dz, to) in enumerate(targets):

        @pl.when(z + dz < 4)
        def _():
            keys_copy(i, target(dz, to)).start()

    @pl.when(lo == 0)
    def _():
        keys_copy(6, {"ctx": 2 + k}).start()

    def keys_share(b):
        there = kv.at[k, b]
        return describe(there, there, cs.at[b], cr.at[b], me.sibling)

    keys_share(index).start()
    for h in range(heads):
        here = slice(h * size, (h + 1) * size)
        q[:, here] = (turned(linear[:, here], cosines[...], sines[...]) * scale).astype(BF)

    def gate_place(half, position, i):
        if half == 0:
            return gate_all.at[position, lax.rem(z + 4 - i, 4), 0]
        return gate_all.at[lax.rem(y + 4 - i, 4), position, 1]

    def gate_source(half, i):
        return halves.at[0, half, lax.rem((z if half == 0 else y) + 4 - i, 4)]

    gates = [
        RingGather(
            me.along_y if half == 0 else me.along_z,
            y if half == 0 else z,
            4,
            functools.partial(gate_place, half),
            functools.partial(gate_source, half),
            [sem.at[half] for sem in (ga, gb, gc, gd)],
        )
        for half in (0, 1)
    ]
    for half in (0, 1):
        for j in offsets:
            ffn_hop(0, half, j).wait()
        for i in range(4):
            gates[half].start(i)
    gate_all[y, :, 0] = halves[0, 0]
    gate_all[:, z, 1] = halves[0, 1]
    for i, half in ((0, t), (1, 1 - t)):
        near_copies[i].wait()
        there = dy_all.at[1 - lo, half, k]
        rest.append(send(there, there, fs.at[i], fr.at[i], me.sibling))

    top[...] = jnp.full_like(top, masked_score)
    total[...] = jnp.zeros_like(total)
    acc[...] = jnp.zeros_like(acc)

    def step(i, _):
        b = index - i

        @pl.when(b > 0)
        def _():
            there = kv.at[k, b - 1]
            describe(there, there, ks.at[0], kr.at[b - 1], me.sibling).wait_recv()
            keys_share(b - 1).start()

        keys_share(b).wait_recv()
        keys = kv[0, b]
        values = kv[1, b]
        seen = visible_pairs(b, first, start, rows)
        for h in range(heads):
            s = by_columns(keys, q[:, h * size : (h + 1) * size])
            s = jnp.where(seen, s, masked_score)
            before = top[h : h + 1]
            now = jnp.maximum(before, jnp.max(s, axis=0, keepdims=True))
            p = jnp.exp(s - now)
            shrink = jnp.exp(before - now)
            top[h : h + 1] = now
            total[h : h + 1] = total[h : h + 1] * shrink + jnp.sum(p, axis=0, keepdims=True)
            acc[h] = acc[h] * shrink + over_rows(values, p.astype(BF))
        return 0

    lax.fori_loop(0, index + 1, step, 0)
    for half in (0, 1):
        for i in range(4):
            gates[half].forward(i)
    lse[...] = jnp.zeros_like(lse)
    for h in range(heads):
        sums = total[h : h + 1]
        lse[h : h + 1] = top[h : h + 1] + jnp.log(sums)
        out = acc[h] / sums
        exact[h] = out
        ob[:, h * size : (h + 1) * size] = out.T.astype(BF)
    outward = w_all[:, :, :, rowed:].reshape(model, width)
    part[...] = by_columns(ob[...], outward).astype(BF).reshape(part.shape)

    for i, (dz, to) in enumerate(targets):

        @pl.when(z + dz < 4)
        def _():
            keys_copy(i, target(dz, to)).wait_send()

    @pl.when(lo == 0)
    def _():
        keys_copy(6, {"ctx": 2 + k}).wait_send()

    def shared(b, _):
        keys_share(b).wait_send()
        return 0

    lax.fori_loop(0, index + 1, shared, 0)
    for i in (1, 2):
        for half in (0, 1):
            for j in offsets:
                ffn_hop(i, half, j).wait()
    for ring in gates:
        ring.finish()
    for copy in rest:
        copy.wait()


def front(heads, w, ffn, tok, dy, segments, gain, bias, frequency):
    shard, total = w.shape
    hidden = ffn.shape[2]
    count, model = tok.shape
    rows = 2 * count
    width = bias.shape[1] - frequency.shape[1]
    size = frequency.shape[1]
    args = (w, ffn, tok, dy, segments, gain, bias, frequency)
    outs = [
        shape((4, 4, shard, total), BF),
        shape((4, 4, 2, shard // 2, hidden), BF),
        shape((3, 2, 4, shard // 2, hidden), BF),
        shape((2, 2, 2, count // 2, model), BF),
        shape((rows, model), BF),
        shape((rows, width), BF),
        shape((2, 8, rows, size), BF),
        shape((heads, size, rows), F32),
        shape((rows, width), BF),
        shape((8, rows), F32),
        shape((1, rows), jnp.int32),
        shape((rows, size), F32),
        shape((rows, size), F32),
        shape((2, 2, count // 2, model), BF),
    ]
    return pl.pallas_call(
        functools.partial(front_kernel, heads),
        out_shape=outs,
        in_specs=[VM] * len(args),
        out_specs=[VM] * len(outs),
        scratch_shapes=[
            pltpu.VMEM((count, model), BF),
            pltpu.VMEM((8, rows), F32),
            pltpu.VMEM((8, rows), F32),
            pltpu.VMEM((heads, size, rows), F32),
            DMA((2, 3)),
            DMA((2, 3)),
            DMA((2, 4, 2)),
            DMA((2, 4, 2)),
            DMA((2, 4)),
            DMA((2, 4)),
            DMA((3, 2, 3)),
            DMA((3, 2, 3)),
            DMA((2, 4, 2)),
            DMA((2, 4, 2)),
            DMA((2, 4)),
            DMA((2, 4)),
            DMA,
            DMA,
            DMA((2,)),
            DMA((2,)),
            DMA((4,)),
            DMA((4,)),
            DMA((7,)),
            DMA((8,)),
            DMA((8,)),
            DMA((8,)),
        ],
        compiler_params=pltpu.CompilerParams(
            collective_id=1, has_side_effects=True, vmem_limit_bytes=56 << 20
        ),
    )(*args)


def norm_back(grad_normed, normed, factor):
    return factor * (grad_normed - normed * jnp.mean(grad_normed * normed, axis=-1, keepdims=True))


def block_kernel(
    part, tok, gain, dy_hbm, gate_hbm, halves,
    x1, dx1, dxl, gnf, ysum, down_sum, g_hbm,
    w, dy, dy_t, h2, h2_t, hid, gate_back, up_back, whole, m1, m2, m3, pb, s1, r1, r2, yb, ry, pd,
    ba, bb, bc, bd, cs, cr, ls, ms, hs, hr, fs, fr, ps, pr, xs, xr, ys, yr, gs, gr,
):
    me = Place()
    y, z, lo, k, t = me.y, me.z, me.lo, me.k, me.t
    rows, model = tok.shape
    both = 2 * rows
    inner = w.shape[-1]
    offsets = (2, 1, 3)

    def chip(i):
        return lax.rem(lo + lax.rem((i + 1) // 2, 2), 2), lax.rem(t + i // 2, 2)

    def columns(i):
        return pl.ds(pl.multiple_of(i * both, both), both)

    loads = [pltpu.make_async_copy(dy_hbm, dy, ls.at[3])]
    loads.append(pltpu.make_async_copy(gate_hbm, w.at[0], ls.at[0]))
    for i in (1, 2):
        loads.append(pltpu.make_async_copy(halves.at[i, 0], w.at[i, y, :, 0], ls.at[2 * i + 2]))
        loads.append(pltpu.make_async_copy(halves.at[i, 1], w.at[i, :, z, 1], ls.at[2 * i + 3]))
    for copy in loads:
        copy.start()
    greet(
        [me.in_ring(*chip(i)) for i in (1, 2, 3)]
        + [me.sibling]
        + [me.along_z(j) for j in (1, 2, 3)]
        + [me.along_y(j) for j in (1, 2, 3)]
    )
    cores = send(part.at[1 - k], m1, ms.at[0], ms.at[1], me.sibling)
    here = w.at[2]

    def weight_place(i, half, position, piece):
        if half == 0:
            return w.at[i, position, lax.rem(z + 4 - piece, 4), 0]
        return w.at[i, lax.rem(y + 4 - piece, 4), position, 1]

    def weight_source(i, half, piece):
        return halves.at[i, half, lax.rem((z if half == 0 else y) + 4 - piece, 4)]

    rings = [
        RingGather(
            me.along_y if half == 0 else me.along_z,
            y if half == 0 else z,
            4,
            functools.partial(weight_place, i, half),
            functools.partial(weight_source, i, half),
            [sem.at[i - 1, half] for sem in (ba, bb, bc, bd)],
        )
        for i in (1, 2)
        for half in (0, 1)
    ]
    for ring in rings:
        for piece in range(4):
            ring.start(piece)
    loads[0].wait()

    def weight(i):
        return w[i].reshape(model, inner)


    def turn_dy(i, _):
        lo_i, t_i = chip(i)
        dy_t[:, columns(i)] = dy[lo_i, t_i].reshape(both, model).T
        return 0

    cores.wait()
    m2[...] = (part[k, 1 - t].astype(F32) + m1[1 - t].astype(F32)).astype(BF)
    across = send(m2, m3, ms.at[2], ms.at[3], me.in_ring(lo, 1 - t))
    lax.fori_loop(0, 4, turn_dy, 0)
    x = tok[...].astype(F32) + part[k, t].astype(F32) + m1[t].astype(F32)
    across.wait()
    x = x + m3[...].astype(F32)
    x1[...] = x
    factor = lax.rsqrt(jnp.mean(x * x, axis=-1, keepdims=True) + epsilon)
    h2[lo, t, k] = (x * factor * gain[...]).astype(BF)

    def hidden_copy(i):
        block = h2.at[lo, t, k]
        return describe(block, block, hs.at[i - 1], hr.at[i - 1], me.in_ring(*chip(i)))

    def hidden_share(i):
        lo_i, t_i = chip(i)
        block = h2.at[lo_i, t_i, k]
        return describe(block, block, fs.at[i], fr.at[i], me.sibling)

    def part_share(i):
        return describe(pb.at[i], r1.at[i], ps.at[i], pr.at[i], me.sibling)

    def part_copy(i):
        return describe(
            s1.at[i], r2.at[i - 1], xs.at[i - 1], xr.at[i - 1], me.in_ring(*chip(i))
        )

    def result_share(i):
        return describe(yb.at[i], ry.at[i], ys.at[i], yr.at[i], me.sibling)

    for i in (1, 2, 3):
        hidden_copy(i).start()
    hidden_share(0).start()
    for ring in rings:
        for piece in range(4):
            ring.forward(piece)
    for copy in loads[1:]:
        copy.wait()
    for ring in rings:
        ring.finish()

    def finish(i):
        part_share(i).wait_recv()
        s1[i] = (s1[i].astype(F32) + r1[i].astype(F32)).astype(BF)

        @pl.when(i > 0)
        def _():
            part_copy(i).start()

        whole[...] = by_columns(hid[i], weight(2)).reshape(2, rows, model)
        yb[i] = whole[1 - k].astype(BF)
        ysum[i] = whole[k].astype(BF)
        result_share(i).start()
        lo_i, t_i = chip(i)
        h2_t[:, columns(i)] = h2[lo_i, t_i].reshape(both, model).T

    def step(i, _):
        lo_i, t_i = chip(i)

        @pl.when(i > 0)
        def _():
            hidden_copy(i).wait_recv()
            hidden_share(i).start()
            finish(i - 1)

        hidden_share(i).wait_recv()
        h = h2[lo_i, t_i].reshape(both, model)
        d = dy[lo_i, t_i].reshape(both, model)
        gate = plain(h, weight(0))
        up = plain(h, weight(1))
        sigmoid_gate = jax.nn.sigmoid(gate)
        silu_gate = gate * sigmoid_gate
        hid[i] = (silu_gate * up).astype(BF)
        grad_inner = plain(d, weight(2))
        slope = sigmoid_gate * (1.0 + gate * (1.0 - sigmoid_gate))
        gate_back[i] = (grad_inner * up * slope).astype(BF)
        up_back[i] = (grad_inner * silu_gate).astype(BF)
        whole[...] = (
            by_columns(gate_back[i], weight(0)) + by_columns(up_back[i], weight(1))
        ).reshape(2, rows, model)
        pb[i] = whole[1 - k].astype(BF)
        s1[i] = whole[k].astype(BF)
        part_share(i).start()
        return 0

    lax.fori_loop(0, 4, step, 0)
    finish(3)

    def gradient(i, left_t, right):
        flat = right.shape[0] * right.shape[1]
        step_rows = model // 4

        def some(m, _):
            r = pl.ds(pl.multiple_of(m * step_rows, step_rows), step_rows)
            value = plain(left_t[r, :], right[...].reshape(flat, inner))
            w[i, m] = value.astype(BF).reshape(w.shape[2:])
            return 0

        lax.fori_loop(0, 4, some, 0)

    def gradient_out(i):
        copy = pltpu.make_async_copy(w.at[i], g_hbm.at[i], ls.at[i])
        copy.start()
        return copy

    gradient(2, dy_t, hid)
    downs_back = []
    for j in offsets:
        downs_back.append(
            send(
                here.at[:, lax.rem(z + j, 4), 0], pd.at[0, j - 1], cs.at[0, j - 1], cr.at[0, j - 1], me.along_z(j)
            )
        )
        downs_back.append(
            send(
                here.at[lax.rem(y + j, 4), :, 1], pd.at[1, j - 1], cs.at[1, j - 1], cr.at[1, j - 1], me.along_y(j)
            )
        )

    grad = s1[0].astype(F32)
    for i in (1, 2, 3):
        part_copy(i).wait_recv()
        grad = grad + r2[i - 1].astype(F32)
    x = x1[...]
    factor = lax.rsqrt(jnp.mean(x * x, axis=-1, keepdims=True) + epsilon)
    normed = x * factor
    gnf[...] = jnp.sum(grad * normed, axis=0, keepdims=True)
    back = dy[lo, t, k].astype(F32) + norm_back(grad * gain[...], normed, factor)
    dx1[...] = back
    dxl[k, t] = back.astype(BF)
    block = dxl.at[k, t]
    across = send(block, block, gs.at[0], gr.at[0], me.in_ring(lo, 1 - t))
    rest = [send(block, block, gs.at[1], gr.at[1], me.sibling)]
    gradient(0, h2_t, gate_back)
    outs = [gradient_out(0)]
    across.wait()
    block = dxl.at[k, 1 - t]
    rest.append(send(block, block, gs.at[2], gr.at[2], me.sibling))
    gradient(1, h2_t, up_back)
    outs.append(gradient_out(1))
    for i in range(4):
        result_share(i).wait()
        ysum[i] = (ysum[i].astype(F32) + ry[i].astype(F32)).astype(BF)
        hidden_share(i).wait_send()
        part_share(i).wait_send()
    for i in (1, 2, 3):
        hidden_copy(i).wait_send()
        part_copy(i).wait_send()
    for copy in downs_back:
        copy.wait()
    for half in (0, 1):
        mine = w[2, :, z, 0] if half == 0 else w[2, y, :, 1]
        total = mine.astype(F32)
        for j in range(3):
            total = total + pd[half, j].astype(F32)
        down_sum[half] = total.astype(BF)
    for copy in rest + outs:
        copy.wait()


def block(part, tok, gain, dy, gate, halves):
    rows, model = tok.shape
    hidden = gate.shape[-1]
    sums = halves.shape[1:]
    any_place = pl.BlockSpec(memory_space=pl.ANY)
    quarter = pltpu.VMEM((4, rows, model), BF)
    inner = pltpu.VMEM((4, 2 * rows, hidden), BF)
    turned = pltpu.VMEM((model, 8 * rows), BF)
    return pl.pallas_call(
        block_kernel,
        out_shape=[
            shape((rows, model), F32),
            shape((rows, model), F32),
            shape((2, 2, rows, model), BF),
            shape((1, model), F32),
            shape((4, rows, model), BF),
            shape(sums, BF),
            shape((2,) + gate.shape, BF),
        ],
        in_specs=[VM] * 3 + [any_place] * 3,
        out_specs=[VM] * 6 + [any_place],
        scratch_shapes=[
            pltpu.VMEM((3,) + gate.shape, BF),
            pltpu.VMEM(dy.shape, BF),
            turned,
            pltpu.VMEM(dy.shape, BF),
            turned,
            inner,
            inner,
            inner,
            pltpu.VMEM((2, rows, model), F32),
            pltpu.VMEM((2, rows, model), BF),
            pltpu.VMEM((rows, model), BF),
            pltpu.VMEM((rows, model), BF),
            quarter,
            quarter,
            quarter,
            pltpu.VMEM((3, rows, model), BF),
            quarter,
            quarter,
            pltpu.VMEM((2, 3) + sums[1:], BF),
            DMA((2, 2, 4, 2)),
            DMA((2, 2, 4, 2)),
            DMA((2, 2, 4)),
            DMA((2, 2, 4)),
            DMA((2, 3)),
            DMA((2, 3)),
            DMA((8,)),
            DMA((4,)),
            DMA((3,)),
            DMA((3,)),
            DMA((4,)),
            DMA((4,)),
            DMA((4,)),
            DMA((4,)),
            DMA((3,)),
            DMA((3,)),
            DMA((4,)),
            DMA((4,)),
            DMA((3,)),
            DMA((3,)),
        ],
        compiler_params=pltpu.CompilerParams(
            collective_id=3, has_side_effects=True, vmem_limit_bytes=62 << 20
        ),
    )(part, tok, gain, dy, gate, halves)


def rear_kernel(
    heads,
    g_hbm, down_sum, dxl, attn, q, kv, exact, lse, start_ref, ob, h1, cosines, sines, ysum, x1, dx1, tok, gain, gnf,
    a_all, ext_all, ffn_all, down_all, out, grad,
    do, dots, acc, keep, give, arrived, sums, landed, back, part, m1, m2, m3, left_t, ga,
    own, p1, p2, q1, sm, q2, fin, fin_d, wide, narrow, e0, e1, es, e2, y2,
    ls, d1, d2, d3, d4, ms, fs1, fr1, fs2, fr2, as1, ar1, as2, ar2, as3, ar3, xs, xr, ss, sr, ts, tr, us, ur, ys, yr,
    gs, gr,
):
    me = Place()
    y, z, lo, k, t = me.y, me.z, me.lo, me.k, me.t
    c = lo * 2 + k
    index = z * 2 + lo
    rows, width = q.shape
    size = width // heads
    slice_rows, model = tok.shape
    rowed = width + size
    offsets = (2, 1, 3)

    def in_x(dt, dc):
        return {"ctx": lax.rem(c + dc, 4), "tp": lax.rem(t + dt, 2)}

    def owner(b):
        return {"fsdp": y * 4 + b // 2, "ctx": lax.rem(b, 2) * 2 + k}

    ring = [(dt, dc) for dt in (0, 1) for dc in range(4) if dt or dc]

    def first_hop(w, half, j):
        if half == 0:
            source, device = g_hbm.at[w, :, lax.rem(z + j, 4), 0], me.along_z(j)
        else:
            source, device = g_hbm.at[w, lax.rem(y + j, 4), :, 1], me.along_y(j)
        return describe(
            source, p1.at[w, half, j - 1], fs1.at[w, half, j - 1], fr1.at[w, half, j - 1], device
        )

    def second_hop(w, half, j):
        if half == 0:
            source, device = own.at[w, 0, lax.rem(y + j, 4)], me.along_y(j)
        else:
            source, device = own.at[w, 1, lax.rem(z + j, 4)], me.along_z(j)
        return describe(
            source, p2.at[w, half, j - 1], fs2.at[w, half, j - 1], fr2.at[w, half, j - 1], device
        )

    def own_load(w, half):
        source = g_hbm.at[w, :, z, 0] if half == 0 else g_hbm.at[w, y, :, 1]
        return pltpu.make_async_copy(source, own.at[w, half], ls.at[w, half])

    def start_hop(half, *span):
        def some(w, _):
            for j in offsets:
                first_hop(w, half, j).start()
            own_load(w, half).start()
            return 0

        lax.fori_loop(*span, some, 0)

    greet(
        [me.along_z(j) for j in (1, 2, 3)]
        + [me.along_y(j) for j in (1, 2, 3)]
        + [in_x(dt, dc) for dt, dc in ring]
        + [{"fsdp": y * 4 + lax.rem(z + j, 4), "ctx": (1 - lo) * 2 + k} for j in (1, 2, 3)]
    )
    own[2] = down_sum[...]
    for half in (0, 1):
        for j in offsets:
            second_hop(2, half, j).start()
    start_hop(1, 0, 2)
    start_hop(0, 0, 1)
    near = [(1 - lo, t), (1 - lo, 1 - t), (lo, 1 - t)]
    results = [
        send(ysum.at[i + 1], y2.at[i], ys.at[i], yr.at[i], me.in_ring(*near[i])) for i in range(3)
    ]

    do[...] = plain(dxl[...], attn[:, rowed:]).astype(BF)
    for h in range(heads):
        product = exact[h] * do[:, h * size : (h + 1) * size].astype(F32).T
        dots[h : h + 1] = jnp.sum(product, axis=0, keepdims=True)
    acc[...] = jnp.zeros_like(acc)
    start = start_ref[...]
    first = index * rows

    def core_share(b):
        return describe(give.at[b], arrived.at[b], d1.at[b], d2.at[b], me.sibling)

    def home(b):
        return describe(sums.at[b], landed.at[index], d3.at[b], d4.at[index], owner(b))

    def step(b, _):
        keys = kv[0, b]
        values = kv[1, b]
        seen = visible_pairs(b, first, start, rows)
        dk = jnp.zeros((KEYS, size), F32)
        dv = jnp.zeros((KEYS, size), F32)
        for h in range(heads):
            q_h = q[:, h * size : (h + 1) * size]
            do_h = do[:, h * size : (h + 1) * size]
            s = jnp.where(seen, by_columns(keys, q_h), masked_score)
            p = jnp.exp(s - lse[h : h + 1])
            dv = dv + plain(p.astype(BF), do_h)
            dp = by_columns(values, do_h)
            ds = (p * (dp - dots[h : h + 1])).astype(BF)
            dk = dk + plain(ds, q_h)
            acc[h] = acc[h] + over_rows(keys, ds)
        keep[b] = jnp.where(k == 0, dk, dv)
        give[b] = jnp.where(k == 0, dv, dk)
        core_share(b).start()

        @pl.when(b > 0)
        def _():
            core_share(b - 1).wait_recv()
            sums[b - 1] = (keep[b - 1] + arrived[b - 1]).astype(BF)
            home(b - 1).start()

        return 0

    lax.fori_loop(0, index + 1, step, 0)
    start_hop(0, 1, 2)

    scale = 1.0 / math.sqrt(size)
    for h in range(heads):
        dq = turned(acc[h].T * scale, cosines[...], -sines[...])
        e0[2:3, h * size : (h + 1) * size] = jnp.sum(dq, axis=0, keepdims=True)
        back[:, h * size : (h + 1) * size] = dq.astype(BF)
    left_t[...] = dxl[...].T
    blocks = ga.shape[:4]

    def spread(value):
        return value.astype(BF).reshape(blocks + (value.shape[1],))

    ga[:, :, :, :, rowed:] = spread(plain(left_t[...], ob[...]))
    left_t[...] = h1[...].T
    ga[:, :, :, :, :width] = spread(plain(left_t[...], back[:, :width]))

    core_share(index).wait_recv()
    dkv = keep[index] + arrived[index]
    keep[index] = dkv
    for b in range(1, 8):

        @pl.when(b > index)
        def _():
            describe(sums.at[0], landed.at[b], d3.at[0], d4.at[b], owner(0)).wait_recv()
            keep[index] = keep[index] + landed[b].astype(F32)

    is_key = k == 0
    dkv = turned(
        keep[index], jnp.where(is_key, cosines[...], 1.0), jnp.where(is_key, -sines[...], 0.0)
    )
    e0[2:3, width:rowed] = jnp.sum(dkv, axis=0, keepdims=True)
    back[:, width:] = dkv.astype(BF)
    part[...] = (
        by_columns(back[...], attn[:, :rowed]).astype(BF).reshape(2, 2, slice_rows, model)
    )
    cores = send(part.at[1 - k], m1, ms.at[0], ms.at[1], me.sibling)
    ga[:, :, :, :, width:rowed] = spread(plain(left_t[...], back[:, width:]))

    large = []
    for j in offsets:
        large.append(
            send(
                ga.at[:, lax.rem(z + j, 4), 0], q1.at[0, j - 1], as1.at[0, j - 1], ar1.at[0, j - 1], me.along_z(j)
            )
        )
        large.append(
            send(
                ga.at[lax.rem(y + j, 4), :, 1], q1.at[1, j - 1], as1.at[1, j - 1], ar1.at[1, j - 1], me.along_y(j)
            )
        )

    cores.wait()
    m2[...] = (part[k, 1 - t].astype(F32) + m1[1 - t].astype(F32)).astype(BF)
    across = send(m2, m3, ms.at[2], ms.at[3], me.in_ring(lo, 1 - t))
    x = tok[...].astype(F32)
    factor = lax.rsqrt(jnp.mean(x * x, axis=-1, keepdims=True) + epsilon)
    normed = x * factor
    dh1 = part[k, t].astype(F32) + m1[t].astype(F32)
    across.wait()
    dh1 = dh1 + m3[...].astype(F32)
    e0[0:1] = jnp.sum(dh1 * normed, axis=0, keepdims=True)
    e0[1:2] = gnf[...]
    e0[2:3, rowed:] = jnp.zeros((1, model - rowed), F32)
    e0[3:] = jnp.zeros((5, model), F32)
    small = [
        send(e0, e1.at[j - 1], ss.at[0, j - 1], sr.at[0, j - 1], me.along_z(j)) for j in offsets
    ]
    grad[t] = (dx1[...] + norm_back(dh1 * gain[...], normed, factor)).astype(BF)
    mine = grad.at[t]
    rest = [send(mine, mine, gs.at[0], gr.at[0], me.in_ring(lo, 1 - t))]

    quarter = sm.shape[2] // 2

    def summed(w, half):
        for j in offsets:
            second_hop(w, half, j).wait()
        here = own[w, 0, y] if half == 0 else own[w, 1, z]
        total = here.astype(F32)
        for j in range(3):
            total = total + p2[w, half, j].astype(F32)
        return total

    for half in (0, 1):
        total = summed(2, half)
        fin_d[2 * half] = total[:quarter]
        fin_d[2 * half + 1] = total[quarter:]
    down_all[c] = fin_d[c]
    rest += [
        send(fin_d.at[lax.rem(c + j, 4)], down_all.at[c], us.at[j - 1], ur.at[j - 1], in_x(0, j))
        for j in (2, 1, 3)
    ]

    result = x1[...] + ysum[0].astype(F32)
    for i in range(3):
        results[i].wait()
        result = result + y2[i].astype(F32)
    out[t] = result.astype(BF)
    mine = out.at[t]
    rest.append(send(mine, mine, gs.at[1], gr.at[1], me.in_ring(lo, 1 - t)))

    for copy in small:
        copy.wait()
    es[...] = (e0[...] + e1[0]) + (e1[1] + e1[2])
    small = [
        send(es, e2.at[j - 1], ss.at[1, j - 1], sr.at[1, j - 1], me.along_y(j)) for j in offsets
    ]

    def first_sum(w, _):
        for half in (0, 1):
            own_load(w, half).wait()
            for j in offsets:
                first_hop(w, half, j).wait()
            total = own[w, half].astype(F32)
            for j in range(3):
                total = total + p1[w, half, j].astype(F32)
            own[w, half] = total.astype(BF)
            for j in offsets:
                second_hop(w, half, j).start()
        return 0

    lax.fori_loop(0, 2, first_sum, 0)

    for copy in small:
        copy.wait()
    ext_all[t, c] = (es[...] + e2[0]) + (e2[1] + e2[2])
    mine = ext_all.at[t, c]
    rest += [
        send(mine, mine, xs.at[i], xr.at[i], in_x(dt, dc)) for i, (dt, dc) in enumerate(ring)
    ]
    for copy in large:
        copy.wait()
    for half in (0, 1):
        here = ga[:, z, 0] if half == 0 else ga[y, :, 1]
        total = here.astype(F32)
        for j in range(3):
            total = total + q1[half, j].astype(F32)
        sm[half] = total.astype(BF)
    last = []
    for j in offsets:
        last.append(
            send(
                sm.at[0, lax.rem(y + j, 4)], q2.at[0, j - 1], as2.at[0, j - 1], ar2.at[0, j - 1], me.along_y(j)
            )
        )
        last.append(
            send(
                sm.at[1, lax.rem(z + j, 4)], q2.at[1, j - 1], as2.at[1, j - 1], ar2.at[1, j - 1], me.along_z(j)
            )
        )

    def second_sum(w, _):
        for half in (0, 1):
            total = summed(w, half)
            place = pl.ds(pl.multiple_of(w * quarter, 8), quarter)
            wide[2 * half, place] = total[:quarter]
            wide[2 * half + 1, place] = total[quarter:]
        return 0

    lax.fori_loop(0, 2, second_sum, 0)
    narrow[...] = wide[...].astype(BF)
    ffn_all[c] = narrow[c]
    rest += [
        send(narrow.at[lax.rem(c + j, 4)], ffn_all.at[c], ts.at[j - 1], tr.at[j - 1], in_x(0, j))
        for j in (2, 1, 3)
    ]
    for copy in last:
        copy.wait()
    for half in (0, 1):
        here = sm[0, y] if half == 0 else sm[1, z]
        total = here.astype(F32)
        for j in range(3):
            total = total + q2[half, j].astype(F32)
        fin[2 * half] = total[:quarter]
        fin[2 * half + 1] = total[quarter:]
    a_all[c] = fin[c]
    rest += [
        send(fin.at[lax.rem(c + j, 4)], a_all.at[c], as3.at[j - 1], ar3.at[j - 1], in_x(0, j))
        for j in (2, 1, 3)
    ]

    def sent(b, _):
        core_share(b).wait_send()

        @pl.when(b < index)
        def _():
            home(b).wait_send()

        return 0

    lax.fori_loop(0, index + 1, sent, 0)
    for copy in rest:
        copy.wait()


def rear(heads, g, down_sum, dxl, attn, q, kv, exact, lse, start, ob, h1, cosines, sines, ysum, x1, dx1, tok, gain, gnf):
    rows, width = q.shape
    size = width // heads
    slice_rows, model = tok.shape
    hidden = g.shape[-1]
    total = attn.shape[1]
    half_rows = model // 32
    quarter = half_rows // 2
    packed = 2 * quarter
    shared = pltpu.VMEM(kv.shape[1:], F32)
    shared_low = pltpu.VMEM(kv.shape[1:], BF)
    slab = pltpu.VMEM((slice_rows, model), BF)
    args = (down_sum, dxl, attn, q, kv, exact, lse, start, ob, h1, cosines, sines, ysum, x1, dx1, tok, gain, gnf)
    outs = [
        shape((4, quarter, total), F32),
        shape((2, 4, 8, model), F32),
        shape((4, packed, hidden), BF),
        shape((4, quarter, hidden), F32),
        shape((2, slice_rows, model), BF),
        shape((2, slice_rows, model), BF),
    ]
    return pl.pallas_call(
        functools.partial(rear_kernel, heads),
        out_shape=outs,
        in_specs=[pl.BlockSpec(memory_space=pl.ANY)] + [VM] * len(args),
        out_specs=[VM] * len(outs),
        scratch_shapes=[
            pltpu.VMEM((rows, width), BF),
            pltpu.VMEM((8, rows), F32),
            pltpu.VMEM((heads, size, rows), F32),
            shared,
            shared,
            shared,
            shared_low,
            shared_low,
            pltpu.VMEM((rows, width + size), BF),
            pltpu.VMEM((2, 2, slice_rows, model), BF),
            pltpu.VMEM((2, slice_rows, model), BF),
            slab,
            slab,
            pltpu.VMEM((model, rows), BF),
            pltpu.VMEM((4, 4, 2, half_rows, total), BF),
            pltpu.VMEM((3, 2, 4, half_rows, hidden), BF),
            pltpu.VMEM((2, 2, 3, 4, half_rows, hidden), BF),
            pltpu.VMEM((3, 2, 3, half_rows, hidden), BF),
            pltpu.VMEM((2, 3, 4, half_rows, total), BF),
            pltpu.VMEM((2, 4, half_rows, total), BF),
            pltpu.VMEM((2, 3, half_rows, total), BF),
            pltpu.VMEM((4, quarter, total), F32),
            pltpu.VMEM((4, quarter, hidden), F32),
            pltpu.VMEM((4, packed, hidden), F32),
            pltpu.VMEM((4, packed, hidden), BF),
            pltpu.VMEM((8, model), F32),
            pltpu.VMEM((3, 8, model), F32),
            pltpu.VMEM((8, model), F32),
            pltpu.VMEM((3, 8, model), F32),
            pltpu.VMEM((3, slice_rows, model), BF),
            DMA((2, 2)),
            DMA((8,)),
            DMA((8,)),
            DMA((8,)),
            DMA((8,)),
            DMA((4,)),
            DMA((2, 2, 3)),
            DMA((2, 2, 3)),
            DMA((3, 2, 3)),
            DMA((3, 2, 3)),
            DMA((2, 3)),
            DMA((2, 3)),
            DMA((2, 3)),
            DMA((2, 3)),
            DMA((3,)),
            DMA((3,)),
            DMA((7,)),
            DMA((7,)),
            DMA((2, 3)),
            DMA((2, 3)),
            DMA((3,)),
            DMA((3,)),
            DMA((3,)),
            DMA((3,)),
            DMA((3,)),
            DMA((3,)),
            DMA((2,)),
            DMA((2,)),
        ],
        compiler_params=pltpu.CompilerParams(
            collective_id=7, has_side_effects=True, vmem_limit_bytes=62 << 20
        ),
    )(g, *args)


def shards(
    tokens,
    segments,
    w_query,
    key_matrix,
    value_matrix,
    b_query,
    key_bias_vector,
    value_bias_vector,
    w_out,
    norm_attn,
    norm_ffn,
    w_gate,
    w_up,
    w_down,
    cotangent,
):
    f = lax.axis_index("fsdp")
    c = lax.axis_index("ctx")
    t = lax.axis_index("tp")
    k = c % 2
    is_key = k == 0
    size = key_matrix.shape[1]
    query_width = w_query.shape[1] // 2
    heads = query_width // size
    own_width = query_width + size
    model = tokens.shape[1]
    count = tokens.shape[0]
    slice_rows = count // 2
    shard_rows = w_query.shape[0]
    hidden = w_gate.shape[1] // 4
    padded = -(-hidden // 128) * 128

    def hidden_slice(w, axis):
        return lax.dynamic_slice_in_dim(w, c * hidden, hidden, axis)

    def widened(w):
        return jnp.pad(w, ((0, 0), (0, padded - hidden)))

    own_ffn = jnp.stack(
        [
            widened(hidden_slice(w_gate, 1)),
            widened(hidden_slice(w_up, 1)),
            widened(hidden_slice(w_down, 0).T),
        ]
    )

    own_attn = jnp.concatenate(
        [
            lax.dynamic_slice_in_dim(w_query, k * query_width, query_width, 1),
            jnp.where(is_key, key_matrix, value_matrix),
            lax.dynamic_slice_in_dim(w_out, k * query_width, query_width, 0).T,
        ],
        axis=1,
    )
    own_tokens = lax.dynamic_slice_in_dim(tokens, t * slice_rows, slice_rows, 0)
    rows = 2 * count
    half_size = size // 2
    frequency = jnp.exp(jnp.arange(half_size, dtype=F32) * (-2.0 * math.log(rope_base) / size))
    frequency = jnp.concatenate([frequency, frequency])[None]
    gain_attn = norm_attn.astype(F32)[None]
    gain_ffn = norm_ffn.astype(F32)[None]
    bias = jnp.concatenate(
        [
            lax.dynamic_slice_in_dim(b_query, k * query_width, query_width, 0),
            jnp.where(is_key, key_bias_vector, value_bias_vector),
        ]
    ).astype(F32)[None]
    (
        attn_all,
        gate_all,
        halves,
        dy_all,
        h1,
        q,
        kv,
        exact,
        ob,
        lse,
        starts,
        cosines,
        sines,
        part,
    ) = front(heads, own_attn, own_ffn, tokens, cotangent, segments, gain_attn, bias, frequency)
    x1, dx1, dxl, grad_norm_two, ysum, down_sum, ffn_grads = block(
        part, own_tokens, gain_ffn, dy_all, gate_all, halves
    )
    a_all, ext_all, ffn_all, down_all, output, grad_tokens = rear(
        heads,
        ffn_grads,
        down_sum,
        dxl.reshape(rows, model),
        attn_all.reshape(model, own_width + query_width),
        q,
        kv,
        exact,
        lse,
        starts,
        ob,
        h1,
        cosines,
        sines,
        ysum,
        x1,
        dx1,
        own_tokens,
        gain_attn,
        grad_norm_two,
    )
    owner_rows = shard_rows // 4
    a_all = a_all[:2] + a_all[2:]

    def side_by_side(pieces):
        return jnp.concatenate([pieces[i, :, :hidden].astype(F32) for i in range(4)], axis=1)

    owner = f * 4 + c
    norms = lax.dynamic_slice_in_dim(
        jnp.sum(ext_all[:, :, :2].reshape(8, 2, model), axis=0), owner * owner_rows, owner_rows, 1
    )
    biases = lax.dynamic_index_in_dim(ext_all[:, :, 2, :own_width], t, 0, keepdims=False)
    biases = (biases[:2] + biases[2:]).reshape(2, heads + 1, size)
    biases = lax.dynamic_slice_in_dim(biases, owner * 2, 2, 2)
    return (
        output.reshape(count, model),
        grad_tokens.reshape(count, model).astype(F32),
        jnp.concatenate([a_all[0, :, :query_width], a_all[1, :, :query_width]], axis=1),
        a_all[0, :, query_width:own_width],
        a_all[1, :, query_width:own_width],
        biases[:, :heads].reshape(2 * heads, 2),
        biases[0, heads:],
        biases[1, heads:],
        jnp.concatenate([a_all[0, :, own_width:], a_all[1, :, own_width:]], axis=1).T,
        norms[0],
        norms[1],
        side_by_side(ffn_all[:, :owner_rows]),
        side_by_side(ffn_all[:, owner_rows:]),
        side_by_side(down_all).T,
    )


def solution(mesh):
    both = ("fsdp", "ctx")
    in_specs = (
        P(both, None),
        P(),
        P("fsdp", "tp"),
        P("fsdp", "tp"),
        P("fsdp", "tp"),
        P("tp"),
        P("tp"),
        P("tp"),
        P("tp", "fsdp"),
        P(),
        P(),
        P("fsdp", "tp"),
        P("fsdp", "tp"),
        P("tp", "fsdp"),
        P(both, None),
    )
    out_specs = (
        P(both, None),
        P(both, None),
        P(both, "tp"),
        P(both, "tp"),
        P(both, "tp"),
        P("tp", both),
        P("tp", both),
        P("tp", both),
        P("tp", both),
        P(both),
        P(both),
        P(both, "tp"),
        P(both, "tp"),
        P("tp", both),
    )
    return jax.shard_map(shards, mesh=mesh, in_specs=in_specs, out_specs=out_specs, check_vma=False)
```

```python
import functools
import math

import jax
import jax.numpy as jnp
from jax import lax
from jax.experimental import pallas as pl
from jax.experimental.pallas import tpu as pltpu
from jax.sharding import PartitionSpec as P

MESH = pl.DeviceIdType.MESH
VM = pl.BlockSpec(memory_space=pltpu.VMEM)
DMA = pltpu.SemaphoreType.DMA
BF = jnp.bfloat16
F32 = jnp.float32

epsilon = 1e-06
rope_base = 1000000.0
masked_score = -1e30
KEYS = 512


class Place:
    def __init__(self):
        f = lax.axis_index("fsdp")
        c = lax.axis_index("ctx")
        self.y, self.z = f // 4, f % 4
        self.lo, self.k = c // 2, c % 2
        self.t = lax.axis_index("tp")

    def along_y(self, j):
        return {"fsdp": lax.rem(self.y + j, 4) * 4 + self.z}

    def along_z(self, j):
        return {"fsdp": self.y * 4 + lax.rem(self.z + j, 4)}

    @property
    def sibling(self):
        return {"ctx": self.lo * 2 + 1 - self.k}

    def in_ring(self, lo, t):
        return {"ctx": lo * 2 + self.k, "tp": t}

    @property
    def others(self):
        return [(self.lo, 1 - self.t), (1 - self.lo, self.t), (1 - self.lo, 1 - self.t)]


def greet(devices):
    barrier = pltpu.get_barrier_semaphore()
    for device in devices:
        pl.semaphore_signal(barrier, inc=1, device_id=device, device_id_type=MESH)
    pl.semaphore_wait(barrier, len(devices))


def describe(source, target, send_sem, recv_sem, device):
    return pltpu.make_async_remote_copy(
        src_ref=source,
        dst_ref=target,
        send_sem=send_sem,
        recv_sem=recv_sem,
        device_id=device,
        device_id_type=MESH,
    )


def send(source, target, send_sem, recv_sem, device):
    copy = describe(source, target, send_sem, recv_sem, device)
    copy.start()
    return copy


def comm_call(body, outs, scratch, collective_id, mib, *args):
    return pl.pallas_call(
        body,
        out_shape=outs,
        in_specs=[VM] * len(args),
        out_specs=[VM] * len(outs),
        scratch_shapes=scratch,
        compiler_params=pltpu.CompilerParams(
            collective_id=collective_id, has_side_effects=True, vmem_limit_bytes=mib << 20
        ),
    )(*args)


def shape(dims, kind):
    return jax.ShapeDtypeStruct(dims, kind)


def over_rows(a, b):
    return lax.dot_general(a, b, (((0,), (0,)), ((), ())), preferred_element_type=F32)


def by_columns(a, b):
    return lax.dot_general(a, b, (((1,), (1,)), ((), ())), preferred_element_type=F32)


def plain(a, b):
    return lax.dot_general(a, b, (((1,), (0,)), ((), ())), preferred_element_type=F32)


def visible_pairs(block, first, start, rows):
    key = block * KEYS + lax.broadcasted_iota(jnp.int32, (KEYS, rows), 0)
    row = first + lax.broadcasted_iota(jnp.int32, (1, rows), 1)
    return (key >= start) & (key <= row)


class RingGather:
    def __init__(self, along, position, pieces, target, source, sems):
        self.along, self.position, self.pieces = along, position, pieces
        self.target, self.source, self.sems = target, source, sems

    def hop(self, i, way):
        s, r = self.sems[:2]
        return describe(
            self.source(i),
            self.target(self.position, i),
            s.at[i, way],
            r.at[i, way],
            self.along(1 if way == 0 else 3),
        )

    def onward(self, i):
        s, r = self.sems[2:]
        way = i // 2
        block = self.target(lax.rem(self.position + (3 if way == 0 else 1), 4), i)
        return describe(block, block, s.at[i], r.at[i], self.along(1 if way == 0 else 3))

    def start(self, i):
        self.hop(i, 0).start()
        self.hop(i, 1).start()

    def forward(self, i):
        self.hop(i, i // 2).wait_recv()
        self.onward(i).start()

    def finish(self):
        for i in range(4):
            self.hop(i, 1 - i // 2).wait_recv()
            self.onward(i).wait()
            self.hop(i, 0).wait_send()
            self.hop(i, 1).wait_send()


class RingSum:
    def __init__(self, along, position, source, passing, got, sems):
        self.along, self.position, self.source = along, position, source
        self.passing, self.got, self.sems = passing, got, sems

    def at(self, offset):
        return lax.rem(self.position + offset, 4)

    def first(self, way):
        s, r = self.sems[:2]
        return describe(
            self.source(self.at(2), 2 * way, 2),
            self.passing.at[way],
            s.at[way],
            r.at[way],
            self.along(1 if way == 0 else 3),
        )

    def second(self, way):
        s, r = self.sems[2:]
        offset = 1 if way == 0 else 3
        return describe(
            self.source(self.at(offset), 0, 4), self.got.at[way], s.at[way], r.at[way], self.along(offset)
        )

    def start(self):
        for way in (0, 1):
            self.first(way).start()

    def middle(self):
        for way in (0, 1):
            self.first(way).wait()
            near = self.source(self.at(1 if way == 0 else 3), 2 * way, 2)
            near[...] = (near[...].astype(F32) + self.passing[way].astype(F32)).astype(BF)
            self.second(way).start()

    def finish(self):
        total = self.source(self.position, 0, 4)[...].astype(F32)
        for way in (0, 1):
            self.second(way).wait()
            total = total + self.got[way].astype(F32)
        return total


def turned(values, cosines, sines):
    return values * cosines - pltpu.roll(values, values.shape[-1] // 2, 1) * sines


def front_kernel(
    heads,
    w, ffn, tok, dy, segments, gain, bias, frequency,
    w_all, halves, dy_all, h1, q, kv, exact, ob, lse, starts, cosines, sines, part,
    tok2, top, total, acc,
    s1, r1, wa, wb, wc, wd, s3, r3, ts, tr, ds, dr, fs, fr, ks, kr, cs, cr,
):
    me = Place()
    y, z, lo, k, t = me.y, me.z, me.lo, me.k, me.t
    index = z * 2 + lo
    count, model = tok.shape
    rows = 2 * count
    width, size = q.shape[1], exact.shape[1]
    rowed = width + size
    shard = w.shape[0] // 2
    parts = (pl.ds(0, shard), pl.ds(shard, shard))
    near = [me.in_ring(1 - lo, t), me.in_ring(1 - lo, 1 - t)]
    offsets = (1, 3, 2)
    greet(
        [me.along_z(j) for j in (1, 2, 3)]
        + [me.along_y(j) for j in (1, 2, 3)]
        + [me.sibling]
        + near
        + [{"fsdp": y * 4 + lax.rem(z + j, 4), "ctx": (1 - lo) * 2 + k} for j in (1, 2, 3)]
    )

    def attn_place(half, position, i):
        if half == 0:
            return w_all.at[position, lax.rem(z + 4 - i, 4), parts[0]]
        return w_all.at[lax.rem(y + 4 - i, 4), position, parts[1]]

    def attn_source(half, i):
        if i == 0:
            return w.at[parts[half]]
        return attn_place(half, y if half == 0 else z, i)

    def first_hop(half, j):
        along = me.along_z if half == 0 else me.along_y
        return describe(
            w.at[parts[half]],
            w_all.at[y, z, parts[half]],
            s1.at[half, j - 1],
            r1.at[half, j - 1],
            along(j),
        )

    rings = [
        RingGather(
            me.along_y if half == 0 else me.along_z,
            y if half == 0 else z,
            4,
            functools.partial(attn_place, half),
            functools.partial(attn_source, half),
            [sem.at[half] for sem in (wa, wb, wc, wd)],
        )
        for half in (0, 1)
    ]
    for j in offsets:
        for half in (0, 1):
            first_hop(half, j).start()
    for ring in rings:
        ring.start(0)
    tokens_share = send(tok, tok2, ts, tr, me.sibling)
    slab = count // 2
    near_copies = [
        send(dy.at[pl.ds(t * slab, slab)], dy_all.at[lo, t, k], ds.at[i], dr.at[i], near[i])
        for i in (0, 1)
    ]
    rest = [
        send(dy.at[pl.ds(h * slab, slab)], dy_all.at[lo, h, k], fs.at[2 + h], fr.at[2 + h], me.sibling)
        for h in (0, 1)
    ]
    w_all[y, z] = w[...]
    for h in (0, 1):
        dy_all[lo, h, k] = dy[pl.ds(h * slab, slab)]

    first = pl.multiple_of(index * rows, rows)
    everyone = segments[pl.ds(y, 1), :]
    mine = segments[pl.ds(y, 1), pl.ds(first, rows)]
    start = jnp.zeros((1, rows), jnp.int32)
    for number in (1, 2, 3):
        begin = jnp.sum(jnp.where(everyone < number, 1.0, 0.0), axis=1, keepdims=True)
        start = jnp.where(mine == number, begin.astype(jnp.int32), start)
    starts[...] = start
    row = first + lax.broadcasted_iota(jnp.int32, (1, rows), 1)
    pos = jnp.broadcast_to((row - start).astype(F32), (8, rows)).T[:, :1]
    angles = pos * frequency[...]
    lane = lax.broadcasted_iota(jnp.int32, (1, size), 1)
    cosines[...] = jnp.cos(angles)
    sines[...] = jnp.sin(angles) * jnp.where(lane < size // 2, 1.0, -1.0)

    for j in offsets:
        for half in (0, 1):
            first_hop(half, j).wait()
            rings[half].start(j)

    def normed(x):
        x = x.astype(F32)
        factor = lax.rsqrt(jnp.mean(x * x, axis=-1, keepdims=True) + epsilon)
        return (x * factor * gain[...]).astype(BF)

    h1[pl.ds(pl.multiple_of(k * count, count), count)] = normed(tok[...])
    tokens_share.wait()
    h1[pl.ds(pl.multiple_of((1 - k) * count, count), count)] = normed(tok2[...])

    for i in (0, 1, 3, 2):
        for ring in rings:
            ring.forward(i)

    def ffn_hop(i, half, j):
        along, here = (me.along_z, z) if half == 0 else (me.along_y, y)
        return describe(
            ffn.at[i, parts[half]],
            halves.at[i, half, here],
            s3.at[i, half, j - 1],
            r3.at[i, half, j - 1],
            along(j),
        )

    def ffn_hops(i):
        for half in (0, 1):
            for j in offsets:
                ffn_hop(i, half, j).start()
            halves[i, half, z if half == 0 else y] = ffn[i, parts[half]]

    ffn_hops(0)
    for ring in rings:
        ring.finish()

    inward = w_all[:, :, :, :rowed].reshape(model, rowed)
    linear = plain(h1[...], inward) + bias[...]
    scale = 1.0 / math.sqrt(size)
    is_key = k == 0
    own = turned(
        linear[:, width:],
        jnp.where(is_key, cosines[...], 1.0),
        jnp.where(is_key, sines[...], 0.0),
    )
    kv[k, index] = own.astype(BF)
    own_keys = kv.at[k, index]

    def keys_copy(i, device):
        return describe(own_keys, own_keys, ks.at[i], kr.at[index], device)

    targets = [(dz, to) for dz in (1, 2, 3) for to in (0, 1)]

    def target(dz, to):
        return {"fsdp": y * 4 + lax.rem(z + dz, 4), "ctx": to * 2 + k}

    for i, (dz, to) in enumerate(targets):

        @pl.when(z + dz < 4)
        def _():
            keys_copy(i, target(dz, to)).start()

    @pl.when(lo == 0)
    def _():
        keys_copy(6, {"ctx": 2 + k}).start()

    def keys_share(b):
        there = kv.at[k, b]
        return describe(there, there, cs.at[b], cr.at[b], me.sibling)

    keys_share(index).start()
    for h in range(heads):
        here = slice(h * size, (h + 1) * size)
        q[:, here] = (turned(linear[:, here], cosines[...], sines[...]) * scale).astype(BF)

    ffn_hops(1)
    ffn_hops(2)
    for i, half in ((0, t), (1, 1 - t)):
        near_copies[i].wait()
        there = dy_all.at[1 - lo, half, k]
        rest.append(send(there, there, fs.at[i], fr.at[i], me.sibling))

    top[...] = jnp.full_like(top, masked_score)
    total[...] = jnp.zeros_like(total)
    acc[...] = jnp.zeros_like(acc)

    def step(i, _):
        b = index - i

        @pl.when(b > 0)
        def _():
            there = kv.at[k, b - 1]
            describe(there, there, ks.at[0], kr.at[b - 1], me.sibling).wait_recv()
            keys_share(b - 1).start()

        keys_share(b).wait_recv()
        keys = kv[0, b]
        values = kv[1, b]
        seen = visible_pairs(b, first, start, rows)
        for h in range(heads):
            s = by_columns(keys, q[:, h * size : (h + 1) * size])
            s = jnp.where(seen, s, masked_score)
            before = top[h : h + 1]
            now = jnp.maximum(before, jnp.max(s, axis=0, keepdims=True))
            p = jnp.exp(s - now)
            shrink = jnp.exp(before - now)
            top[h : h + 1] = now
            total[h : h + 1] = total[h : h + 1] * shrink + jnp.sum(p, axis=0, keepdims=True)
            acc[h] = acc[h] * shrink + over_rows(values, p.astype(BF))
        return 0

    lax.fori_loop(0, index + 1, step, 0)
    lse[...] = jnp.zeros_like(lse)
    for h in range(heads):
        sums = total[h : h + 1]
        lse[h : h + 1] = top[h : h + 1] + jnp.log(sums)
        out = acc[h] / sums
        exact[h] = out
        ob[:, h * size : (h + 1) * size] = out.T.astype(BF)
    outward = w_all[:, :, :, rowed:].reshape(model, width)
    part[...] = by_columns(ob[...], outward).astype(BF).reshape(part.shape)

    for i, (dz, to) in enumerate(targets):

        @pl.when(z + dz < 4)
        def _():
            keys_copy(i, target(dz, to)).wait_send()

    @pl.when(lo == 0)
    def _():
        keys_copy(6, {"ctx": 2 + k}).wait_send()

    def shared(b, _):
        keys_share(b).wait_send()
        return 0

    lax.fori_loop(0, index + 1, shared, 0)
    for i in range(3):
        for half in (0, 1):
            for j in offsets:
                ffn_hop(i, half, j).wait()
    for copy in rest:
        copy.wait()


def front(heads, w, ffn, tok, dy, segments, gain, bias, frequency):
    shard, total = w.shape
    hidden = ffn.shape[2]
    count, model = tok.shape
    rows = 2 * count
    width = bias.shape[1] - frequency.shape[1]
    size = frequency.shape[1]
    args = (w, ffn, tok, dy, segments, gain, bias, frequency)
    outs = [
        shape((4, 4, shard, total), BF),
        shape((3, 2, 4, shard // 2, hidden), BF),
        shape((2, 2, 2, count // 2, model), BF),
        shape((rows, model), BF),
        shape((rows, width), BF),
        shape((2, 8, rows, size), BF),
        shape((heads, size, rows), F32),
        shape((rows, width), BF),
        shape((8, rows), F32),
        shape((1, rows), jnp.int32),
        shape((rows, size), F32),
        shape((rows, size), F32),
        shape((2, 2, count // 2, model), BF),
    ]
    return pl.pallas_call(
        functools.partial(front_kernel, heads),
        out_shape=outs,
        in_specs=[VM] * len(args),
        out_specs=[VM] * len(outs),
        scratch_shapes=[
            pltpu.VMEM((count, model), BF),
            pltpu.VMEM((8, rows), F32),
            pltpu.VMEM((8, rows), F32),
            pltpu.VMEM((heads, size, rows), F32),
            DMA((2, 3)),
            DMA((2, 3)),
            DMA((2, 4, 2)),
            DMA((2, 4, 2)),
            DMA((2, 4)),
            DMA((2, 4)),
            DMA((3, 2, 3)),
            DMA((3, 2, 3)),
            DMA,
            DMA,
            DMA((2,)),
            DMA((2,)),
            DMA((4,)),
            DMA((4,)),
            DMA((7,)),
            DMA((8,)),
            DMA((8,)),
            DMA((8,)),
        ],
        compiler_params=pltpu.CompilerParams(
            collective_id=1, has_side_effects=True, vmem_limit_bytes=56 << 20
        ),
    )(*args)


def norm_back(grad_normed, normed, factor):
    return factor * (grad_normed - normed * jnp.mean(grad_normed * normed, axis=-1, keepdims=True))


def block_kernel(
    part, tok, gain, dy_hbm, halves,
    x1, dx1, dxl, gnf, ysum, gate_sum, down_sum, up_grad,
    w, dy, dy_t, h2, h2_t, hid, gate_back, up_back, whole, pb, s1, r1, r2, ry, passing, got, gx,
    ba, bb, bc, bd, ca, cb, cc, cd, ls, ms, hs, hr, fs, fr, ps, pr, xs, xr, ys, yr, gs, gr,
):
    me = Place()
    y, z, lo, k, t = me.y, me.z, me.lo, me.k, me.t
    rows, model = tok.shape
    both = 2 * rows
    inner = w.shape[-1]
    offsets = (2, 1, 3)

    def chip(i):
        return lax.rem(lo + lax.rem((i + 1) // 2, 2), 2), lax.rem(t + i // 2, 2)

    def columns(i):
        return pl.ds(pl.multiple_of(i * both, both), both)

    loads = [pltpu.make_async_copy(dy_hbm, dy, ls.at[6])]
    for i in range(3):
        loads.append(pltpu.make_async_copy(halves.at[i, 0], w.at[i, y, :, 0], ls.at[2 * i]))
        loads.append(pltpu.make_async_copy(halves.at[i, 1], w.at[i, :, z, 1], ls.at[2 * i + 1]))
    for copy in loads:
        copy.start()
    greet(
        [me.in_ring(*chip(i)) for i in (1, 2, 3)]
        + [me.sibling]
        + [me.along_z(j) for j in (1, 2, 3)]
        + [me.along_y(j) for j in (1, 2, 3)]
    )
    m1, m2, m3 = r1.at[pl.ds(0, 2)], s1.at[0], r2.at[2]
    cores = send(part.at[1 - k], m1, ms.at[0], ms.at[1], me.sibling)

    def weight_place(i, half, position, piece):
        if half == 0:
            return w.at[i, position, lax.rem(z + 4 - piece, 4), 0]
        return w.at[i, lax.rem(y + 4 - piece, 4), position, 1]

    def weight_source(i, half, piece):
        return halves.at[i, half, lax.rem((z if half == 0 else y) + 4 - piece, 4)]

    rings = [
        [
            RingGather(
                me.along_y if half == 0 else me.along_z,
                y if half == 0 else z,
                4,
                functools.partial(weight_place, i, half),
                functools.partial(weight_source, i, half),
                [sem.at[i, half] for sem in (ba, bb, bc, bd)],
            )
            for half in (0, 1)
        ]
        for i in range(3)
    ]

    def gather_start(i):
        for ring in rings[i]:
            for piece in range(4):
                ring.start(piece)

    def gather_forward(i):
        for ring in rings[i]:
            for piece in range(4):
                ring.forward(piece)

    def gather_finish(i):
        for ring in rings[i]:
            ring.finish()
        for copy in loads[2 * i + 1 : 2 * i + 3]:
            copy.wait()

    def weight(i):
        return w[i].reshape(model, inner)

    gather_start(0)
    loads[0].wait()

    def turn_dy(i, _):
        lo_i, t_i = chip(i)
        dy_t[:, columns(i)] = dy[lo_i, t_i].reshape(both, model).T
        return 0

    cores.wait()
    m2[...] = (part[k, 1 - t].astype(F32) + m1[1 - t].astype(F32)).astype(BF)
    across = send(m2, m3, ms.at[2], ms.at[3], me.in_ring(lo, 1 - t))
    lax.fori_loop(0, 4, turn_dy, 0)
    x = tok[...].astype(F32) + part[k, t].astype(F32) + m1[t].astype(F32)
    gather_forward(0)
    gather_start(1)
    across.wait()
    x = x + m3[...].astype(F32)
    x1[...] = x
    factor = lax.rsqrt(jnp.mean(x * x, axis=-1, keepdims=True) + epsilon)
    h2[lo, t, k] = (x * factor * gain[...]).astype(BF)

    def hidden_copy(i):
        block = h2.at[lo, t, k]
        return describe(block, block, hs.at[i - 1], hr.at[i - 1], me.in_ring(*chip(i)))

    def hidden_share(i):
        lo_i, t_i = chip(i)
        block = h2.at[lo_i, t_i, k]
        return describe(block, block, fs.at[i], fr.at[i], me.sibling)

    def part_share(i):
        return describe(pb.at[i], r1.at[i], ps.at[i], pr.at[i], me.sibling)

    def part_copy(i):
        return describe(
            s1.at[i], r2.at[i - 1], xs.at[i - 1], xr.at[i - 1], me.in_ring(*chip(i))
        )

    def result_share(i):
        return describe(pb.at[i], ry.at[i], ys.at[i], yr.at[i], me.sibling)

    for i in (1, 2, 3):
        hidden_copy(i).start()
    hidden_share(0).start()
    gather_forward(1)
    gather_start(2)

    def inward(i, _):
        lo_i, t_i = chip(i)
        hidden_share(i).wait_recv()

        @pl.when(i == 0)
        def _():
            gather_finish(0)

        h = h2[lo_i, t_i].reshape(both, model)
        gate = plain(h, weight(0))
        h2_t[:, columns(i)] = h.T

        @pl.when(i == 0)
        def _():
            gather_finish(1)

        up = plain(h, weight(1))
        sigmoid_gate = jax.nn.sigmoid(gate)
        silu_gate = gate * sigmoid_gate
        hid[i] = (silu_gate * up).astype(BF)
        slope = sigmoid_gate * (1.0 + gate * (1.0 - sigmoid_gate))
        gate_back[i] = (up * slope).astype(BF)
        up_back[i] = silu_gate.astype(BF)

        @pl.when(i < 3)
        def _():
            hidden_copy(i + 1).wait_recv()
            hidden_share(i + 1).start()

        return 0

    def gradient(target, left_t, right):
        flat = right.shape[0] * right.shape[1]
        step_rows = model // 4

        def some(m, _):
            r = pl.ds(pl.multiple_of(m * step_rows, step_rows), step_rows)
            value = plain(left_t[r, :], right[...].reshape(flat, inner))
            target[m] = value.astype(BF).reshape(target.shape[1:])
            return 0

        lax.fori_loop(0, 4, some, 0)

    def ring_sums(n, target):
        def along_z(position, piece, count):
            return target.at[pl.ds(piece, count), position, 0]

        def along_y(position, piece, count):
            return target.at[position, pl.ds(piece, count), 1]

        return [
            RingSum(
                along,
                position,
                source,
                passing.at[n, half],
                got.at[n, half],
                [sem.at[n, half] for sem in (ca, cb, cc, cd)],
            )
            for half, (along, position, source) in enumerate(
                ((me.along_z, z, along_z), (me.along_y, y, along_y))
            )
        ]

    lax.fori_loop(0, 4, inward, 0)
    gather_forward(2)
    down_rings, gate_rings = ring_sums(0, gx), ring_sums(1, w.at[0])
    gradient(gx, dy_t, hid)
    for one in down_rings:
        one.start()
    gather_finish(2)

    def homeward(i):
        part_share(i).wait_recv()
        s1[i] = (s1[i].astype(F32) + r1[i].astype(F32)).astype(BF)

        @pl.when(i > 0)
        def _():
            part_copy(i).start()

    def outward(n, _):
        i = lax.rem(n + 1, 4)
        lo_i, t_i = chip(i)
        grad_inner = plain(dy[lo_i, t_i].reshape(both, model), weight(2))

        @pl.when(n > 0)
        def _():
            homeward(n)

        @pl.when(n == 2)
        def _():
            for one in down_rings:
                one.middle()

        gate_back[i] = (grad_inner * gate_back[i].astype(F32)).astype(BF)
        up_back[i] = (grad_inner * up_back[i].astype(F32)).astype(BF)
        whole[...] = (
            by_columns(gate_back[i], weight(0)) + by_columns(up_back[i], weight(1))
        ).reshape(2, rows, model)
        pb[i] = whole[1 - k].astype(BF)
        s1[i] = whole[k].astype(BF)
        part_share(i).start()
        return 0

    lax.fori_loop(0, 4, outward, 0)
    gradient(w.at[0], h2_t, gate_back)
    for one in gate_rings:
        one.start()

    homeward(0)

    grad = s1[0].astype(F32)
    for i in (1, 2, 3):
        part_copy(i).wait_recv()
        grad = grad + r2[i - 1].astype(F32)
    x = x1[...]
    factor = lax.rsqrt(jnp.mean(x * x, axis=-1, keepdims=True) + epsilon)
    normed = x * factor
    gnf[...] = jnp.sum(grad * normed, axis=0, keepdims=True)
    back = dy[lo, t, k].astype(F32) + norm_back(grad * gain[...], normed, factor)
    dx1[...] = back
    dxl[k, t] = back.astype(BF)
    block = dxl.at[k, t]
    across = send(block, block, gs.at[0], gr.at[0], me.in_ring(lo, 1 - t))
    rest = [send(block, block, gs.at[1], gr.at[1], me.sibling)]
    def result(i, _):
        whole[...] = by_columns(hid[i], weight(2)).reshape(2, rows, model)
        part_share(i).wait_send()
        pb[i] = whole[1 - k].astype(BF)
        ysum[i] = whole[k].astype(BF)
        result_share(i).start()
        return 0

    lax.fori_loop(0, 4, result, 0)

    for one in gate_rings:
        one.middle()
    gradient(w.at[1], h2_t, up_back)
    last = pltpu.make_async_copy(w.at[1], up_grad, ls.at[0])
    last.start()
    rest.append(last)
    across.wait()
    block = dxl.at[k, 1 - t]
    rest.append(send(block, block, gs.at[2], gr.at[2], me.sibling))
    for i in range(4):
        result_share(i).wait()
        ysum[i] = (ysum[i].astype(F32) + ry[i].astype(F32)).astype(BF)
        hidden_share(i).wait_send()
    for i in (1, 2, 3):
        hidden_copy(i).wait_send()
        part_copy(i).wait_send()
    for half in (0, 1):
        down_sum[half] = down_rings[half].finish().astype(BF)
    for half in (0, 1):
        gate_sum[half] = gate_rings[half].finish().astype(BF)
    for copy in rest:
        copy.wait()


def block(part, tok, gain, dy, halves):
    rows, model = tok.shape
    half_rows, hidden = halves.shape[-2:]
    sums = halves.shape[1:]
    weights = (3, 4, 4, 2, half_rows, hidden)
    any_place = pl.BlockSpec(memory_space=pl.ANY)
    quarter = pltpu.VMEM((4, rows, model), BF)
    inner = pltpu.VMEM((4, 2 * rows, hidden), BF)
    flipped = pltpu.VMEM((model, 8 * rows), BF)
    return pl.pallas_call(
        block_kernel,
        out_shape=[
            shape((rows, model), F32),
            shape((rows, model), F32),
            shape((2, 2, rows, model), BF),
            shape((1, model), F32),
            shape((4, rows, model), BF),
            shape(sums, BF),
            shape(sums, BF),
            shape(weights[1:], BF),
        ],
        in_specs=[VM] * 3 + [any_place] * 2,
        out_specs=[VM] * 7 + [any_place],
        scratch_shapes=[
            pltpu.VMEM(weights, BF),
            pltpu.VMEM(dy.shape, BF),
            flipped,
            pltpu.VMEM(dy.shape, BF),
            flipped,
            inner,
            inner,
            inner,
            pltpu.VMEM((2, rows, model), F32),
            quarter,
            quarter,
            quarter,
            pltpu.VMEM((3, rows, model), BF),
            quarter,
            pltpu.VMEM((2, 2, 2, 2, half_rows, hidden), BF),
            pltpu.VMEM((2, 2, 2, 4, half_rows, hidden), BF),
            pltpu.VMEM(weights[1:], BF),
            DMA((3, 2, 4, 2)),
            DMA((3, 2, 4, 2)),
            DMA((3, 2, 4)),
            DMA((3, 2, 4)),
            DMA((2, 2, 2)),
            DMA((2, 2, 2)),
            DMA((2, 2, 2)),
            DMA((2, 2, 2)),
            DMA((7,)),
            DMA((4,)),
            DMA((3,)),
            DMA((3,)),
            DMA((4,)),
            DMA((4,)),
            DMA((4,)),
            DMA((4,)),
            DMA((3,)),
            DMA((3,)),
            DMA((4,)),
            DMA((4,)),
            DMA((3,)),
            DMA((3,)),
        ],
        compiler_params=pltpu.CompilerParams(
            collective_id=3, has_side_effects=True, vmem_limit_bytes=62 << 20
        ),
    )(part, tok, gain, dy, halves)


def rear_kernel(
    heads,
    g_hbm, gate_sum, down_sum, dxl, attn, q, kv, exact, lse, start_ref, ob, h1, cosines, sines, ysum, x1, dx1, tok, gain, gnf,
    a_all, ext_all, ffn_all, out, grad,
    do, dots, acc, keep, give, arrived, sums, landed, back, part, m1, m2, m3, left_t, ga,
    g, own, passing, got, p2, q1, sm, q2, fin, fin_w, e0, e1, es, e2, y2,
    ls, d1, d2, d3, d4, ms, ca, cb, cc, cd, fs2, fr2, as1, ar1, as2, ar2, as3, ar3, xs, xr, ss, sr, ts, tr, ys, yr,
    gs, gr,
):
    me = Place()
    y, z, lo, k, t = me.y, me.z, me.lo, me.k, me.t
    c = lo * 2 + k
    index = z * 2 + lo
    rows, width = q.shape
    size = width // heads
    slice_rows, model = tok.shape
    rowed = width + size
    offsets = (2, 1, 3)

    def in_x(dt, dc):
        return {"ctx": lax.rem(c + dc, 4), "tp": lax.rem(t + dt, 2)}

    def owner(b):
        return {"fsdp": y * 4 + b // 2, "ctx": lax.rem(b, 2) * 2 + k}

    ring = [(dt, dc) for dt in (0, 1) for dc in range(4) if dt or dc]

    summed_once = (gate_sum, own, down_sum)

    def second_hop(w, half, j):
        if half == 0:
            source, device = summed_once[w].at[0, lax.rem(y + j, 4)], me.along_y(j)
        else:
            source, device = summed_once[w].at[1, lax.rem(z + j, 4)], me.along_z(j)
        return describe(
            source, p2.at[w, half, j - 1], fs2.at[w, half, j - 1], fr2.at[w, half, j - 1], device
        )

    def second_hops(w, half):
        for j in offsets:
            second_hop(w, half, j).start()

    def up_along_z(position, piece, count):
        return g.at[pl.ds(piece, count), position, 0]

    def up_along_y(position, piece, count):
        return g.at[position, pl.ds(piece, count), 1]

    up_rings = [
        RingSum(
            along,
            position,
            source,
            passing.at[half],
            got.at[half],
            [sem.at[half] for sem in (ca, cb, cc, cd)],
        )
        for half, (along, position, source) in enumerate(
            ((me.along_z, z, up_along_z), (me.along_y, y, up_along_y))
        )
    ]

    def up_end(half):
        own[half] = up_rings[half].finish().astype(BF)
        second_hops(1, half)

    def early():
        for one in up_rings:
            one.middle()

    load = pltpu.make_async_copy(g_hbm, g, ls)
    load.start()
    greet(
        [me.along_z(j) for j in (1, 2, 3)]
        + [me.along_y(j) for j in (1, 2, 3)]
        + [in_x(dt, dc) for dt, dc in ring]
        + [{"fsdp": y * 4 + lax.rem(z + j, 4), "ctx": (1 - lo) * 2 + k} for j in (1, 2, 3)]
    )
    load.wait()
    for one in up_rings:
        one.start()
    second_hops(0, 0)
    second_hops(2, 0)
    near = [(1 - lo, t), (1 - lo, 1 - t), (lo, 1 - t)]
    results = [
        send(ysum.at[i + 1], y2.at[i], ys.at[i], yr.at[i], me.in_ring(*near[i])) for i in range(3)
    ]

    do[...] = plain(dxl[...], attn[:, rowed:]).astype(BF)
    for h in range(heads):
        product = exact[h] * do[:, h * size : (h + 1) * size].astype(F32).T
        dots[h : h + 1] = jnp.sum(product, axis=0, keepdims=True)
    acc[...] = jnp.zeros_like(acc)
    start = start_ref[...]
    first = index * rows

    def core_share(b):
        return describe(give.at[b], arrived.at[b], d1.at[b], d2.at[b], me.sibling)

    def home(b):
        return describe(sums.at[b], landed.at[index], d3.at[b], d4.at[index], owner(b))

    def step(b, _):
        keys = kv[0, b]
        values = kv[1, b]
        seen = visible_pairs(b, first, start, rows)
        dk = jnp.zeros((KEYS, size), F32)
        dv = jnp.zeros((KEYS, size), F32)
        for h in range(heads):
            q_h = q[:, h * size : (h + 1) * size]
            do_h = do[:, h * size : (h + 1) * size]
            s = jnp.where(seen, by_columns(keys, q_h), masked_score)
            p = jnp.exp(s - lse[h : h + 1])
            dv = dv + plain(p.astype(BF), do_h)
            dp = by_columns(values, do_h)
            ds = (p * (dp - dots[h : h + 1])).astype(BF)
            dk = dk + plain(ds, q_h)
            acc[h] = acc[h] + over_rows(keys, ds)
        keep[b] = jnp.where(k == 0, dk, dv)
        give[b] = jnp.where(k == 0, dv, dk)
        core_share(b).start()

        @pl.when(b > 0)
        def _():
            @pl.when(b == 2)
            def _():
                early()

            core_share(b - 1).wait_recv()
            sums[b - 1] = (keep[b - 1] + arrived[b - 1]).astype(BF)
            home(b - 1).start()

        return 0

    lax.fori_loop(0, index + 1, step, 0)

    @pl.when(index < 2)
    def _():
        early()

    second_hops(0, 1)
    second_hops(2, 1)

    result = x1[...] + ysum[0].astype(F32)
    for i in range(3):
        results[i].wait()
        result = result + y2[i].astype(F32)
    out[t] = result.astype(BF)
    mine = out.at[t]
    rest = [send(mine, mine, gs.at[1], gr.at[1], me.in_ring(lo, 1 - t))]
    up_end(1)
    up_end(0)

    scale = 1.0 / math.sqrt(size)
    for h in range(heads):
        dq = turned(acc[h].T * scale, cosines[...], -sines[...])
        e0[2:3, h * size : (h + 1) * size] = jnp.sum(dq, axis=0, keepdims=True)
        back[:, h * size : (h + 1) * size] = dq.astype(BF)
    left_t[...] = dxl[...].T
    blocks = ga.shape[:4]

    def spread(value):
        return value.astype(BF).reshape(blocks + (value.shape[1],))

    ga[:, :, :, :, rowed:] = spread(plain(left_t[...], ob[...]))
    left_t[...] = h1[...].T
    ga[:, :, :, :, :width] = spread(plain(left_t[...], back[:, :width]))

    core_share(index).wait_recv()
    dkv = keep[index] + arrived[index]
    keep[index] = dkv
    for b in range(1, 8):

        @pl.when(b > index)
        def _():
            describe(sums.at[0], landed.at[b], d3.at[0], d4.at[b], owner(0)).wait_recv()
            keep[index] = keep[index] + landed[b].astype(F32)

    is_key = k == 0
    dkv = turned(
        keep[index], jnp.where(is_key, cosines[...], 1.0), jnp.where(is_key, -sines[...], 0.0)
    )
    e0[2:3, width:rowed] = jnp.sum(dkv, axis=0, keepdims=True)
    back[:, width:] = dkv.astype(BF)
    part[...] = (
        by_columns(back[...], attn[:, :rowed]).astype(BF).reshape(2, 2, slice_rows, model)
    )
    cores = send(part.at[1 - k], m1, ms.at[0], ms.at[1], me.sibling)
    ga[:, :, :, :, width:rowed] = spread(plain(left_t[...], back[:, width:]))

    large = []
    for j in offsets:
        large.append(
            send(
                ga.at[:, lax.rem(z + j, 4), 0], q1.at[0, j - 1], as1.at[0, j - 1], ar1.at[0, j - 1], me.along_z(j)
            )
        )
        large.append(
            send(
                ga.at[lax.rem(y + j, 4), :, 1], q1.at[1, j - 1], as1.at[1, j - 1], ar1.at[1, j - 1], me.along_y(j)
            )
        )

    cores.wait()
    m2[...] = (part[k, 1 - t].astype(F32) + m1[1 - t].astype(F32)).astype(BF)
    across = send(m2, m3, ms.at[2], ms.at[3], me.in_ring(lo, 1 - t))
    quarter = sm.shape[2] // 2

    def summed(w, half):
        for j in offsets:
            second_hop(w, half, j).wait()
        here = summed_once[w][0, y] if half == 0 else summed_once[w][1, z]
        total = here.astype(F32)
        for j in range(3):
            total = total + p2[w, half, j].astype(F32)
        return total

    def to_owners(w):
        for half in (0, 1):
            total = summed(w, half)
            fin_w[w, 2 * half] = total[:quarter]
            fin_w[w, 2 * half + 1] = total[quarter:]
        ffn_all[w, c] = fin_w[w, c]
        return [
            send(
                fin_w.at[w, lax.rem(c + j, 4)], ffn_all.at[w, c], ts.at[w, j - 1], tr.at[w, j - 1], in_x(0, j)
            )
            for j in (2, 1, 3)
        ]

    rest += to_owners(2) + to_owners(0) + to_owners(1)

    x = tok[...].astype(F32)
    factor = lax.rsqrt(jnp.mean(x * x, axis=-1, keepdims=True) + epsilon)
    normed = x * factor
    dh1 = part[k, t].astype(F32) + m1[t].astype(F32)
    across.wait()
    dh1 = dh1 + m3[...].astype(F32)
    e0[0:1] = jnp.sum(dh1 * normed, axis=0, keepdims=True)
    e0[1:2] = gnf[...]
    e0[2:3, rowed:] = jnp.zeros((1, model - rowed), F32)
    e0[3:] = jnp.zeros((5, model), F32)
    small = [
        send(e0, e1.at[j - 1], ss.at[0, j - 1], sr.at[0, j - 1], me.along_z(j)) for j in offsets
    ]
    grad[t] = (dx1[...] + norm_back(dh1 * gain[...], normed, factor)).astype(BF)
    mine = grad.at[t]
    rest.append(send(mine, mine, gs.at[0], gr.at[0], me.in_ring(lo, 1 - t)))

    for copy in large:
        copy.wait()
    for half in (0, 1):
        here = ga[:, z, 0] if half == 0 else ga[y, :, 1]
        total = here.astype(F32)
        for j in range(3):
            total = total + q1[half, j].astype(F32)
        sm[half] = total.astype(BF)
    last = []
    for j in offsets:
        last.append(
            send(
                sm.at[0, lax.rem(y + j, 4)], q2.at[0, j - 1], as2.at[0, j - 1], ar2.at[0, j - 1], me.along_y(j)
            )
        )
        last.append(
            send(
                sm.at[1, lax.rem(z + j, 4)], q2.at[1, j - 1], as2.at[1, j - 1], ar2.at[1, j - 1], me.along_z(j)
            )
        )
    for copy in small:
        copy.wait()
    es[...] = (e0[...] + e1[0]) + (e1[1] + e1[2])
    small = [
        send(es, e2.at[j - 1], ss.at[1, j - 1], sr.at[1, j - 1], me.along_y(j)) for j in offsets
    ]

    for copy in small:
        copy.wait()
    ext_all[t, c] = (es[...] + e2[0]) + (e2[1] + e2[2])
    mine = ext_all.at[t, c]
    rest += [
        send(mine, mine, xs.at[i], xr.at[i], in_x(dt, dc)) for i, (dt, dc) in enumerate(ring)
    ]
    for copy in last:
        copy.wait()
    for half in (0, 1):
        here = sm[0, y] if half == 0 else sm[1, z]
        total = here.astype(F32)
        for j in range(3):
            total = total + q2[half, j].astype(F32)
        fin[2 * half] = total[:quarter]
        fin[2 * half + 1] = total[quarter:]
    a_all[c] = fin[c]
    rest += [
        send(fin.at[lax.rem(c + j, 4)], a_all.at[c], as3.at[j - 1], ar3.at[j - 1], in_x(0, j))
        for j in (2, 1, 3)
    ]

    def sent(b, _):
        core_share(b).wait_send()

        @pl.when(b < index)
        def _():
            home(b).wait_send()

        return 0

    lax.fori_loop(0, index + 1, sent, 0)
    for copy in rest:
        copy.wait()


def rear(heads, g, gate_sum, down_sum, dxl, attn, q, kv, exact, lse, start, ob, h1, cosines, sines, ysum, x1, dx1, tok, gain, gnf):
    rows, width = q.shape
    size = width // heads
    slice_rows, model = tok.shape
    hidden = g.shape[-1]
    total = attn.shape[1]
    half_rows = model // 32
    quarter = half_rows // 2
    shared = pltpu.VMEM(kv.shape[1:], F32)
    shared_low = pltpu.VMEM(kv.shape[1:], BF)
    slab = pltpu.VMEM((slice_rows, model), BF)
    args = (gate_sum, down_sum, dxl, attn, q, kv, exact, lse, start, ob, h1, cosines, sines, ysum, x1, dx1, tok, gain, gnf)
    outs = [
        shape((4, quarter, total), F32),
        shape((2, 4, 8, model), F32),
        shape((3, 4, quarter, hidden), F32),
        shape((2, slice_rows, model), BF),
        shape((2, slice_rows, model), BF),
    ]
    return pl.pallas_call(
        functools.partial(rear_kernel, heads),
        out_shape=outs,
        in_specs=[pl.BlockSpec(memory_space=pl.ANY)] + [VM] * len(args),
        out_specs=[VM] * len(outs),
        scratch_shapes=[
            pltpu.VMEM((rows, width), BF),
            pltpu.VMEM((8, rows), F32),
            pltpu.VMEM((heads, size, rows), F32),
            shared,
            shared,
            shared,
            shared_low,
            shared_low,
            pltpu.VMEM((rows, width + size), BF),
            pltpu.VMEM((2, 2, slice_rows, model), BF),
            pltpu.VMEM((2, slice_rows, model), BF),
            slab,
            slab,
            pltpu.VMEM((model, rows), BF),
            pltpu.VMEM((4, 4, 2, half_rows, total), BF),
            pltpu.VMEM(g.shape, BF),
            pltpu.VMEM((2, 4, half_rows, hidden), BF),
            pltpu.VMEM((2, 2, 2, half_rows, hidden), BF),
            pltpu.VMEM((2, 2, 4, half_rows, hidden), BF),
            pltpu.VMEM((3, 2, 3, half_rows, hidden), BF),
            pltpu.VMEM((2, 3, 4, half_rows, total), BF),
            pltpu.VMEM((2, 4, half_rows, total), BF),
            pltpu.VMEM((2, 3, half_rows, total), BF),
            pltpu.VMEM((4, quarter, total), F32),
            pltpu.VMEM((3, 4, quarter, hidden), F32),
            pltpu.VMEM((8, model), F32),
            pltpu.VMEM((3, 8, model), F32),
            pltpu.VMEM((8, model), F32),
            pltpu.VMEM((3, 8, model), F32),
            pltpu.VMEM((3, slice_rows, model), BF),
            DMA,
            DMA((8,)),
            DMA((8,)),
            DMA((8,)),
            DMA((8,)),
            DMA((4,)),
            DMA((2, 2)),
            DMA((2, 2)),
            DMA((2, 2)),
            DMA((2, 2)),
            DMA((3, 2, 3)),
            DMA((3, 2, 3)),
            DMA((2, 3)),
            DMA((2, 3)),
            DMA((2, 3)),
            DMA((2, 3)),
            DMA((3,)),
            DMA((3,)),
            DMA((7,)),
            DMA((7,)),
            DMA((2, 3)),
            DMA((2, 3)),
            DMA((3, 3)),
            DMA((3, 3)),
            DMA((3,)),
            DMA((3,)),
            DMA((2,)),
            DMA((2,)),
        ],
        compiler_params=pltpu.CompilerParams(
            collective_id=7, has_side_effects=True, vmem_limit_bytes=62 << 20
        ),
    )(g, *args)


def shards(
    tokens,
    segments,
    w_query,
    key_matrix,
    value_matrix,
    b_query,
    key_bias_vector,
    value_bias_vector,
    w_out,
    norm_attn,
    norm_ffn,
    w_gate,
    w_up,
    w_down,
    cotangent,
):
    f = lax.axis_index("fsdp")
    c = lax.axis_index("ctx")
    t = lax.axis_index("tp")
    k = c % 2
    is_key = k == 0
    size = key_matrix.shape[1]
    query_width = w_query.shape[1] // 2
    heads = query_width // size
    own_width = query_width + size
    model = tokens.shape[1]
    count = tokens.shape[0]
    slice_rows = count // 2
    shard_rows = w_query.shape[0]
    hidden = w_gate.shape[1] // 4
    padded = -(-hidden // 128) * 128

    def hidden_slice(w, axis):
        widths = [(0, 0), (0, 0)]
        widths[axis] = (0, 4 * padded - 4 * hidden)
        return lax.dynamic_slice_in_dim(jnp.pad(w, widths), c * padded, padded, axis)

    own_ffn = jnp.stack(
        [
            hidden_slice(w_gate, 1),
            hidden_slice(w_up, 1),
            hidden_slice(w_down, 0).T,
        ]
    )

    own_attn = jnp.concatenate(
        [
            lax.dynamic_slice_in_dim(w_query, k * query_width, query_width, 1),
            jnp.where(is_key, key_matrix, value_matrix),
            lax.dynamic_slice_in_dim(w_out, k * query_width, query_width, 0).T,
        ],
        axis=1,
    )
    own_tokens = lax.dynamic_slice_in_dim(tokens, t * slice_rows, slice_rows, 0)
    rows = 2 * count
    half_size = size // 2
    frequency = jnp.exp(jnp.arange(half_size, dtype=F32) * (-2.0 * math.log(rope_base) / size))
    frequency = jnp.concatenate([frequency, frequency])[None]
    gain_attn = norm_attn.astype(F32)[None]
    gain_ffn = norm_ffn.astype(F32)[None]
    bias = jnp.concatenate(
        [
            lax.dynamic_slice_in_dim(b_query, k * query_width, query_width, 0),
            jnp.where(is_key, key_bias_vector, value_bias_vector),
        ]
    ).astype(F32)[None]
    (
        attn_all,
        halves,
        dy_all,
        h1,
        q,
        kv,
        exact,
        ob,
        lse,
        starts,
        cosines,
        sines,
        part,
    ) = front(heads, own_attn, own_ffn, tokens, cotangent, segments, gain_attn, bias, frequency)
    x1, dx1, dxl, grad_norm_two, ysum, gate_sum, down_sum, up_grad = block(
        part, own_tokens, gain_ffn, dy_all, halves
    )
    a_all, ext_all, ffn_all, output, grad_tokens = rear(
        heads,
        up_grad,
        gate_sum,
        down_sum,
        dxl.reshape(rows, model),
        attn_all.reshape(model, own_width + query_width),
        q,
        kv,
        exact,
        lse,
        starts,
        ob,
        h1,
        cosines,
        sines,
        ysum,
        x1,
        dx1,
        own_tokens,
        gain_attn,
        grad_norm_two,
    )
    owner_rows = shard_rows // 4
    a_all = a_all[:2] + a_all[2:]

    def side_by_side(pieces):
        return jnp.concatenate([pieces[i] for i in range(4)], axis=1)[:, : 4 * hidden]

    owner = f * 4 + c
    norms = lax.dynamic_slice_in_dim(
        jnp.sum(ext_all[:, :, :2].reshape(8, 2, model), axis=0), owner * owner_rows, owner_rows, 1
    )
    biases = lax.dynamic_index_in_dim(ext_all[:, :, 2, :own_width], t, 0, keepdims=False)
    biases = (biases[:2] + biases[2:]).reshape(2, heads + 1, size)
    biases = lax.dynamic_slice_in_dim(biases, owner * 2, 2, 2)
    return (
        output.reshape(count, model),
        grad_tokens.reshape(count, model).astype(F32),
        jnp.concatenate([a_all[0, :, :query_width], a_all[1, :, :query_width]], axis=1),
        a_all[0, :, query_width:own_width],
        a_all[1, :, query_width:own_width],
        biases[:, :heads].reshape(2 * heads, 2),
        biases[0, heads:],
        biases[1, heads:],
        jnp.concatenate([a_all[0, :, own_width:], a_all[1, :, own_width:]], axis=1).T,
        norms[0],
        norms[1],
        side_by_side(ffn_all[0]),
        side_by_side(ffn_all[1]),
        side_by_side(ffn_all[2]).T,
    )


def solution(mesh):
    both = ("fsdp", "ctx")
    in_specs = (
        P(both, None),
        P(),
        P("fsdp", "tp"),
        P("fsdp", "tp"),
        P("fsdp", "tp"),
        P("tp"),
        P("tp"),
        P("tp"),
        P("tp", "fsdp"),
        P(),
        P(),
        P("fsdp", "tp"),
        P("fsdp", "tp"),
        P("tp", "fsdp"),
        P(both, None),
    )
    out_specs = (
        P(both, None),
        P(both, None),
        P(both, "tp"),
        P(both, "tp"),
        P(both, "tp"),
        P("tp", both),
        P("tp", both),
        P("tp", both),
        P("tp", both),
        P(both),
        P(both),
        P(both, "tp"),
        P(both, "tp"),
        P("tp", both),
    )
    return jax.shard_map(shards, mesh=mesh, in_specs=in_specs, out_specs=out_specs, check_vma=False)
```

```python
import functools
import math

import jax
import jax.numpy as jnp
import numpy as np
from jax import lax
from jax.experimental import pallas as pl
from jax.experimental.pallas import tpu as pltpu
from jax.sharding import PartitionSpec as P

MESH = pl.DeviceIdType.MESH
VM = pl.BlockSpec(memory_space=pltpu.VMEM)
DMA = pltpu.SemaphoreType.DMA
BF = jnp.bfloat16
F32 = jnp.float32

epsilon = 1e-06
rope_base = 1000000.0
masked_score = -1e30
KEYS = 512


class Place:
    def __init__(self):
        f = lax.axis_index("fsdp")
        c = lax.axis_index("ctx")
        self.y, self.z = f // 4, f % 4
        self.lo, self.k = c // 2, c % 2
        self.t = lax.axis_index("tp")

    def along_y(self, j):
        return {"fsdp": lax.rem(self.y + j, 4) * 4 + self.z}

    def along_z(self, j):
        return {"fsdp": self.y * 4 + lax.rem(self.z + j, 4)}

    @property
    def sibling(self):
        return {"ctx": self.lo * 2 + 1 - self.k}

    def in_ring(self, lo, t):
        return {"ctx": lo * 2 + self.k, "tp": t}

    @property
    def others(self):
        return [(self.lo, 1 - self.t), (1 - self.lo, self.t), (1 - self.lo, 1 - self.t)]


def greet(devices):
    barrier = pltpu.get_barrier_semaphore()
    for device in devices:
        pl.semaphore_signal(barrier, inc=1, device_id=device, device_id_type=MESH)
    pl.semaphore_wait(barrier, len(devices))


def describe(source, target, send_sem, recv_sem, device):
    return pltpu.make_async_remote_copy(
        src_ref=source,
        dst_ref=target,
        send_sem=send_sem,
        recv_sem=recv_sem,
        device_id=device,
        device_id_type=MESH,
    )


def send(source, target, send_sem, recv_sem, device):
    copy = describe(source, target, send_sem, recv_sem, device)
    copy.start()
    return copy


def comm_call(body, outs, scratch, collective_id, mib, *args):
    return pl.pallas_call(
        body,
        out_shape=outs,
        in_specs=[VM] * len(args),
        out_specs=[VM] * len(outs),
        scratch_shapes=scratch,
        compiler_params=pltpu.CompilerParams(
            collective_id=collective_id, has_side_effects=True, vmem_limit_bytes=mib << 20
        ),
    )(*args)


def shape(dims, kind):
    return jax.ShapeDtypeStruct(dims, kind)


def over_rows(a, b):
    return lax.dot_general(a, b, (((0,), (0,)), ((), ())), preferred_element_type=F32)


def by_columns(a, b):
    return lax.dot_general(a, b, (((1,), (1,)), ((), ())), preferred_element_type=F32)


def plain(a, b):
    return lax.dot_general(a, b, (((1,), (0,)), ((), ())), preferred_element_type=F32)


def visible_pairs(block, first, start, rows):
    key = block * KEYS + lax.broadcasted_iota(jnp.int32, (KEYS, rows), 0)
    row = first + lax.broadcasted_iota(jnp.int32, (1, rows), 1)
    return (key >= start) & (key <= row)


class RingGather:
    def __init__(self, along, position, pieces, target, source, sems):
        self.along, self.position, self.pieces = along, position, pieces
        self.target, self.source, self.sems = target, source, sems

    def hop(self, i, way):
        s, r = self.sems[:2]
        return describe(
            self.source(i),
            self.target(self.position, i),
            s.at[i, way],
            r.at[i, way],
            self.along(1 if way == 0 else 3),
        )

    def onward(self, i):
        s, r = self.sems[2:]
        way = i // 2
        block = self.target(lax.rem(self.position + (3 if way == 0 else 1), 4), i)
        return describe(block, block, s.at[i], r.at[i], self.along(1 if way == 0 else 3))

    def start(self, i):
        self.hop(i, 0).start()
        self.hop(i, 1).start()

    def forward(self, i):
        self.hop(i, i // 2).wait_recv()
        self.onward(i).start()

    def finish(self):
        for i in range(4):
            self.hop(i, 1 - i // 2).wait_recv()
            self.onward(i).wait()
            self.hop(i, 0).wait_send()
            self.hop(i, 1).wait_send()


class RingSum:
    def __init__(self, along, position, source, passing, got, sems):
        self.along, self.position, self.source = along, position, source
        self.passing, self.got, self.sems = passing, got, sems

    def at(self, offset):
        return lax.rem(self.position + offset, 4)

    def first(self, way):
        s, r = self.sems[:2]
        return describe(
            self.source(self.at(2), 2 * way, 2),
            self.passing.at[way],
            s.at[way],
            r.at[way],
            self.along(1 if way == 0 else 3),
        )

    def second(self, way):
        s, r = self.sems[2:]
        offset = 1 if way == 0 else 3
        return describe(
            self.source(self.at(offset), 0, 4), self.got.at[way], s.at[way], r.at[way], self.along(offset)
        )

    def start(self):
        for way in (0, 1):
            self.first(way).start()

    def middle(self):
        for way in (0, 1):
            self.first(way).wait()
            near = self.source(self.at(1 if way == 0 else 3), 2 * way, 2)
            near[...] = (near[...].astype(F32) + self.passing[way].astype(F32)).astype(BF)
            self.second(way).start()

    def finish(self):
        total = self.source(self.position, 0, 4)[...].astype(F32)
        for way in (0, 1):
            self.second(way).wait()
            total = total + self.got[way].astype(F32)
        return total


def turned(values, cosines, sines):
    return values * cosines - pltpu.roll(values, values.shape[-1] // 2, 1) * sines


def front_kernel(
    heads,
    w, ffn, tok, dy, segments, gain, bias, frequency,
    w_out, halves, dy_all, h1_out, q, kv_out, exact, ob, lse, starts, cosines, sines, part,
    w_all, h1, kv, tok2, top, total, acc,
    s1, r1, wa, wb, wc, wd, s3, r3, ts, tr, ds, dr, fs, fr, ks, kr, cs, cr, ls, os,
):
    me = Place()
    y, z, lo, k, t = me.y, me.z, me.lo, me.k, me.t
    index = z * 2 + lo
    count, model = tok.shape
    rows = 2 * count
    width, size = q.shape[1], exact.shape[1]
    rowed = width + size
    shard = w.shape[0] // 2
    parts = (pl.ds(0, shard), pl.ds(shard, shard))
    near = [me.in_ring(1 - lo, t), me.in_ring(1 - lo, 1 - t)]
    offsets = (1, 3, 2)
    greet(
        [me.along_z(j) for j in (1, 2, 3)]
        + [me.along_y(j) for j in (1, 2, 3)]
        + [me.sibling]
        + near
        + [{"fsdp": y * 4 + lax.rem(z + j, 4), "ctx": (1 - lo) * 2 + k} for j in (1, 2, 3)]
    )

    def attn_place(half, position, i):
        if half == 0:
            return w_all.at[position, lax.rem(z + 4 - i, 4), parts[0]]
        return w_all.at[lax.rem(y + 4 - i, 4), position, parts[1]]

    def attn_source(half, i):
        if i == 0:
            return w.at[parts[half]]
        return attn_place(half, y if half == 0 else z, i)

    def first_hop(half, j):
        along = me.along_z if half == 0 else me.along_y
        return describe(
            w.at[parts[half]],
            w_all.at[y, z, parts[half]],
            s1.at[half, j - 1],
            r1.at[half, j - 1],
            along(j),
        )

    rings = [
        RingGather(
            me.along_y if half == 0 else me.along_z,
            y if half == 0 else z,
            4,
            functools.partial(attn_place, half),
            functools.partial(attn_source, half),
            [sem.at[half] for sem in (wa, wb, wc, wd)],
        )
        for half in (0, 1)
    ]
    for j in offsets:
        for half in (0, 1):
            first_hop(half, j).start()
    for ring in rings:
        ring.start(0)
    tokens_share = send(tok, tok2, ts, tr, me.sibling)
    slab = count // 2
    near_copies = [
        send(dy.at[pl.ds(t * slab, slab)], dy_all.at[lo, t, k], ds.at[i], dr.at[i], near[i])
        for i in (0, 1)
    ]
    rest = [
        send(dy.at[pl.ds(h * slab, slab)], dy_all.at[lo, h, k], fs.at[2 + h], fr.at[2 + h], me.sibling)
        for h in (0, 1)
    ]
    w_all[y, z] = w[...]
    stores = [
        pltpu.make_async_copy(dy.at[pl.ds(h * slab, slab)], dy_all.at[lo, h, k], os.at[h])
        for h in (0, 1)
    ]
    for copy in stores:
        copy.start()

    first = pl.multiple_of(index * rows, rows)
    everyone = segments[pl.ds(y, 1), :]
    mine = segments[pl.ds(y, 1), pl.ds(first, rows)]
    start = jnp.zeros((1, rows), jnp.int32)
    for number in (1, 2, 3):
        begin = jnp.sum(jnp.where(everyone < number, 1.0, 0.0), axis=1, keepdims=True)
        start = jnp.where(mine == number, begin.astype(jnp.int32), start)
    starts[...] = start
    row = first + lax.broadcasted_iota(jnp.int32, (1, rows), 1)
    pos = jnp.broadcast_to((row - start).astype(F32), (8, rows)).T[:, :1]
    angles = pos * frequency[...]
    lane = lax.broadcasted_iota(jnp.int32, (1, size), 1)
    cosines[...] = jnp.cos(angles)
    sines[...] = jnp.sin(angles) * jnp.where(lane < size // 2, 1.0, -1.0)

    for j in offsets:
        for half in (0, 1):
            first_hop(half, j).wait()
            rings[half].start(j)

    def normed(x):
        x = x.astype(F32)
        factor = lax.rsqrt(jnp.mean(x * x, axis=-1, keepdims=True) + epsilon)
        return (x * factor * gain[...]).astype(BF)

    h1[pl.ds(pl.multiple_of(k * count, count), count)] = normed(tok[...])
    tokens_share.wait()
    h1[pl.ds(pl.multiple_of((1 - k) * count, count), count)] = normed(tok2[...])

    for i in (0, 1, 3, 2):
        for ring in rings:
            ring.forward(i)

    def ffn_hop(i, half, j):
        along, here = (me.along_z, z) if half == 0 else (me.along_y, y)
        return describe(
            ffn.at[i, parts[half]],
            halves.at[i, half, here],
            s3.at[i, half, j - 1],
            r3.at[i, half, j - 1],
            along(j),
        )

    def ffn_hops(i):
        for half in (0, 1):
            for j in offsets:
                ffn_hop(i, half, j).start()
            there = halves.at[i, half, z if half == 0 else y]
            copy = pltpu.make_async_copy(ffn.at[i, parts[half]], there, ls.at[i, half])
            copy.start()
            stores.append(copy)

    ffn_hops(0)
    for ring in rings:
        ring.finish()
    for i, (source, there) in enumerate(((w_all, w_out), (h1, h1_out))):
        copy = pltpu.make_async_copy(source, there, os.at[2 + i])
        copy.start()
        stores.append(copy)

    inward = w_all[:, :, :, :rowed].reshape(model, rowed)
    linear = plain(h1[...], inward) + bias[...]
    scale = 1.0 / math.sqrt(size)
    is_key = k == 0
    own = turned(
        linear[:, width:],
        jnp.where(is_key, cosines[...], 1.0),
        jnp.where(is_key, sines[...], 0.0),
    )
    kv[k, index] = own.astype(BF)
    own_keys = kv.at[k, index]

    def keys_copy(i, device):
        return describe(own_keys, own_keys, ks.at[i], kr.at[index], device)

    targets = [(dz, to) for dz in (1, 2, 3) for to in (0, 1)]

    def target(dz, to):
        return {"fsdp": y * 4 + lax.rem(z + dz, 4), "ctx": to * 2 + k}

    for i, (dz, to) in enumerate(targets):

        @pl.when(z + dz < 4)
        def _():
            keys_copy(i, target(dz, to)).start()

    @pl.when(lo == 0)
    def _():
        keys_copy(6, {"ctx": 2 + k}).start()

    def keys_share(b):
        there = kv.at[k, b]
        return describe(there, there, cs.at[b], cr.at[b], me.sibling)

    keys_share(index).start()
    for h in range(heads):
        here = slice(h * size, (h + 1) * size)
        q[:, here] = (turned(linear[:, here], cosines[...], sines[...]) * scale).astype(BF)

    ffn_hops(1)
    ffn_hops(2)
    for i, half in ((0, t), (1, 1 - t)):
        near_copies[i].wait()
        there = dy_all.at[1 - lo, half, k]
        rest.append(send(there, there, fs.at[i], fr.at[i], me.sibling))

    top[...] = jnp.full_like(top, masked_score)
    total[...] = jnp.zeros_like(total)
    acc[...] = jnp.zeros_like(acc)

    def step(i, _):
        b = index - i

        @pl.when(b > 0)
        def _():
            there = kv.at[k, b - 1]
            describe(there, there, ks.at[0], kr.at[b - 1], me.sibling).wait_recv()
            keys_share(b - 1).start()

        keys_share(b).wait_recv()
        keys = kv[0, b]
        values = kv[1, b]
        seen = visible_pairs(b, first, start, rows)
        for h in range(heads):
            s = by_columns(keys, q[:, h * size : (h + 1) * size])
            s = jnp.where(seen, s, masked_score)
            before = top[h : h + 1]
            now = jnp.maximum(before, jnp.max(s, axis=0, keepdims=True))
            p = jnp.exp(s - now)
            shrink = jnp.exp(before - now)
            top[h : h + 1] = now
            total[h : h + 1] = total[h : h + 1] * shrink + jnp.sum(p, axis=0, keepdims=True)
            acc[h] = acc[h] * shrink + over_rows(values, p.astype(BF))
        return 0

    lax.fori_loop(0, index + 1, step, 0)
    copy = pltpu.make_async_copy(kv, kv_out, os.at[4])
    copy.start()
    stores.append(copy)
    lse[...] = jnp.zeros_like(lse)
    for h in range(heads):
        sums = total[h : h + 1]
        lse[h : h + 1] = top[h : h + 1] + jnp.log(sums)
        out = acc[h] / sums
        exact[h] = out
        ob[:, h * size : (h + 1) * size] = out.T.astype(BF)
    outward = w_all[:, :, :, rowed:].reshape(model, width)
    part[...] = by_columns(ob[...], outward).astype(BF).reshape(part.shape)

    for i, (dz, to) in enumerate(targets):

        @pl.when(z + dz < 4)
        def _():
            keys_copy(i, target(dz, to)).wait_send()

    @pl.when(lo == 0)
    def _():
        keys_copy(6, {"ctx": 2 + k}).wait_send()

    def shared(b, _):
        keys_share(b).wait_send()
        return 0

    lax.fori_loop(0, index + 1, shared, 0)
    for i in range(3):
        for half in (0, 1):
            for j in offsets:
                ffn_hop(i, half, j).wait()
    for copy in rest + stores:
        copy.wait()


def front(heads, w, ffn, tok, dy, segments, gain, bias, frequency):
    shard, total = w.shape
    hidden = ffn.shape[2]
    count, model = tok.shape
    rows = 2 * count
    width = bias.shape[1] - frequency.shape[1]
    size = frequency.shape[1]
    far = pl.BlockSpec(memory_space=pl.ANY)
    args = (w, ffn, tok, dy, segments, gain, bias, frequency)
    outs = [
        shape((4, 4, shard, total), BF),
        shape((3, 2, 4, shard // 2, hidden), BF),
        shape((2, 2, 2, count // 2, model), BF),
        shape((rows, model), BF),
        shape((rows, width), BF),
        shape((2, 8, rows, size), BF),
        shape((heads, size, rows), F32),
        shape((rows, width), BF),
        shape((8, rows), F32),
        shape((1, rows), jnp.int32),
        shape((rows, size), F32),
        shape((rows, size), F32),
        shape((2, 2, count // 2, model), BF),
    ]
    return pl.pallas_call(
        functools.partial(front_kernel, heads),
        out_shape=outs,
        in_specs=[VM] * len(args),
        out_specs=[far] * 4 + [VM, far] + [VM] * (len(outs) - 6),
        scratch_shapes=[
            pltpu.VMEM((4, 4, shard, total), BF),
            pltpu.VMEM((rows, model), BF),
            pltpu.VMEM((2, 8, rows, size), BF),
            pltpu.VMEM((count, model), BF),
            pltpu.VMEM((8, rows), F32),
            pltpu.VMEM((8, rows), F32),
            pltpu.VMEM((heads, size, rows), F32),
            DMA((2, 3)),
            DMA((2, 3)),
            DMA((2, 4, 2)),
            DMA((2, 4, 2)),
            DMA((2, 4)),
            DMA((2, 4)),
            DMA((3, 2, 3)),
            DMA((3, 2, 3)),
            DMA,
            DMA,
            DMA((2,)),
            DMA((2,)),
            DMA((4,)),
            DMA((4,)),
            DMA((7,)),
            DMA((8,)),
            DMA((8,)),
            DMA((8,)),
            DMA((3, 2)),
            DMA((5,)),
        ],
        compiler_params=pltpu.CompilerParams(
            collective_id=1, has_side_effects=True, vmem_limit_bytes=56 << 20
        ),
    )(*args)


def norm_back(grad_normed, normed, factor):
    return factor * (grad_normed - normed * jnp.mean(grad_normed * normed, axis=-1, keepdims=True))


def block_kernel(
    part, tok, gain, dy_hbm, halves,
    x1, dx1, dxl, gnf, ysum, gate_sum, down_sum, up_grad,
    w, dy, dy_t, h2, h2_t, hid, gate_back, up_back, whole, pb, s1, r1, r2, ry, passing, got, gx,
    ba, bb, bc, bd, ca, cb, cc, cd, ls, ms, hs, hr, fs, fr, ps, pr, xs, xr, ys, yr, gs, gr,
):
    me = Place()
    y, z, lo, k, t = me.y, me.z, me.lo, me.k, me.t
    rows, model = tok.shape
    both = 2 * rows
    inner = w.shape[-1]
    offsets = (2, 1, 3)

    def chip(i):
        return lax.rem(lo + lax.rem((i + 1) // 2, 2), 2), lax.rem(t + i // 2, 2)

    def columns(i):
        return pl.ds(pl.multiple_of(i * both, both), both)

    loads = [pltpu.make_async_copy(dy_hbm, dy, ls.at[6])]
    for i in range(3):
        loads.append(pltpu.make_async_copy(halves.at[i, 0], w.at[i, y, :, 0], ls.at[2 * i]))
        loads.append(pltpu.make_async_copy(halves.at[i, 1], w.at[i, :, z, 1], ls.at[2 * i + 1]))
    for copy in loads:
        copy.start()
    greet(
        [me.in_ring(*chip(i)) for i in (1, 2, 3)]
        + [me.sibling]
        + [me.along_z(j) for j in (1, 2, 3)]
        + [me.along_y(j) for j in (1, 2, 3)]
    )
    m1, m2, m3 = r1.at[pl.ds(0, 2)], s1.at[0], r2.at[2]
    cores = send(part.at[1 - k], m1, ms.at[0], ms.at[1], me.sibling)

    def weight_place(i, half, position, piece):
        if half == 0:
            return w.at[i, position, lax.rem(z + 4 - piece, 4), 0]
        return w.at[i, lax.rem(y + 4 - piece, 4), position, 1]

    def weight_source(i, half, piece):
        return halves.at[i, half, lax.rem((z if half == 0 else y) + 4 - piece, 4)]

    rings = [
        [
            RingGather(
                me.along_y if half == 0 else me.along_z,
                y if half == 0 else z,
                4,
                functools.partial(weight_place, i, half),
                functools.partial(weight_source, i, half),
                [sem.at[i, half] for sem in (ba, bb, bc, bd)],
            )
            for half in (0, 1)
        ]
        for i in range(3)
    ]

    def gather_start(i):
        for ring in rings[i]:
            for piece in range(4):
                ring.start(piece)

    def gather_forward(i):
        for ring in rings[i]:
            for piece in range(4):
                ring.forward(piece)

    def gather_finish(i):
        for ring in rings[i]:
            ring.finish()
        for copy in loads[2 * i + 1 : 2 * i + 3]:
            copy.wait()

    def weight(i):
        return w[i].reshape(model, inner)

    gather_start(0)
    gather_start(1)
    loads[0].wait()

    def turn_dy(i, _):
        lo_i, t_i = chip(i)
        dy_t[:, columns(i)] = dy[lo_i, t_i].reshape(both, model).T
        return 0

    cores.wait()
    m2[...] = (part[k, 1 - t].astype(F32) + m1[1 - t].astype(F32)).astype(BF)
    across = send(m2, m3, ms.at[2], ms.at[3], me.in_ring(lo, 1 - t))
    lax.fori_loop(0, 4, turn_dy, 0)
    x = tok[...].astype(F32) + part[k, t].astype(F32) + m1[t].astype(F32)
    gather_forward(0)
    across.wait()
    x = x + m3[...].astype(F32)
    x1[...] = x
    factor = lax.rsqrt(jnp.mean(x * x, axis=-1, keepdims=True) + epsilon)
    h2[lo, t, k] = (x * factor * gain[...]).astype(BF)

    def hidden_copy(i):
        block = h2.at[lo, t, k]
        return describe(block, block, hs.at[i - 1], hr.at[i - 1], me.in_ring(*chip(i)))

    def hidden_share(i):
        lo_i, t_i = chip(i)
        block = h2.at[lo_i, t_i, k]
        return describe(block, block, fs.at[i], fr.at[i], me.sibling)

    def part_share(i):
        return describe(pb.at[i], r1.at[i], ps.at[i], pr.at[i], me.sibling)

    def part_copy(i):
        return describe(
            s1.at[i], r2.at[i - 1], xs.at[i - 1], xr.at[i - 1], me.in_ring(*chip(i))
        )

    def result_share(i):
        return describe(pb.at[i], ry.at[i], ys.at[i], yr.at[i], me.sibling)

    for i in (1, 2, 3):
        hidden_copy(i).start()
    hidden_share(0).start()
    gather_forward(1)
    gather_start(2)

    def inward(i, _):
        lo_i, t_i = chip(i)
        hidden_share(i).wait_recv()

        @pl.when(i == 0)
        def _():
            gather_finish(0)

        h = h2[lo_i, t_i].reshape(both, model)
        gate = plain(h, weight(0))
        h2_t[:, columns(i)] = h.T

        @pl.when(i == 0)
        def _():
            gather_finish(1)

        up = plain(h, weight(1))
        sigmoid_gate = jax.nn.sigmoid(gate)
        silu_gate = gate * sigmoid_gate
        hid[i] = (silu_gate * up).astype(BF)
        slope = sigmoid_gate * (1.0 + gate * (1.0 - sigmoid_gate))
        gate_back[i] = (up * slope).astype(BF)
        up_back[i] = silu_gate.astype(BF)

        @pl.when(i < 3)
        def _():
            hidden_copy(i + 1).wait_recv()
            hidden_share(i + 1).start()

        return 0

    def gradient(target, left_t, right):
        flat = right.shape[0] * right.shape[1]
        step_rows = model // 4

        def some(m, _):
            r = pl.ds(pl.multiple_of(m * step_rows, step_rows), step_rows)
            value = plain(left_t[r, :], right[...].reshape(flat, inner))
            target[m] = value.astype(BF).reshape(target.shape[1:])
            return 0

        lax.fori_loop(0, 4, some, 0)

    def ring_sums(n, target):
        def along_z(position, piece, count):
            return target.at[pl.ds(piece, count), position, 0]

        def along_y(position, piece, count):
            return target.at[position, pl.ds(piece, count), 1]

        return [
            RingSum(
                along,
                position,
                source,
                passing.at[n, half],
                got.at[n, half],
                [sem.at[n, half] for sem in (ca, cb, cc, cd)],
            )
            for half, (along, position, source) in enumerate(
                ((me.along_z, z, along_z), (me.along_y, y, along_y))
            )
        ]

    lax.fori_loop(0, 4, inward, 0)
    gather_forward(2)
    down_rings, gate_rings = ring_sums(0, gx), ring_sums(1, w.at[0])
    gradient(gx, dy_t, hid)
    for one in down_rings:
        one.start()
    gather_finish(2)

    def homeward(i):
        part_share(i).wait_recv()
        s1[i] = (s1[i].astype(F32) + r1[i].astype(F32)).astype(BF)

        @pl.when(i > 0)
        def _():
            part_copy(i).start()

    def outward(n, _):
        i = lax.rem(n + 1, 4)
        lo_i, t_i = chip(i)
        grad_inner = plain(dy[lo_i, t_i].reshape(both, model), weight(2))

        @pl.when(n > 0)
        def _():
            homeward(n)

        @pl.when(n == 2)
        def _():
            for one in down_rings:
                one.middle()

        gate_back[i] = (grad_inner * gate_back[i].astype(F32)).astype(BF)
        up_back[i] = (grad_inner * up_back[i].astype(F32)).astype(BF)
        whole[...] = (
            by_columns(gate_back[i], weight(0)) + by_columns(up_back[i], weight(1))
        ).reshape(2, rows, model)
        pb[i] = whole[1 - k].astype(BF)
        s1[i] = whole[k].astype(BF)
        part_share(i).start()
        return 0

    lax.fori_loop(0, 4, outward, 0)
    gradient(w.at[0], h2_t, gate_back)
    for one in gate_rings:
        one.start()

    homeward(0)

    grad = s1[0].astype(F32)
    for i in (1, 2, 3):
        part_copy(i).wait_recv()
        grad = grad + r2[i - 1].astype(F32)
    x = x1[...]
    factor = lax.rsqrt(jnp.mean(x * x, axis=-1, keepdims=True) + epsilon)
    normed = x * factor
    gnf[...] = jnp.sum(grad * normed, axis=0, keepdims=True)
    back = dy[lo, t, k].astype(F32) + norm_back(grad * gain[...], normed, factor)
    dx1[...] = back
    dxl[k, t] = back.astype(BF)
    block = dxl.at[k, t]
    across = send(block, block, gs.at[0], gr.at[0], me.in_ring(lo, 1 - t))
    rest = [send(block, block, gs.at[1], gr.at[1], me.sibling)]
    for one in gate_rings:
        one.middle()

    def result(i, _):
        whole[...] = by_columns(hid[i], weight(2)).reshape(2, rows, model)
        part_share(i).wait_send()
        pb[i] = whole[1 - k].astype(BF)
        ysum[i] = whole[k].astype(BF)
        result_share(i).start()
        return 0

    lax.fori_loop(0, 4, result, 0)

    gradient(w.at[1], h2_t, up_back)
    last = pltpu.make_async_copy(w.at[1], up_grad, ls.at[0])
    last.start()
    rest.append(last)
    across.wait()
    block = dxl.at[k, 1 - t]
    rest.append(send(block, block, gs.at[2], gr.at[2], me.sibling))
    for i in range(4):
        result_share(i).wait()
        ysum[i] = (ysum[i].astype(F32) + ry[i].astype(F32)).astype(BF)
        hidden_share(i).wait_send()
    for i in (1, 2, 3):
        hidden_copy(i).wait_send()
        part_copy(i).wait_send()
    for half in (0, 1):
        down_sum[half] = down_rings[half].finish().astype(BF)
    for half in (0, 1):
        gate_sum[half] = gate_rings[half].finish().astype(BF)
    for copy in rest:
        copy.wait()


def block(part, tok, gain, dy, halves):
    rows, model = tok.shape
    half_rows, hidden = halves.shape[-2:]
    sums = halves.shape[1:]
    weights = (3, 4, 4, 2, half_rows, hidden)
    any_place = pl.BlockSpec(memory_space=pl.ANY)
    quarter = pltpu.VMEM((4, rows, model), BF)
    inner = pltpu.VMEM((4, 2 * rows, hidden), BF)
    flipped = pltpu.VMEM((model, 8 * rows), BF)
    return pl.pallas_call(
        block_kernel,
        out_shape=[
            shape((rows, model), F32),
            shape((rows, model), F32),
            shape((2, 2, rows, model), BF),
            shape((1, model), F32),
            shape((4, rows, model), BF),
            shape(sums, BF),
            shape(sums, BF),
            shape(weights[1:], BF),
        ],
        in_specs=[VM] * 3 + [any_place] * 2,
        out_specs=[VM] * 7 + [any_place],
        scratch_shapes=[
            pltpu.VMEM(weights, BF),
            pltpu.VMEM(dy.shape, BF),
            flipped,
            pltpu.VMEM(dy.shape, BF),
            flipped,
            inner,
            inner,
            inner,
            pltpu.VMEM((2, rows, model), F32),
            quarter,
            quarter,
            quarter,
            pltpu.VMEM((3, rows, model), BF),
            quarter,
            pltpu.VMEM((2, 2, 2, 2, half_rows, hidden), BF),
            pltpu.VMEM((2, 2, 2, 4, half_rows, hidden), BF),
            pltpu.VMEM(weights[1:], BF),
            DMA((3, 2, 4, 2)),
            DMA((3, 2, 4, 2)),
            DMA((3, 2, 4)),
            DMA((3, 2, 4)),
            DMA((2, 2, 2)),
            DMA((2, 2, 2)),
            DMA((2, 2, 2)),
            DMA((2, 2, 2)),
            DMA((7,)),
            DMA((4,)),
            DMA((3,)),
            DMA((3,)),
            DMA((4,)),
            DMA((4,)),
            DMA((4,)),
            DMA((4,)),
            DMA((3,)),
            DMA((3,)),
            DMA((4,)),
            DMA((4,)),
            DMA((3,)),
            DMA((3,)),
        ],
        compiler_params=pltpu.CompilerParams(
            collective_id=3, has_side_effects=True, vmem_limit_bytes=62 << 20
        ),
    )(part, tok, gain, dy, halves)


def rear_kernel(
    heads,
    lse, start_ref, cosines, sines, tok, gain, gnf, *more,
):
    far, outs, near_refs, rest_refs = more[:13], more[13:19], more[19:32], more[32:]
    a_all, norm_sum, bias_sum, ffn_all, out, grad = outs
    g, gate_sum, down_sum, ysum, dxl, attn, exact, q, kv, x1, ob, h1, dx1 = near_refs
    (
    ext_all, do, dots, acc, keep, give, arrived, sums, landed, back, part, m1, m2, m3, left_t, ga,
    own, passing, got, p2, q1, sm, q2, fin, fin_w, e0, e1, es, e2, y2,
    ls, d1, d2, d3, d4, ms, ca, cb, cc, cd, fs2, fr2, as1, ar1, as2, ar2, as3, ar3, xs, xr, ss, sr, ts, tr, ys, yr,
    gs, gr,
    ) = rest_refs
    me = Place()
    y, z, lo, k, t = me.y, me.z, me.lo, me.k, me.t
    c = lo * 2 + k
    index = z * 2 + lo
    rows, width = q.shape
    size = width // heads
    slice_rows, model = tok.shape
    rowed = width + size
    offsets = (2, 1, 3)

    def in_x(dt, dc):
        return {"ctx": lax.rem(c + dc, 4), "tp": lax.rem(t + dt, 2)}

    def owner(b):
        return {"fsdp": y * 4 + b // 2, "ctx": lax.rem(b, 2) * 2 + k}

    ring = [(dt, dc) for dt in (0, 1) for dc in range(4) if dt or dc]

    summed_once = (gate_sum, own, down_sum)

    def second_hop(w, half, j):
        if half == 0:
            source, device = summed_once[w].at[0, lax.rem(y + j, 4)], me.along_y(j)
        else:
            source, device = summed_once[w].at[1, lax.rem(z + j, 4)], me.along_z(j)
        return describe(
            source, p2.at[w, half, j - 1], fs2.at[w, half, j - 1], fr2.at[w, half, j - 1], device
        )

    def second_hops(w, half):
        for j in offsets:
            second_hop(w, half, j).start()

    def up_along_z(position, piece, count):
        return g.at[pl.ds(piece, count), position, 0]

    def up_along_y(position, piece, count):
        return g.at[position, pl.ds(piece, count), 1]

    up_rings = [
        RingSum(
            along,
            position,
            source,
            passing.at[half],
            got.at[half],
            [sem.at[half] for sem in (ca, cb, cc, cd)],
        )
        for half, (along, position, source) in enumerate(
            ((me.along_z, z, up_along_z), (me.along_y, y, up_along_y))
        )
    ]

    def up_end(half):
        own[half] = up_rings[half].finish().astype(BF)
        second_hops(1, half)

    def early():
        for one in up_rings:
            one.middle()

    loads = [
        pltpu.make_async_copy(source, target, ls.at[i])
        for i, (source, target) in enumerate(zip(far, near_refs, strict=True))
    ]
    for copy in loads:
        copy.start()
    greet(
        [me.along_z(j) for j in (1, 2, 3)]
        + [me.along_y(j) for j in (1, 2, 3)]
        + [in_x(dt, dc) for dt, dc in ring]
        + [{"fsdp": y * 4 + lax.rem(z + j, 4), "ctx": (1 - lo) * 2 + k} for j in (1, 2, 3)]
    )
    loads[0].wait()
    for one in up_rings:
        one.start()
    for copy in loads[1:4]:
        copy.wait()
    for half in (0, 1):
        second_hops(0, half)
        second_hops(2, half)
    near = [(1 - lo, t), (1 - lo, 1 - t), (lo, 1 - t)]
    results = [
        send(ysum.at[i + 1], y2.at[i], ys.at[i], yr.at[i], me.in_ring(*near[i])) for i in range(3)
    ]

    for copy in loads[4:9]:
        copy.wait()
    do[...] = plain(dxl[...], attn[:, rowed:]).astype(BF)
    for h in range(heads):
        product = exact[h] * do[:, h * size : (h + 1) * size].astype(F32).T
        dots[h : h + 1] = jnp.sum(product, axis=0, keepdims=True)
    acc[...] = jnp.zeros_like(acc)
    start = start_ref[...]
    first = index * rows

    def core_share(b):
        return describe(give.at[b], arrived.at[b], d1.at[b], d2.at[b], me.sibling)

    def home(b):
        return describe(sums.at[b], landed.at[index], d3.at[b], d4.at[index], owner(b))

    def step(b, _):
        keys = kv[0, b]
        values = kv[1, b]
        seen = visible_pairs(b, first, start, rows)
        dk = jnp.zeros((KEYS, size), F32)
        dv = jnp.zeros((KEYS, size), F32)
        for h in range(heads):
            q_h = q[:, h * size : (h + 1) * size]
            do_h = do[:, h * size : (h + 1) * size]
            s = jnp.where(seen, by_columns(keys, q_h), masked_score)
            p = jnp.exp(s - lse[h : h + 1])
            dv = dv + plain(p.astype(BF), do_h)
            dp = by_columns(values, do_h)
            ds = (p * (dp - dots[h : h + 1])).astype(BF)
            dk = dk + plain(ds, q_h)
            acc[h] = acc[h] + over_rows(keys, ds)
        keep[b] = jnp.where(k == 0, dk, dv)
        give[b] = jnp.where(k == 0, dv, dk)
        core_share(b).start()

        @pl.when(b > 0)
        def _():
            @pl.when(b == 2)
            def _():
                early()

            core_share(b - 1).wait_recv()
            sums[b - 1] = (keep[b - 1] + arrived[b - 1]).astype(BF)
            home(b - 1).start()

        return 0

    lax.fori_loop(0, index + 1, step, 0)

    @pl.when(index < 2)
    def _():
        early()


    for copy in loads[9:]:
        copy.wait()
    result = x1[...] + ysum[0].astype(F32)
    for i in range(3):
        results[i].wait()
        result = result + y2[i].astype(F32)
    out[t] = result.astype(BF)
    mine = out.at[t]
    rest = [send(mine, mine, gs.at[1], gr.at[1], me.in_ring(lo, 1 - t))]
    up_end(1)
    up_end(0)

    scale = 1.0 / math.sqrt(size)
    for h in range(heads):
        dq = turned(acc[h].T * scale, cosines[...], -sines[...])
        e0[2:3, h * size : (h + 1) * size] = jnp.sum(dq, axis=0, keepdims=True)
        back[:, h * size : (h + 1) * size] = dq.astype(BF)
    left_t[...] = dxl[...].T
    blocks = ga.shape[:4]

    def spread(value):
        return value.astype(BF).reshape(blocks + (value.shape[1],))

    ga[:, :, :, :, rowed:] = spread(plain(left_t[...], ob[...]))
    left_t[...] = h1[...].T
    ga[:, :, :, :, :width] = spread(plain(left_t[...], back[:, :width]))

    core_share(index).wait_recv()
    dkv = keep[index] + arrived[index]
    keep[index] = dkv
    for b in range(1, 8):

        @pl.when(b > index)
        def _():
            describe(sums.at[0], landed.at[b], d3.at[0], d4.at[b], owner(0)).wait_recv()
            keep[index] = keep[index] + landed[b].astype(F32)

    is_key = k == 0
    dkv = turned(
        keep[index], jnp.where(is_key, cosines[...], 1.0), jnp.where(is_key, -sines[...], 0.0)
    )
    e0[2:3, width:rowed] = jnp.sum(dkv, axis=0, keepdims=True)
    back[:, width:] = dkv.astype(BF)
    part[...] = (
        by_columns(back[...], attn[:, :rowed]).astype(BF).reshape(2, 2, slice_rows, model)
    )
    cores = send(part.at[1 - k], m1, ms.at[0], ms.at[1], me.sibling)
    ga[:, :, :, :, width:rowed] = spread(plain(left_t[...], back[:, width:]))

    large = []
    for j in offsets:
        large.append(
            send(
                ga.at[:, lax.rem(z + j, 4), 0], q1.at[0, j - 1], as1.at[0, j - 1], ar1.at[0, j - 1], me.along_z(j)
            )
        )
        large.append(
            send(
                ga.at[lax.rem(y + j, 4), :, 1], q1.at[1, j - 1], as1.at[1, j - 1], ar1.at[1, j - 1], me.along_y(j)
            )
        )

    cores.wait()
    m2[...] = (part[k, 1 - t].astype(F32) + m1[1 - t].astype(F32)).astype(BF)
    across = send(m2, m3, ms.at[2], ms.at[3], me.in_ring(lo, 1 - t))
    quarter = sm.shape[2] // 2

    def summed(w, half):
        for j in offsets:
            second_hop(w, half, j).wait()
        here = summed_once[w][0, y] if half == 0 else summed_once[w][1, z]
        total = here.astype(F32)
        for j in range(3):
            total = total + p2[w, half, j].astype(F32)
        return total

    def to_owners(w):
        for half in (0, 1):
            total = summed(w, half)
            fin_w[w, 2 * half] = total[:quarter]
            fin_w[w, 2 * half + 1] = total[quarter:]
        width = fin_w.shape[3]
        place = pl.ds(pl.multiple_of(c * width, 128), width)
        ffn_all[w, :, place] = fin_w[w, c]
        return [
            send(
                fin_w.at[w, lax.rem(c + j, 4)], ffn_all.at[w, :, place], ts.at[w, j - 1], tr.at[w, j - 1], in_x(0, j)
            )
            for j in (2, 1, 3)
        ]

    rest += to_owners(2) + to_owners(0) + to_owners(1)

    x = tok[...].astype(F32)
    factor = lax.rsqrt(jnp.mean(x * x, axis=-1, keepdims=True) + epsilon)
    normed = x * factor
    dh1 = part[k, t].astype(F32) + m1[t].astype(F32)
    across.wait()
    dh1 = dh1 + m3[...].astype(F32)
    e0[0:1] = jnp.sum(dh1 * normed, axis=0, keepdims=True)
    e0[1:2] = gnf[...]
    e0[2:3, rowed:] = jnp.zeros((1, model - rowed), F32)
    e0[3:] = jnp.zeros((5, model), F32)
    small = [
        send(e0, e1.at[j - 1], ss.at[0, j - 1], sr.at[0, j - 1], me.along_z(j)) for j in offsets
    ]
    grad[t] = (dx1[...] + norm_back(dh1 * gain[...], normed, factor)).astype(BF)
    mine = grad.at[t]
    rest.append(send(mine, mine, gs.at[0], gr.at[0], me.in_ring(lo, 1 - t)))

    for copy in large:
        copy.wait()
    for half in (0, 1):
        here = ga[:, z, 0] if half == 0 else ga[y, :, 1]
        total = here.astype(F32)
        for j in range(3):
            total = total + q1[half, j].astype(F32)
        sm[half] = total.astype(BF)
    last = []
    for j in offsets:
        last.append(
            send(
                sm.at[0, lax.rem(y + j, 4)], q2.at[0, j - 1], as2.at[0, j - 1], ar2.at[0, j - 1], me.along_y(j)
            )
        )
        last.append(
            send(
                sm.at[1, lax.rem(z + j, 4)], q2.at[1, j - 1], as2.at[1, j - 1], ar2.at[1, j - 1], me.along_z(j)
            )
        )
    for copy in small:
        copy.wait()
    es[...] = (e0[...] + e1[0]) + (e1[1] + e1[2])
    small = [
        send(es, e2.at[j - 1], ss.at[1, j - 1], sr.at[1, j - 1], me.along_y(j)) for j in offsets
    ]

    for copy in small:
        copy.wait()
    ext_all[t, c] = (es[...] + e2[0]) + (e2[1] + e2[2])
    mine = ext_all.at[t, c]
    rest += [
        send(mine, mine, xs.at[i], xr.at[i], in_x(dt, dc)) for i, (dt, dc) in enumerate(ring)
    ]
    for copy in last:
        copy.wait()
    for half in (0, 1):
        here = sm[0, y] if half == 0 else sm[1, z]
        total = here.astype(F32)
        for j in range(3):
            total = total + q2[half, j].astype(F32)
        fin[2 * half] = total[:quarter]
        fin[2 * half + 1] = total[quarter:]
    a_all[c] = fin[c]
    rest += [
        send(fin.at[lax.rem(c + j, 4)], a_all.at[c], as3.at[j - 1], ar3.at[j - 1], in_x(0, j))
        for j in (2, 1, 3)
    ]

    def sent(b, _):
        core_share(b).wait_send()

        @pl.when(b < index)
        def _():
            home(b).wait_send()

        return 0

    lax.fori_loop(0, index + 1, sent, 0)
    for copy in rest:
        copy.wait()
    total = ext_all[0, 0]
    for i in range(1, 8):
        total = total + ext_all[i // 4, i % 4]
    norm_sum[...] = total
    for core in (0, 1):
        bias_sum[core] = ext_all[t, core] + ext_all[t, 2 + core]


def rear(heads, g, gate_sum, down_sum, dxl, attn, q, kv, exact, lse, start, ob, h1, cosines, sines, ysum, x1, dx1, tok, gain, gnf):
    rows, width = q.shape
    size = width // heads
    slice_rows, model = tok.shape
    hidden = g.shape[-1]
    total = attn.shape[1]
    half_rows = model // 32
    quarter = half_rows // 2
    shared = pltpu.VMEM(kv.shape[1:], F32)
    shared_low = pltpu.VMEM(kv.shape[1:], BF)
    slab = pltpu.VMEM((slice_rows, model), BF)
    args = (lse, start, cosines, sines, tok, gain, gnf)
    far = (g, gate_sum, down_sum, ysum, dxl, attn, exact, q, kv, x1, ob, h1, dx1)
    outs = [
        shape((4, quarter, total), F32),
        shape((8, model), F32),
        shape((2, 8, model), F32),
        shape((3, quarter, 4 * hidden), F32),
        shape((2, slice_rows, model), BF),
        shape((2, slice_rows, model), BF),
    ]
    return pl.pallas_call(
        functools.partial(rear_kernel, heads),
        out_shape=outs,
        in_specs=[VM] * len(args) + [pl.BlockSpec(memory_space=pl.ANY)] * len(far),
        out_specs=[VM] * len(outs),
        scratch_shapes=[pltpu.VMEM(array.shape, array.dtype) for array in far]
        + [
            pltpu.VMEM((2, 4, 8, model), F32),
            pltpu.VMEM((rows, width), BF),
            pltpu.VMEM((8, rows), F32),
            pltpu.VMEM((heads, size, rows), F32),
            shared,
            shared,
            shared,
            shared_low,
            shared_low,
            pltpu.VMEM((rows, width + size), BF),
            pltpu.VMEM((2, 2, slice_rows, model), BF),
            pltpu.VMEM((2, slice_rows, model), BF),
            slab,
            slab,
            pltpu.VMEM((model, rows), BF),
            pltpu.VMEM((4, 4, 2, half_rows, total), BF),
            pltpu.VMEM((2, 4, half_rows, hidden), BF),
            pltpu.VMEM((2, 2, 2, half_rows, hidden), BF),
            pltpu.VMEM((2, 2, 4, half_rows, hidden), BF),
            pltpu.VMEM((3, 2, 3, half_rows, hidden), BF),
            pltpu.VMEM((2, 3, 4, half_rows, total), BF),
            pltpu.VMEM((2, 4, half_rows, total), BF),
            pltpu.VMEM((2, 3, half_rows, total), BF),
            pltpu.VMEM((4, quarter, total), F32),
            pltpu.VMEM((3, 4, quarter, hidden), F32),
            pltpu.VMEM((8, model), F32),
            pltpu.VMEM((3, 8, model), F32),
            pltpu.VMEM((8, model), F32),
            pltpu.VMEM((3, 8, model), F32),
            pltpu.VMEM((3, slice_rows, model), BF),
            DMA((13,)),
            DMA((8,)),
            DMA((8,)),
            DMA((8,)),
            DMA((8,)),
            DMA((4,)),
            DMA((2, 2)),
            DMA((2, 2)),
            DMA((2, 2)),
            DMA((2, 2)),
            DMA((3, 2, 3)),
            DMA((3, 2, 3)),
            DMA((2, 3)),
            DMA((2, 3)),
            DMA((2, 3)),
            DMA((2, 3)),
            DMA((3,)),
            DMA((3,)),
            DMA((7,)),
            DMA((7,)),
            DMA((2, 3)),
            DMA((2, 3)),
            DMA((3, 3)),
            DMA((3, 3)),
            DMA((3,)),
            DMA((3,)),
            DMA((2,)),
            DMA((2,)),
        ],
        compiler_params=pltpu.CompilerParams(
            collective_id=7, has_side_effects=True, vmem_limit_bytes=62 << 20
        ),
    )(*args, *far)


def shards(
    tokens,
    segments,
    w_query,
    key_matrix,
    value_matrix,
    b_query,
    key_bias_vector,
    value_bias_vector,
    w_out,
    norm_attn,
    norm_ffn,
    w_gate,
    w_up,
    w_down,
    cotangent,
):
    f = lax.axis_index("fsdp")
    c = lax.axis_index("ctx")
    t = lax.axis_index("tp")
    k = c % 2
    is_key = k == 0
    size = key_matrix.shape[1]
    query_width = w_query.shape[1] // 2
    heads = query_width // size
    own_width = query_width + size
    model = tokens.shape[1]
    count = tokens.shape[0]
    slice_rows = count // 2
    shard_rows = w_query.shape[0]
    hidden = w_gate.shape[1] // 4
    padded = -(-hidden // 128) * 128

    def hidden_slice(w, axis):
        widths = [(0, 0), (0, 0)]
        widths[axis] = (0, 4 * padded - 4 * hidden)
        return lax.dynamic_slice_in_dim(jnp.pad(w, widths), c * padded, padded, axis)

    own_ffn = jnp.stack(
        [
            hidden_slice(w_gate, 1),
            hidden_slice(w_up, 1),
            hidden_slice(w_down, 0).T,
        ]
    )

    own_attn = jnp.concatenate(
        [
            lax.dynamic_slice_in_dim(w_query, k * query_width, query_width, 1),
            jnp.where(is_key, key_matrix, value_matrix),
            lax.dynamic_slice_in_dim(w_out, k * query_width, query_width, 0).T,
        ],
        axis=1,
    )
    own_tokens = lax.dynamic_slice_in_dim(tokens, t * slice_rows, slice_rows, 0)
    rows = 2 * count
    half_size = size // 2
    frequency = np.exp(np.arange(half_size) * (-2.0 * math.log(rope_base) / size))
    frequency = jnp.asarray(np.concatenate([frequency, frequency])[None].astype(np.float32))
    gain_attn = norm_attn.astype(F32)[None]
    gain_ffn = norm_ffn.astype(F32)[None]
    bias = jnp.concatenate(
        [
            lax.dynamic_slice_in_dim(b_query, k * query_width, query_width, 0),
            jnp.where(is_key, key_bias_vector, value_bias_vector),
        ]
    ).astype(F32)[None]
    (
        attn_all,
        halves,
        dy_all,
        h1,
        q,
        kv,
        exact,
        ob,
        lse,
        starts,
        cosines,
        sines,
        part,
    ) = front(heads, own_attn, own_ffn, tokens, cotangent, segments, gain_attn, bias, frequency)
    x1, dx1, dxl, grad_norm_two, ysum, gate_sum, down_sum, up_grad = block(
        part, own_tokens, gain_ffn, dy_all, halves
    )
    a_all, norm_sum, bias_sum, ffn_all, output, grad_tokens = rear(
        heads,
        up_grad,
        gate_sum,
        down_sum,
        dxl.reshape(rows, model),
        attn_all.reshape(model, own_width + query_width),
        q,
        kv,
        exact,
        lse,
        starts,
        ob,
        h1,
        cosines,
        sines,
        ysum,
        x1,
        dx1,
        own_tokens,
        gain_attn,
        grad_norm_two,
    )
    owner_rows = shard_rows // 4
    a_all = a_all[:2] + a_all[2:]

    owner = f * 4 + c
    norms = lax.dynamic_slice_in_dim(norm_sum[:2], owner * owner_rows, owner_rows, 1)
    biases = bias_sum[:, 2, :own_width].reshape(2, heads + 1, size)
    biases = lax.dynamic_slice_in_dim(biases, owner * 2, 2, 2)
    return (
        output.reshape(count, model),
        grad_tokens.reshape(count, model).astype(F32),
        jnp.concatenate([a_all[0, :, :query_width], a_all[1, :, :query_width]], axis=1),
        a_all[0, :, query_width:own_width],
        a_all[1, :, query_width:own_width],
        biases[:, :heads].reshape(2 * heads, 2),
        biases[0, heads:],
        biases[1, heads:],
        jnp.concatenate([a_all[0, :, own_width:], a_all[1, :, own_width:]], axis=1).T,
        norms[0],
        norms[1],
        ffn_all[0, :, : 4 * hidden],
        ffn_all[1, :, : 4 * hidden],
        ffn_all[2, :, : 4 * hidden].T,
    )


def solution(mesh):
    both = ("fsdp", "ctx")
    in_specs = (
        P(both, None),
        P(),
        P("fsdp", "tp"),
        P("fsdp", "tp"),
        P("fsdp", "tp"),
        P("tp"),
        P("tp"),
        P("tp"),
        P("tp", "fsdp"),
        P(),
        P(),
        P("fsdp", "tp"),
        P("fsdp", "tp"),
        P("tp", "fsdp"),
        P(both, None),
    )
    out_specs = (
        P(both, None),
        P(both, None),
        P(both, "tp"),
        P(both, "tp"),
        P(both, "tp"),
        P("tp", both),
        P("tp", both),
        P("tp", both),
        P("tp", both),
        P(both),
        P(both),
        P(both, "tp"),
        P(both, "tp"),
        P("tp", both),
    )
    return jax.shard_map(shards, mesh=mesh, in_specs=in_specs, out_specs=out_specs, check_vma=False)
```

```python
import functools
import math

import jax
import jax.numpy as jnp
import numpy as np
from jax import lax
from jax.experimental import pallas as pl
from jax.experimental.pallas import tpu as pltpu
from jax.sharding import PartitionSpec as P

MESH = pl.DeviceIdType.MESH
VM = pl.BlockSpec(memory_space=pltpu.VMEM)
DMA = pltpu.SemaphoreType.DMA
BF = jnp.bfloat16
F32 = jnp.float32

epsilon = 1e-06
rope_base = 1000000.0
masked_score = -1e30
KEYS = 512


class Place:
    def __init__(self):
        f = lax.axis_index("fsdp")
        c = lax.axis_index("ctx")
        self.y, self.z = f // 4, f % 4
        self.lo, self.k = c // 2, c % 2
        self.t = lax.axis_index("tp")

    def along_y(self, j):
        return {"fsdp": lax.rem(self.y + j, 4) * 4 + self.z}

    def along_z(self, j):
        return {"fsdp": self.y * 4 + lax.rem(self.z + j, 4)}

    @property
    def sibling(self):
        return {"ctx": self.lo * 2 + 1 - self.k}

    def in_ring(self, lo, t):
        return {"ctx": lo * 2 + self.k, "tp": t}

    @property
    def others(self):
        return [(self.lo, 1 - self.t), (1 - self.lo, self.t), (1 - self.lo, 1 - self.t)]


def greet(devices):
    barrier = pltpu.get_barrier_semaphore()
    for device in devices:
        pl.semaphore_signal(barrier, inc=1, device_id=device, device_id_type=MESH)
    pl.semaphore_wait(barrier, len(devices))


def describe(source, target, send_sem, recv_sem, device):
    return pltpu.make_async_remote_copy(
        src_ref=source,
        dst_ref=target,
        send_sem=send_sem,
        recv_sem=recv_sem,
        device_id=device,
        device_id_type=MESH,
    )


def send(source, target, send_sem, recv_sem, device):
    copy = describe(source, target, send_sem, recv_sem, device)
    copy.start()
    return copy


def comm_call(body, outs, scratch, collective_id, mib, *args):
    return pl.pallas_call(
        body,
        out_shape=outs,
        in_specs=[VM] * len(args),
        out_specs=[VM] * len(outs),
        scratch_shapes=scratch,
        compiler_params=pltpu.CompilerParams(
            collective_id=collective_id, has_side_effects=True, vmem_limit_bytes=mib << 20
        ),
    )(*args)


def shape(dims, kind):
    return jax.ShapeDtypeStruct(dims, kind)


def over_rows(a, b):
    return lax.dot_general(a, b, (((0,), (0,)), ((), ())), preferred_element_type=F32)


def by_columns(a, b):
    return lax.dot_general(a, b, (((1,), (1,)), ((), ())), preferred_element_type=F32)


def plain(a, b):
    return lax.dot_general(a, b, (((1,), (0,)), ((), ())), preferred_element_type=F32)


def visible_pairs(block, first, start, rows):
    key = block * KEYS + lax.broadcasted_iota(jnp.int32, (KEYS, rows), 0)
    row = first + lax.broadcasted_iota(jnp.int32, (1, rows), 1)
    return (key >= start) & (key <= row)


class RingGather:
    def __init__(self, along, position, pieces, target, source, sems):
        self.along, self.position, self.pieces = along, position, pieces
        self.target, self.source, self.sems = target, source, sems

    def hop(self, i, way):
        s, r = self.sems[:2]
        return describe(
            self.source(i),
            self.target(self.position, i),
            s.at[i, way],
            r.at[i, way],
            self.along(1 if way == 0 else 3),
        )

    def onward(self, i):
        s, r = self.sems[2:]
        way = i // 2
        block = self.target(lax.rem(self.position + (3 if way == 0 else 1), 4), i)
        return describe(block, block, s.at[i], r.at[i], self.along(1 if way == 0 else 3))

    def start(self, i):
        self.hop(i, 0).start()
        self.hop(i, 1).start()

    def forward(self, i):
        self.hop(i, i // 2).wait_recv()
        self.onward(i).start()

    def finish(self):
        for i in range(4):
            self.hop(i, 1 - i // 2).wait_recv()
            self.onward(i).wait()
            self.hop(i, 0).wait_send()
            self.hop(i, 1).wait_send()


class RingSum:
    def __init__(self, along, position, source, passing, got, sems):
        self.along, self.position, self.source = along, position, source
        self.passing, self.got, self.sems = passing, got, sems

    def at(self, offset):
        return lax.rem(self.position + offset, 4)

    def first(self, way):
        s, r = self.sems[:2]
        return describe(
            self.source(self.at(2), 2 * way, 2),
            self.passing.at[way],
            s.at[way],
            r.at[way],
            self.along(1 if way == 0 else 3),
        )

    def second(self, way):
        s, r = self.sems[2:]
        offset = 1 if way == 0 else 3
        return describe(
            self.source(self.at(offset), 0, 4), self.got.at[way], s.at[way], r.at[way], self.along(offset)
        )

    def start(self):
        for way in (0, 1):
            self.first(way).start()

    def middle(self):
        for way in (0, 1):
            self.first(way).wait()
            near = self.source(self.at(1 if way == 0 else 3), 2 * way, 2)
            near[...] = (near[...].astype(F32) + self.passing[way].astype(F32)).astype(BF)
            self.second(way).start()

    def finish(self):
        total = self.source(self.position, 0, 4)[...].astype(F32)
        for way in (0, 1):
            self.second(way).wait()
            total = total + self.got[way].astype(F32)
        return total


def turned(values, cosines, sines):
    return values * cosines - pltpu.roll(values, values.shape[-1] // 2, 1) * sines


def front_kernel(
    heads,
    w, ffn, tok, dy, segments, gain, bias, frequency,
    w_out, halves, dy_all, h1_out, q, kv_out, exact, ob, lse, starts, cosines, sines, part,
    w_all, h1, kv, tok2, top, total, acc,
    s1, r1, wa, wb, wc, wd, s3, r3, ts, tr, ds, dr, fs, fr, ks, kr, cs, cr, ls, os,
):
    me = Place()
    y, z, lo, k, t = me.y, me.z, me.lo, me.k, me.t
    index = z * 2 + lo
    count, model = tok.shape
    rows = 2 * count
    width, size = q.shape[1], exact.shape[1]
    rowed = width + size
    shard = w.shape[0] // 2
    parts = (pl.ds(0, shard), pl.ds(shard, shard))
    near = [me.in_ring(1 - lo, t), me.in_ring(1 - lo, 1 - t)]
    offsets = (1, 3, 2)
    greet(
        [me.along_z(j) for j in (1, 2, 3)]
        + [me.along_y(j) for j in (1, 2, 3)]
        + [me.sibling]
        + near
        + [{"fsdp": y * 4 + lax.rem(z + j, 4), "ctx": (1 - lo) * 2 + k} for j in (1, 2, 3)]
    )

    def attn_place(half, position, i):
        if half == 0:
            return w_all.at[position, lax.rem(z + 4 - i, 4), parts[0]]
        return w_all.at[lax.rem(y + 4 - i, 4), position, parts[1]]

    def attn_source(half, i):
        if i == 0:
            return w.at[parts[half]]
        return attn_place(half, y if half == 0 else z, i)

    def first_hop(half, j):
        along = me.along_z if half == 0 else me.along_y
        return describe(
            w.at[parts[half]],
            w_all.at[y, z, parts[half]],
            s1.at[half, j - 1],
            r1.at[half, j - 1],
            along(j),
        )

    rings = [
        RingGather(
            me.along_y if half == 0 else me.along_z,
            y if half == 0 else z,
            4,
            functools.partial(attn_place, half),
            functools.partial(attn_source, half),
            [sem.at[half] for sem in (wa, wb, wc, wd)],
        )
        for half in (0, 1)
    ]
    for j in offsets:
        for half in (0, 1):
            first_hop(half, j).start()
    for ring in rings:
        ring.start(0)
    tokens_share = send(tok, tok2, ts, tr, me.sibling)
    slab = count // 2
    near_copies = [
        send(dy.at[pl.ds(t * slab, slab)], dy_all.at[lo, t, k], ds.at[i], dr.at[i], near[i])
        for i in (0, 1)
    ]
    rest = [
        send(dy.at[pl.ds(h * slab, slab)], dy_all.at[lo, h, k], fs.at[2 + h], fr.at[2 + h], me.sibling)
        for h in (0, 1)
    ]
    w_all[y, z] = w[...]
    stores = [
        pltpu.make_async_copy(dy.at[pl.ds(h * slab, slab)], dy_all.at[lo, h, k], os.at[h])
        for h in (0, 1)
    ]
    for copy in stores:
        copy.start()

    first = pl.multiple_of(index * rows, rows)
    everyone = segments[pl.ds(y, 1), :]
    mine = segments[pl.ds(y, 1), pl.ds(first, rows)]
    start = jnp.zeros((1, rows), jnp.int32)
    for number in (1, 2, 3):
        begin = jnp.sum(jnp.where(everyone < number, 1.0, 0.0), axis=1, keepdims=True)
        start = jnp.where(mine == number, begin.astype(jnp.int32), start)
    starts[...] = start
    row = first + lax.broadcasted_iota(jnp.int32, (1, rows), 1)
    pos = jnp.broadcast_to((row - start).astype(F32), (8, rows)).T[:, :1]
    angles = pos * frequency[...]
    lane = lax.broadcasted_iota(jnp.int32, (1, size), 1)
    cosines[...] = jnp.cos(angles)
    sines[...] = jnp.sin(angles) * jnp.where(lane < size // 2, 1.0, -1.0)

    for j in offsets:
        for half in (0, 1):
            first_hop(half, j).wait()
            rings[half].start(j)

    def normed(x):
        x = x.astype(F32)
        factor = lax.rsqrt(jnp.mean(x * x, axis=-1, keepdims=True) + epsilon)
        return (x * factor * gain[...]).astype(BF)

    h1[pl.ds(pl.multiple_of(k * count, count), count)] = normed(tok[...])
    tokens_share.wait()
    h1[pl.ds(pl.multiple_of((1 - k) * count, count), count)] = normed(tok2[...])

    for i in (0, 1, 3, 2):
        for ring in rings:
            ring.forward(i)

    def ffn_hop(i, half, j):
        along, here = (me.along_z, z) if half == 0 else (me.along_y, y)
        return describe(
            ffn.at[i, parts[half]],
            halves.at[i, half, here],
            s3.at[i, half, j - 1],
            r3.at[i, half, j - 1],
            along(j),
        )

    def ffn_hops(i):
        for half in (0, 1):
            for j in offsets:
                ffn_hop(i, half, j).start()
            there = halves.at[i, half, z if half == 0 else y]
            copy = pltpu.make_async_copy(ffn.at[i, parts[half]], there, ls.at[i, half])
            copy.start()
            stores.append(copy)

    ffn_hops(0)
    for ring in rings:
        ring.finish()
    for i, (source, there) in enumerate(((w_all, w_out), (h1, h1_out))):
        copy = pltpu.make_async_copy(source, there, os.at[2 + i])
        copy.start()
        stores.append(copy)

    inward = w_all[:, :, :, :rowed].reshape(model, rowed)
    linear = plain(h1[...], inward) + bias[...]
    scale = 1.0 / math.sqrt(size)
    is_key = k == 0
    own = turned(
        linear[:, width:],
        jnp.where(is_key, cosines[...], 1.0),
        jnp.where(is_key, sines[...], 0.0),
    )
    kv[k, index] = own.astype(BF)
    own_keys = kv.at[k, index]

    def keys_copy(i, device):
        return describe(own_keys, own_keys, ks.at[i], kr.at[index], device)

    targets = [(dz, to) for dz in (1, 2, 3) for to in (0, 1)]

    def target(dz, to):
        return {"fsdp": y * 4 + lax.rem(z + dz, 4), "ctx": to * 2 + k}

    for i, (dz, to) in enumerate(targets):

        @pl.when(z + dz < 4)
        def _():
            keys_copy(i, target(dz, to)).start()

    @pl.when(lo == 0)
    def _():
        keys_copy(6, {"ctx": 2 + k}).start()

    def keys_share(b):
        there = kv.at[k, b]
        return describe(there, there, cs.at[b], cr.at[b], me.sibling)

    keys_share(index).start()
    for h in range(heads):
        here = slice(h * size, (h + 1) * size)
        q[:, here] = (turned(linear[:, here], cosines[...], sines[...]) * scale).astype(BF)

    ffn_hops(1)
    ffn_hops(2)
    for i, half in ((0, t), (1, 1 - t)):
        near_copies[i].wait()
        there = dy_all.at[1 - lo, half, k]
        rest.append(send(there, there, fs.at[i], fr.at[i], me.sibling))

    top[...] = jnp.full_like(top, masked_score)
    total[...] = jnp.zeros_like(total)
    acc[...] = jnp.zeros_like(acc)

    def step(i, _):
        b = index - i

        @pl.when(b > 0)
        def _():
            there = kv.at[k, b - 1]
            describe(there, there, ks.at[0], kr.at[b - 1], me.sibling).wait_recv()
            keys_share(b - 1).start()

        keys_share(b).wait_recv()
        keys = kv[0, b]
        values = kv[1, b]
        seen = visible_pairs(b, first, start, rows)
        for h in range(heads):
            s = by_columns(keys, q[:, h * size : (h + 1) * size])
            s = jnp.where(seen, s, masked_score)
            before = top[h : h + 1]
            now = jnp.maximum(before, jnp.max(s, axis=0, keepdims=True))
            p = jnp.exp(s - now)
            shrink = jnp.exp(before - now)
            top[h : h + 1] = now
            total[h : h + 1] = total[h : h + 1] * shrink + jnp.sum(p, axis=0, keepdims=True)
            acc[h] = acc[h] * shrink + over_rows(values, p.astype(BF))
        return 0

    lax.fori_loop(0, index + 1, step, 0)
    copy = pltpu.make_async_copy(kv, kv_out, os.at[4])
    copy.start()
    stores.append(copy)
    lse[...] = jnp.zeros_like(lse)
    for h in range(heads):
        sums = total[h : h + 1]
        lse[h : h + 1] = top[h : h + 1] + jnp.log(sums)
        out = acc[h] / sums
        exact[h] = out
        ob[:, h * size : (h + 1) * size] = out.T.astype(BF)
    outward = w_all[:, :, :, rowed:].reshape(model, width)
    part[...] = by_columns(ob[...], outward).astype(BF).reshape(part.shape)

    for i, (dz, to) in enumerate(targets):

        @pl.when(z + dz < 4)
        def _():
            keys_copy(i, target(dz, to)).wait_send()

    @pl.when(lo == 0)
    def _():
        keys_copy(6, {"ctx": 2 + k}).wait_send()

    def shared(b, _):
        keys_share(b).wait_send()
        return 0

    lax.fori_loop(0, index + 1, shared, 0)
    for i in range(3):
        for half in (0, 1):
            for j in offsets:
                ffn_hop(i, half, j).wait()
    for copy in rest + stores:
        copy.wait()


def front(heads, w, ffn, tok, dy, segments, gain, bias, frequency):
    shard, total = w.shape
    hidden = ffn.shape[2]
    count, model = tok.shape
    rows = 2 * count
    width = bias.shape[1] - frequency.shape[1]
    size = frequency.shape[1]
    far = pl.BlockSpec(memory_space=pl.ANY)
    args = (w, ffn, tok, dy, segments, gain, bias, frequency)
    outs = [
        shape((4, 4, shard, total), BF),
        shape((3, 2, 4, shard // 2, hidden), BF),
        shape((2, 2, 2, count // 2, model), BF),
        shape((rows, model), BF),
        shape((rows, width), BF),
        shape((2, 8, rows, size), BF),
        shape((heads, size, rows), F32),
        shape((rows, width), BF),
        shape((8, rows), F32),
        shape((1, rows), jnp.int32),
        shape((rows, size), F32),
        shape((rows, size), F32),
        shape((2, 2, count // 2, model), BF),
    ]
    return pl.pallas_call(
        functools.partial(front_kernel, heads),
        out_shape=outs,
        in_specs=[VM] * len(args),
        out_specs=[far] * 4 + [VM, far] + [VM] * (len(outs) - 6),
        scratch_shapes=[
            pltpu.VMEM((4, 4, shard, total), BF),
            pltpu.VMEM((rows, model), BF),
            pltpu.VMEM((2, 8, rows, size), BF),
            pltpu.VMEM((count, model), BF),
            pltpu.VMEM((8, rows), F32),
            pltpu.VMEM((8, rows), F32),
            pltpu.VMEM((heads, size, rows), F32),
            DMA((2, 3)),
            DMA((2, 3)),
            DMA((2, 4, 2)),
            DMA((2, 4, 2)),
            DMA((2, 4)),
            DMA((2, 4)),
            DMA((3, 2, 3)),
            DMA((3, 2, 3)),
            DMA,
            DMA,
            DMA((2,)),
            DMA((2,)),
            DMA((4,)),
            DMA((4,)),
            DMA((7,)),
            DMA((8,)),
            DMA((8,)),
            DMA((8,)),
            DMA((3, 2)),
            DMA((5,)),
        ],
        compiler_params=pltpu.CompilerParams(
            collective_id=1, has_side_effects=True, vmem_limit_bytes=56 << 20
        ),
    )(*args)


def norm_back(grad_normed, normed, factor):
    return factor * (grad_normed - normed * jnp.mean(grad_normed * normed, axis=-1, keepdims=True))


def block_kernel(
    part, tok, gain, dy_hbm, halves,
    x1, dx1, dxl, gnf, ysum, gate_sum, down_sum, up_grad,
    w, dy, dy_t, h2, h2_t, hid, gate_back, up_back, whole, pb, s1, r1, r2, ry, passing, got, gx,
    ba, bb, bc, bd, ca, cb, cc, cd, ls, ms, hs, hr, fs, fr, ps, pr, xs, xr, ys, yr, gs, gr,
):
    me = Place()
    y, z, lo, k, t = me.y, me.z, me.lo, me.k, me.t
    rows, model = tok.shape
    both = 2 * rows
    inner = w.shape[-1]
    offsets = (2, 1, 3)

    def chip(i):
        return lax.rem(lo + lax.rem((i + 1) // 2, 2), 2), lax.rem(t + i // 2, 2)

    def columns(i):
        return pl.ds(pl.multiple_of(i * both, both), both)

    loads = [pltpu.make_async_copy(dy_hbm, dy, ls.at[6])]
    for i in range(3):
        loads.append(pltpu.make_async_copy(halves.at[i, 0], w.at[i, y, :, 0], ls.at[2 * i]))
        loads.append(pltpu.make_async_copy(halves.at[i, 1], w.at[i, :, z, 1], ls.at[2 * i + 1]))
    for copy in loads:
        copy.start()
    greet(
        [me.in_ring(*chip(i)) for i in (1, 2, 3)]
        + [me.sibling]
        + [me.along_z(j) for j in (1, 2, 3)]
        + [me.along_y(j) for j in (1, 2, 3)]
    )
    m1, m2, m3 = r1.at[pl.ds(0, 2)], s1.at[0], r2.at[2]
    cores = send(part.at[1 - k], m1, ms.at[0], ms.at[1], me.sibling)

    def weight_place(i, half, position, piece):
        if half == 0:
            return w.at[i, position, lax.rem(z + 4 - piece, 4), 0]
        return w.at[i, lax.rem(y + 4 - piece, 4), position, 1]

    def weight_source(i, half, piece):
        return halves.at[i, half, lax.rem((z if half == 0 else y) + 4 - piece, 4)]

    rings = [
        [
            RingGather(
                me.along_y if half == 0 else me.along_z,
                y if half == 0 else z,
                4,
                functools.partial(weight_place, i, half),
                functools.partial(weight_source, i, half),
                [sem.at[i, half] for sem in (ba, bb, bc, bd)],
            )
            for half in (0, 1)
        ]
        for i in range(3)
    ]

    def gather_start(i):
        for ring in rings[i]:
            for piece in range(4):
                ring.start(piece)

    def gather_forward(i):
        for ring in rings[i]:
            for piece in range(4):
                ring.forward(piece)

    def gather_finish(i):
        for ring in rings[i]:
            ring.finish()
        for copy in loads[2 * i + 1 : 2 * i + 3]:
            copy.wait()

    def weight(i):
        return w[i].reshape(model, inner)

    gather_start(0)
    gather_start(1)
    loads[0].wait()

    def turn_dy(i, _):
        lo_i, t_i = chip(i)
        dy_t[:, columns(i)] = dy[lo_i, t_i].reshape(both, model).T
        return 0

    cores.wait()
    m2[...] = (part[k, 1 - t].astype(F32) + m1[1 - t].astype(F32)).astype(BF)
    across = send(m2, m3, ms.at[2], ms.at[3], me.in_ring(lo, 1 - t))
    lax.fori_loop(0, 4, turn_dy, 0)
    x = tok[...].astype(F32) + part[k, t].astype(F32) + m1[t].astype(F32)
    gather_forward(0)
    across.wait()
    x = x + m3[...].astype(F32)
    x1[...] = x
    factor = lax.rsqrt(jnp.mean(x * x, axis=-1, keepdims=True) + epsilon)
    h2[lo, t, k] = (x * factor * gain[...]).astype(BF)

    def hidden_copy(i):
        block = h2.at[lo, t, k]
        return describe(block, block, hs.at[i - 1], hr.at[i - 1], me.in_ring(*chip(i)))

    def hidden_share(i):
        lo_i, t_i = chip(i)
        block = h2.at[lo_i, t_i, k]
        return describe(block, block, fs.at[i], fr.at[i], me.sibling)

    def part_share(i):
        return describe(pb.at[i], r1.at[i], ps.at[i], pr.at[i], me.sibling)

    def part_copy(i):
        return describe(
            s1.at[i], r2.at[i - 1], xs.at[i - 1], xr.at[i - 1], me.in_ring(*chip(i))
        )

    def result_share(i):
        return describe(pb.at[i], ry.at[i], ys.at[i], yr.at[i], me.sibling)

    for i in (1, 2, 3):
        hidden_copy(i).start()
    hidden_share(0).start()
    gather_forward(1)
    gather_start(2)

    def inward(i, _):
        lo_i, t_i = chip(i)
        hidden_share(i).wait_recv()

        @pl.when(i == 0)
        def _():
            gather_finish(0)

        h = h2[lo_i, t_i].reshape(both, model)
        gate = plain(h, weight(0))
        h2_t[:, columns(i)] = h.T

        @pl.when(i == 0)
        def _():
            gather_finish(1)

        up = plain(h, weight(1))
        sigmoid_gate = jax.nn.sigmoid(gate)
        silu_gate = gate * sigmoid_gate
        hid[i] = (silu_gate * up).astype(BF)
        slope = sigmoid_gate * (1.0 + gate * (1.0 - sigmoid_gate))
        gate_back[i] = (up * slope).astype(BF)
        up_back[i] = silu_gate.astype(BF)

        @pl.when(i < 3)
        def _():
            hidden_copy(i + 1).wait_recv()
            hidden_share(i + 1).start()

        return 0

    def gradient(target, left_t, right):
        flat = right.shape[0] * right.shape[1]
        step_rows = model // 4

        def some(m, _):
            r = pl.ds(pl.multiple_of(m * step_rows, step_rows), step_rows)
            value = plain(left_t[r, :], right[...].reshape(flat, inner))
            target[m] = value.astype(BF).reshape(target.shape[1:])
            return 0

        lax.fori_loop(0, 4, some, 0)

    def ring_sums(n, target):
        def along_z(position, piece, count):
            return target.at[pl.ds(piece, count), position, 0]

        def along_y(position, piece, count):
            return target.at[position, pl.ds(piece, count), 1]

        return [
            RingSum(
                along,
                position,
                source,
                passing.at[n, half],
                got.at[n, half],
                [sem.at[n, half] for sem in (ca, cb, cc, cd)],
            )
            for half, (along, position, source) in enumerate(
                ((me.along_z, z, along_z), (me.along_y, y, along_y))
            )
        ]

    lax.fori_loop(0, 4, inward, 0)
    gather_forward(2)
    down_rings, gate_rings = ring_sums(0, gx), ring_sums(1, w.at[0])
    gradient(gx, dy_t, hid)
    for one in down_rings:
        one.start()
    gather_finish(2)

    def homeward(i):
        part_share(i).wait_recv()
        s1[i] = (s1[i].astype(F32) + r1[i].astype(F32)).astype(BF)

        @pl.when(i > 0)
        def _():
            part_copy(i).start()

    def outward(n, _):
        i = lax.rem(n + 1, 4)
        lo_i, t_i = chip(i)
        grad_inner = plain(dy[lo_i, t_i].reshape(both, model), weight(2))

        @pl.when(n > 0)
        def _():
            homeward(n)

        @pl.when(n == 2)
        def _():
            for one in down_rings:
                one.middle()

        gate_back[i] = (grad_inner * gate_back[i].astype(F32)).astype(BF)
        up_back[i] = (grad_inner * up_back[i].astype(F32)).astype(BF)
        whole[...] = (
            by_columns(gate_back[i], weight(0)) + by_columns(up_back[i], weight(1))
        ).reshape(2, rows, model)
        pb[i] = whole[1 - k].astype(BF)
        s1[i] = whole[k].astype(BF)
        part_share(i).start()
        return 0

    lax.fori_loop(0, 4, outward, 0)
    gradient(w.at[0], h2_t, gate_back)
    for one in gate_rings:
        one.start()

    homeward(0)

    grad = s1[0].astype(F32)
    for i in (1, 2, 3):
        part_copy(i).wait_recv()
        grad = grad + r2[i - 1].astype(F32)
    x = x1[...]
    factor = lax.rsqrt(jnp.mean(x * x, axis=-1, keepdims=True) + epsilon)
    normed = x * factor
    gnf[...] = jnp.sum(grad * normed, axis=0, keepdims=True)
    back = dy[lo, t, k].astype(F32) + norm_back(grad * gain[...], normed, factor)
    dx1[...] = back
    dxl[k, t] = back.astype(BF)
    block = dxl.at[k, t]
    across = send(block, block, gs.at[0], gr.at[0], me.in_ring(lo, 1 - t))
    rest = [send(block, block, gs.at[1], gr.at[1], me.sibling)]
    for one in gate_rings:
        one.middle()

    def result(i, _):
        whole[...] = by_columns(hid[i], weight(2)).reshape(2, rows, model)
        part_share(i).wait_send()
        pb[i] = whole[1 - k].astype(BF)
        ysum[i] = whole[k].astype(BF)
        result_share(i).start()
        return 0

    lax.fori_loop(0, 4, result, 0)

    gradient(w.at[1], h2_t, up_back)
    last = pltpu.make_async_copy(w.at[1], up_grad, ls.at[0])
    last.start()
    rest.append(last)
    across.wait()
    block = dxl.at[k, 1 - t]
    rest.append(send(block, block, gs.at[2], gr.at[2], me.sibling))
    for i in range(4):
        result_share(i).wait()
        ysum[i] = (ysum[i].astype(F32) + ry[i].astype(F32)).astype(BF)
        hidden_share(i).wait_send()
    for i in (1, 2, 3):
        hidden_copy(i).wait_send()
        part_copy(i).wait_send()
    for half in (0, 1):
        down_sum[half] = down_rings[half].finish().astype(BF)
    for half in (0, 1):
        gate_sum[half] = gate_rings[half].finish().astype(BF)
    for copy in rest:
        copy.wait()


def block(part, tok, gain, dy, halves):
    rows, model = tok.shape
    half_rows, hidden = halves.shape[-2:]
    sums = halves.shape[1:]
    weights = (3, 4, 4, 2, half_rows, hidden)
    any_place = pl.BlockSpec(memory_space=pl.ANY)
    quarter = pltpu.VMEM((4, rows, model), BF)
    inner = pltpu.VMEM((4, 2 * rows, hidden), BF)
    flipped = pltpu.VMEM((model, 8 * rows), BF)
    return pl.pallas_call(
        block_kernel,
        out_shape=[
            shape((rows, model), F32),
            shape((rows, model), F32),
            shape((2, 2, rows, model), BF),
            shape((1, model), F32),
            shape((4, rows, model), BF),
            shape(sums, BF),
            shape(sums, BF),
            shape(weights[1:], BF),
        ],
        in_specs=[VM] * 3 + [any_place] * 2,
        out_specs=[VM] * 7 + [any_place],
        scratch_shapes=[
            pltpu.VMEM(weights, BF),
            pltpu.VMEM(dy.shape, BF),
            flipped,
            pltpu.VMEM(dy.shape, BF),
            flipped,
            inner,
            inner,
            inner,
            pltpu.VMEM((2, rows, model), F32),
            quarter,
            quarter,
            quarter,
            pltpu.VMEM((3, rows, model), BF),
            quarter,
            pltpu.VMEM((2, 2, 2, 2, half_rows, hidden), BF),
            pltpu.VMEM((2, 2, 2, 4, half_rows, hidden), BF),
            pltpu.VMEM(weights[1:], BF),
            DMA((3, 2, 4, 2)),
            DMA((3, 2, 4, 2)),
            DMA((3, 2, 4)),
            DMA((3, 2, 4)),
            DMA((2, 2, 2)),
            DMA((2, 2, 2)),
            DMA((2, 2, 2)),
            DMA((2, 2, 2)),
            DMA((7,)),
            DMA((4,)),
            DMA((3,)),
            DMA((3,)),
            DMA((4,)),
            DMA((4,)),
            DMA((4,)),
            DMA((4,)),
            DMA((3,)),
            DMA((3,)),
            DMA((4,)),
            DMA((4,)),
            DMA((3,)),
            DMA((3,)),
        ],
        compiler_params=pltpu.CompilerParams(
            collective_id=3, has_side_effects=True, vmem_limit_bytes=62 << 20
        ),
    )(part, tok, gain, dy, halves)


def rear_kernel(
    heads,
    lse, start_ref, cosines, sines, tok, gain, gnf, *more,
):
    far, outs, near_refs, rest_refs = more[:13], more[13:22], more[22:35], more[35:]
    q_grad, k_grad, v_grad, o_grad, norm_sum, bias_sum, ffn_all, out, grad = outs
    g, gate_sum, down_sum, ysum, dxl, attn, exact, q, kv, x1, ob, h1, dx1 = near_refs
    (
    a_all, ext_all, do, dots, acc, keep, give, arrived, sums, landed, back, part, m1, m2, m3, left_t, ga,
    own, passing, got, p2, q1, sm, q2, fin, fin_w, e0, e1, es, e2, y2,
    ls, d1, d2, d3, d4, ms, ca, cb, cc, cd, fs2, fr2, as1, ar1, as2, ar2, as3, ar3, xs, xr, ss, sr, ts, tr, ys, yr,
    gs, gr,
    ) = rest_refs
    me = Place()
    y, z, lo, k, t = me.y, me.z, me.lo, me.k, me.t
    c = lo * 2 + k
    index = z * 2 + lo
    rows, width = q.shape
    size = width // heads
    slice_rows, model = tok.shape
    rowed = width + size
    offsets = (2, 1, 3)

    def in_x(dt, dc):
        return {"ctx": lax.rem(c + dc, 4), "tp": lax.rem(t + dt, 2)}

    def owner(b):
        return {"fsdp": y * 4 + b // 2, "ctx": lax.rem(b, 2) * 2 + k}

    ring = [(dt, dc) for dt in (0, 1) for dc in range(4) if dt or dc]

    summed_once = (gate_sum, own, down_sum)

    def second_hop(w, half, j):
        if half == 0:
            source, device = summed_once[w].at[0, lax.rem(y + j, 4)], me.along_y(j)
        else:
            source, device = summed_once[w].at[1, lax.rem(z + j, 4)], me.along_z(j)
        return describe(
            source, p2.at[w, half, j - 1], fs2.at[w, half, j - 1], fr2.at[w, half, j - 1], device
        )

    def second_hops(w, half):
        for j in offsets:
            second_hop(w, half, j).start()

    def up_along_z(position, piece, count):
        return g.at[pl.ds(piece, count), position, 0]

    def up_along_y(position, piece, count):
        return g.at[position, pl.ds(piece, count), 1]

    up_rings = [
        RingSum(
            along,
            position,
            source,
            passing.at[half],
            got.at[half],
            [sem.at[half] for sem in (ca, cb, cc, cd)],
        )
        for half, (along, position, source) in enumerate(
            ((me.along_z, z, up_along_z), (me.along_y, y, up_along_y))
        )
    ]

    def up_end(half):
        own[half] = up_rings[half].finish().astype(BF)
        second_hops(1, half)

    def early():
        for one in up_rings:
            one.middle()

    loads = [
        pltpu.make_async_copy(source, target, ls.at[i])
        for i, (source, target) in enumerate(zip(far, near_refs, strict=True))
    ]
    for copy in loads:
        copy.start()
    greet(
        [me.along_z(j) for j in (1, 2, 3)]
        + [me.along_y(j) for j in (1, 2, 3)]
        + [in_x(dt, dc) for dt, dc in ring]
        + [{"fsdp": y * 4 + lax.rem(z + j, 4), "ctx": (1 - lo) * 2 + k} for j in (1, 2, 3)]
    )
    loads[0].wait()
    for one in up_rings:
        one.start()
    for copy in loads[1:4]:
        copy.wait()
    for half in (0, 1):
        second_hops(0, half)
        second_hops(2, half)
    near = [(1 - lo, t), (1 - lo, 1 - t), (lo, 1 - t)]
    results = [
        send(ysum.at[i + 1], y2.at[i], ys.at[i], yr.at[i], me.in_ring(*near[i])) for i in range(3)
    ]

    for copy in loads[4:9]:
        copy.wait()
    do[...] = plain(dxl[...], attn[:, rowed:]).astype(BF)
    for h in range(heads):
        product = exact[h] * do[:, h * size : (h + 1) * size].astype(F32).T
        dots[h : h + 1] = jnp.sum(product, axis=0, keepdims=True)
    acc[...] = jnp.zeros_like(acc)
    start = start_ref[...]
    first = index * rows

    def core_share(b):
        return describe(give.at[b], arrived.at[b], d1.at[b], d2.at[b], me.sibling)

    def home(b):
        return describe(sums.at[b], landed.at[index], d3.at[b], d4.at[index], owner(b))

    def step(b, _):
        keys = kv[0, b]
        values = kv[1, b]
        seen = visible_pairs(b, first, start, rows)
        dk = jnp.zeros((KEYS, size), F32)
        dv = jnp.zeros((KEYS, size), F32)
        for h in range(heads):
            q_h = q[:, h * size : (h + 1) * size]
            do_h = do[:, h * size : (h + 1) * size]
            s = jnp.where(seen, by_columns(keys, q_h), masked_score)
            p = jnp.exp(s - lse[h : h + 1])
            dv = dv + plain(p.astype(BF), do_h)
            dp = by_columns(values, do_h)
            ds = (p * (dp - dots[h : h + 1])).astype(BF)
            dk = dk + plain(ds, q_h)
            acc[h] = acc[h] + over_rows(keys, ds)
        keep[b] = jnp.where(k == 0, dk, dv)
        give[b] = jnp.where(k == 0, dv, dk)
        core_share(b).start()

        @pl.when(b > 0)
        def _():
            @pl.when(b == 1)
            def _():
                early()

            core_share(b - 1).wait_recv()
            sums[b - 1] = (keep[b - 1] + arrived[b - 1]).astype(BF)
            home(b - 1).start()

        return 0

    lax.fori_loop(0, index + 1, step, 0)

    @pl.when(index < 1)
    def _():
        early()


    for copy in loads[9:]:
        copy.wait()
    result = x1[...] + ysum[0].astype(F32)
    for i in range(3):
        results[i].wait()
        result = result + y2[i].astype(F32)
    out[t] = result.astype(BF)
    mine = out.at[t]
    rest = [send(mine, mine, gs.at[1], gr.at[1], me.in_ring(lo, 1 - t))]
    up_end(1)
    up_end(0)

    scale = 1.0 / math.sqrt(size)
    for h in range(heads):
        dq = turned(acc[h].T * scale, cosines[...], -sines[...])
        e0[2:3, h * size : (h + 1) * size] = jnp.sum(dq, axis=0, keepdims=True)
        back[:, h * size : (h + 1) * size] = dq.astype(BF)
    left_t[...] = dxl[...].T
    blocks = ga.shape[:4]

    def spread(value):
        return value.astype(BF).reshape(blocks + (value.shape[1],))

    ga[:, :, :, :, rowed:] = spread(plain(left_t[...], ob[...]))
    left_t[...] = h1[...].T
    ga[:, :, :, :, :width] = spread(plain(left_t[...], back[:, :width]))

    core_share(index).wait_recv()
    dkv = keep[index] + arrived[index]
    keep[index] = dkv
    for b in range(1, 8):

        @pl.when(b > index)
        def _():
            describe(sums.at[0], landed.at[b], d3.at[0], d4.at[b], owner(0)).wait_recv()
            keep[index] = keep[index] + landed[b].astype(F32)

    is_key = k == 0
    dkv = turned(
        keep[index], jnp.where(is_key, cosines[...], 1.0), jnp.where(is_key, -sines[...], 0.0)
    )
    e0[2:3, width:rowed] = jnp.sum(dkv, axis=0, keepdims=True)
    back[:, width:] = dkv.astype(BF)
    part[...] = (
        by_columns(back[...], attn[:, :rowed]).astype(BF).reshape(2, 2, slice_rows, model)
    )
    cores = send(part.at[1 - k], m1, ms.at[0], ms.at[1], me.sibling)
    ga[:, :, :, :, width:rowed] = spread(plain(left_t[...], back[:, width:]))

    large = []
    for j in offsets:
        large.append(
            send(
                ga.at[:, lax.rem(z + j, 4), 0], q1.at[0, j - 1], as1.at[0, j - 1], ar1.at[0, j - 1], me.along_z(j)
            )
        )
        large.append(
            send(
                ga.at[lax.rem(y + j, 4), :, 1], q1.at[1, j - 1], as1.at[1, j - 1], ar1.at[1, j - 1], me.along_y(j)
            )
        )

    cores.wait()
    m2[...] = (part[k, 1 - t].astype(F32) + m1[1 - t].astype(F32)).astype(BF)
    across = send(m2, m3, ms.at[2], ms.at[3], me.in_ring(lo, 1 - t))
    quarter = sm.shape[2] // 2

    def summed(w, half):
        for j in offsets:
            second_hop(w, half, j).wait()
        here = summed_once[w][0, y] if half == 0 else summed_once[w][1, z]
        total = here.astype(F32)
        for j in range(3):
            total = total + p2[w, half, j].astype(F32)
        return total

    def to_owners(w):
        for half in (0, 1):
            total = summed(w, half)
            fin_w[w, 2 * half] = total[:quarter]
            fin_w[w, 2 * half + 1] = total[quarter:]
        width = fin_w.shape[3]
        place = pl.ds(pl.multiple_of(c * width, 128), width)
        ffn_all[w, :, place] = fin_w[w, c]
        return [
            send(
                fin_w.at[w, lax.rem(c + j, 4)], ffn_all.at[w, :, place], ts.at[w, j - 1], tr.at[w, j - 1], in_x(0, j)
            )
            for j in (2, 1, 3)
        ]

    rest += to_owners(2) + to_owners(0) + to_owners(1)

    x = tok[...].astype(F32)
    factor = lax.rsqrt(jnp.mean(x * x, axis=-1, keepdims=True) + epsilon)
    normed = x * factor
    dh1 = part[k, t].astype(F32) + m1[t].astype(F32)
    across.wait()
    dh1 = dh1 + m3[...].astype(F32)
    e0[0:1] = jnp.sum(dh1 * normed, axis=0, keepdims=True)
    e0[1:2] = gnf[...]
    e0[2:3, rowed:] = jnp.zeros((1, model - rowed), F32)
    e0[3:] = jnp.zeros((5, model), F32)
    small = [
        send(e0, e1.at[j - 1], ss.at[0, j - 1], sr.at[0, j - 1], me.along_z(j)) for j in offsets
    ]
    grad[t] = (dx1[...] + norm_back(dh1 * gain[...], normed, factor)).astype(BF)
    mine = grad.at[t]
    rest.append(send(mine, mine, gs.at[0], gr.at[0], me.in_ring(lo, 1 - t)))

    for copy in large:
        copy.wait()
    for half in (0, 1):
        here = ga[:, z, 0] if half == 0 else ga[y, :, 1]
        total = here.astype(F32)
        for j in range(3):
            total = total + q1[half, j].astype(F32)
        sm[half] = total.astype(BF)
    last = []
    for j in offsets:
        last.append(
            send(
                sm.at[0, lax.rem(y + j, 4)], q2.at[0, j - 1], as2.at[0, j - 1], ar2.at[0, j - 1], me.along_y(j)
            )
        )
        last.append(
            send(
                sm.at[1, lax.rem(z + j, 4)], q2.at[1, j - 1], as2.at[1, j - 1], ar2.at[1, j - 1], me.along_z(j)
            )
        )
    for copy in small:
        copy.wait()
    es[...] = (e0[...] + e1[0]) + (e1[1] + e1[2])
    small = [
        send(es, e2.at[j - 1], ss.at[1, j - 1], sr.at[1, j - 1], me.along_y(j)) for j in offsets
    ]

    for copy in small:
        copy.wait()
    ext_all[t, c] = (es[...] + e2[0]) + (e2[1] + e2[2])
    mine = ext_all.at[t, c]
    rest += [
        send(mine, mine, xs.at[i], xr.at[i], in_x(dt, dc)) for i, (dt, dc) in enumerate(ring)
    ]
    for copy in last:
        copy.wait()
    for half in (0, 1):
        here = sm[0, y] if half == 0 else sm[1, z]
        total = here.astype(F32)
        for j in range(3):
            total = total + q2[half, j].astype(F32)
        fin[2 * half] = total[:quarter]
        fin[2 * half + 1] = total[quarter:]
    a_all[c] = fin[c]
    rest += [
        send(fin.at[lax.rem(c + j, 4)], a_all.at[c], as3.at[j - 1], ar3.at[j - 1], in_x(0, j))
        for j in (2, 1, 3)
    ]

    def sent(b, _):
        core_share(b).wait_send()

        @pl.when(b < index)
        def _():
            home(b).wait_send()

        return 0

    lax.fori_loop(0, index + 1, sent, 0)
    for copy in rest:
        copy.wait()
    total = ext_all[0, 0]
    for i in range(1, 8):
        total = total + ext_all[i // 4, i % 4]
    norm_sum[...] = total
    for core in (0, 1):
        bias_sum[core] = ext_all[t, core] + ext_all[t, 2 + core]
        total = a_all[core] + a_all[2 + core]
        place = slice(core * width, (core + 1) * width)
        q_grad[:, place] = total[:, :width]
        (k_grad, v_grad)[core][...] = total[:, width:rowed]
        o_grad[:, place] = total[:, rowed:]


def rear(heads, g, gate_sum, down_sum, dxl, attn, q, kv, exact, lse, start, ob, h1, cosines, sines, ysum, x1, dx1, tok, gain, gnf):
    rows, width = q.shape
    size = width // heads
    slice_rows, model = tok.shape
    hidden = g.shape[-1]
    total = attn.shape[1]
    half_rows = model // 32
    quarter = half_rows // 2
    shared = pltpu.VMEM(kv.shape[1:], F32)
    shared_low = pltpu.VMEM(kv.shape[1:], BF)
    slab = pltpu.VMEM((slice_rows, model), BF)
    args = (lse, start, cosines, sines, tok, gain, gnf)
    far = (g, gate_sum, down_sum, ysum, dxl, attn, exact, q, kv, x1, ob, h1, dx1)
    outs = [
        shape((quarter, 2 * width), F32),
        shape((quarter, size), F32),
        shape((quarter, size), F32),
        shape((quarter, 2 * width), F32),
        shape((8, model), F32),
        shape((2, 8, model), F32),
        shape((3, quarter, 4 * hidden), F32),
        shape((2, slice_rows, model), BF),
        shape((2, slice_rows, model), BF),
    ]
    return pl.pallas_call(
        functools.partial(rear_kernel, heads),
        out_shape=outs,
        in_specs=[VM] * len(args) + [pl.BlockSpec(memory_space=pl.ANY)] * len(far),
        out_specs=[VM] * len(outs),
        scratch_shapes=[pltpu.VMEM(array.shape, array.dtype) for array in far]
        + [
            pltpu.VMEM((4, quarter, total), F32),
            pltpu.VMEM((2, 4, 8, model), F32),
            pltpu.VMEM((rows, width), BF),
            pltpu.VMEM((8, rows), F32),
            pltpu.VMEM((heads, size, rows), F32),
            shared,
            shared,
            shared,
            shared_low,
            shared_low,
            pltpu.VMEM((rows, width + size), BF),
            pltpu.VMEM((2, 2, slice_rows, model), BF),
            pltpu.VMEM((2, slice_rows, model), BF),
            slab,
            slab,
            pltpu.VMEM((model, rows), BF),
            pltpu.VMEM((4, 4, 2, half_rows, total), BF),
            pltpu.VMEM((2, 4, half_rows, hidden), BF),
            pltpu.VMEM((2, 2, 2, half_rows, hidden), BF),
            pltpu.VMEM((2, 2, 4, half_rows, hidden), BF),
            pltpu.VMEM((3, 2, 3, half_rows, hidden), BF),
            pltpu.VMEM((2, 3, 4, half_rows, total), BF),
            pltpu.VMEM((2, 4, half_rows, total), BF),
            pltpu.VMEM((2, 3, half_rows, total), BF),
            pltpu.VMEM((4, quarter, total), F32),
            pltpu.VMEM((3, 4, quarter, hidden), F32),
            pltpu.VMEM((8, model), F32),
            pltpu.VMEM((3, 8, model), F32),
            pltpu.VMEM((8, model), F32),
            pltpu.VMEM((3, 8, model), F32),
            pltpu.VMEM((3, slice_rows, model), BF),
            DMA((13,)),
            DMA((8,)),
            DMA((8,)),
            DMA((8,)),
            DMA((8,)),
            DMA((4,)),
            DMA((2, 2)),
            DMA((2, 2)),
            DMA((2, 2)),
            DMA((2, 2)),
            DMA((3, 2, 3)),
            DMA((3, 2, 3)),
            DMA((2, 3)),
            DMA((2, 3)),
            DMA((2, 3)),
            DMA((2, 3)),
            DMA((3,)),
            DMA((3,)),
            DMA((7,)),
            DMA((7,)),
            DMA((2, 3)),
            DMA((2, 3)),
            DMA((3, 3)),
            DMA((3, 3)),
            DMA((3,)),
            DMA((3,)),
            DMA((2,)),
            DMA((2,)),
        ],
        compiler_params=pltpu.CompilerParams(
            collective_id=7, has_side_effects=True, vmem_limit_bytes=62 << 20
        ),
    )(*args, *far)


def shards(
    tokens,
    segments,
    w_query,
    key_matrix,
    value_matrix,
    b_query,
    key_bias_vector,
    value_bias_vector,
    w_out,
    norm_attn,
    norm_ffn,
    w_gate,
    w_up,
    w_down,
    cotangent,
):
    f = lax.axis_index("fsdp")
    c = lax.axis_index("ctx")
    t = lax.axis_index("tp")
    k = c % 2
    is_key = k == 0
    size = key_matrix.shape[1]
    query_width = w_query.shape[1] // 2
    heads = query_width // size
    own_width = query_width + size
    model = tokens.shape[1]
    count = tokens.shape[0]
    slice_rows = count // 2
    shard_rows = w_query.shape[0]
    hidden = w_gate.shape[1] // 4
    padded = -(-hidden // 128) * 128

    def hidden_slice(w, axis):
        widths = [(0, 0), (0, 0)]
        widths[axis] = (0, 4 * padded - 4 * hidden)
        return lax.dynamic_slice_in_dim(jnp.pad(w, widths), c * padded, padded, axis)

    own_ffn = jnp.stack(
        [
            hidden_slice(w_gate, 1),
            hidden_slice(w_up, 1),
            hidden_slice(w_down, 0).T,
        ]
    )

    own_attn = jnp.concatenate(
        [
            lax.dynamic_slice_in_dim(w_query, k * query_width, query_width, 1),
            jnp.where(is_key, key_matrix, value_matrix),
            lax.dynamic_slice_in_dim(w_out, k * query_width, query_width, 0).T,
        ],
        axis=1,
    )
    own_tokens = lax.dynamic_slice_in_dim(tokens, t * slice_rows, slice_rows, 0)
    rows = 2 * count
    half_size = size // 2
    frequency = np.exp(np.arange(half_size) * (-2.0 * math.log(rope_base) / size))
    frequency = jnp.asarray(np.concatenate([frequency, frequency])[None].astype(np.float32))
    gain_attn = norm_attn.astype(F32)[None]
    gain_ffn = norm_ffn.astype(F32)[None]
    bias = jnp.concatenate(
        [
            lax.dynamic_slice_in_dim(b_query, k * query_width, query_width, 0),
            jnp.where(is_key, key_bias_vector, value_bias_vector),
        ]
    ).astype(F32)[None]
    (
        attn_all,
        halves,
        dy_all,
        h1,
        q,
        kv,
        exact,
        ob,
        lse,
        starts,
        cosines,
        sines,
        part,
    ) = front(heads, own_attn, own_ffn, tokens, cotangent, segments, gain_attn, bias, frequency)
    x1, dx1, dxl, grad_norm_two, ysum, gate_sum, down_sum, up_grad = block(
        part, own_tokens, gain_ffn, dy_all, halves
    )
    q_grad, k_grad, v_grad, o_grad, norm_sum, bias_sum, ffn_all, output, grad_tokens = rear(
        heads,
        up_grad,
        gate_sum,
        down_sum,
        dxl.reshape(rows, model),
        attn_all.reshape(model, own_width + query_width),
        q,
        kv,
        exact,
        lse,
        starts,
        ob,
        h1,
        cosines,
        sines,
        ysum,
        x1,
        dx1,
        own_tokens,
        gain_attn,
        grad_norm_two,
    )
    owner_rows = shard_rows // 4

    owner = f * 4 + c
    norms = lax.dynamic_slice_in_dim(norm_sum[:2], owner * owner_rows, owner_rows, 1)
    biases = bias_sum[:, 2, :own_width].reshape(2, heads + 1, size)
    biases = lax.dynamic_slice_in_dim(biases, owner * 2, 2, 2)
    return (
        output.reshape(count, model),
        grad_tokens.reshape(count, model).astype(F32),
        q_grad,
        k_grad,
        v_grad,
        biases[:, :heads].reshape(2 * heads, 2),
        biases[0, heads:],
        biases[1, heads:],
        o_grad.T,
        norms[0],
        norms[1],
        ffn_all[0, :, : 4 * hidden],
        ffn_all[1, :, : 4 * hidden],
        ffn_all[2, :, : 4 * hidden].T,
    )


def solution(mesh):
    both = ("fsdp", "ctx")
    in_specs = (
        P(both, None),
        P(),
        P("fsdp", "tp"),
        P("fsdp", "tp"),
        P("fsdp", "tp"),
        P("tp"),
        P("tp"),
        P("tp"),
        P("tp", "fsdp"),
        P(),
        P(),
        P("fsdp", "tp"),
        P("fsdp", "tp"),
        P("tp", "fsdp"),
        P(both, None),
    )
    out_specs = (
        P(both, None),
        P(both, None),
        P(both, "tp"),
        P(both, "tp"),
        P(both, "tp"),
        P("tp", both),
        P("tp", both),
        P("tp", both),
        P("tp", both),
        P(both),
        P(both),
        P(both, "tp"),
        P(both, "tp"),
        P("tp", both),
    )
    return jax.shard_map(shards, mesh=mesh, in_specs=in_specs, out_specs=out_specs, check_vma=False)
```

```python
import functools
import math

import jax
import jax.numpy as jnp
import numpy as np
from jax import lax
from jax.experimental import pallas as pl
from jax.experimental.pallas import tpu as pltpu
from jax.sharding import PartitionSpec as P

MESH = pl.DeviceIdType.MESH
VM = pl.BlockSpec(memory_space=pltpu.VMEM)
DMA = pltpu.SemaphoreType.DMA
BF = jnp.bfloat16
F32 = jnp.float32

epsilon = 1e-06
rope_base = 1000000.0
masked_score = -1e30
KEYS = 512


class Place:
    def __init__(self):
        f = lax.axis_index("fsdp")
        c = lax.axis_index("ctx")
        self.y, self.z = f // 4, f % 4
        self.lo, self.k = c // 2, c % 2
        self.t = lax.axis_index("tp")

    def along_y(self, j):
        return {"fsdp": lax.rem(self.y + j, 4) * 4 + self.z}

    def along_z(self, j):
        return {"fsdp": self.y * 4 + lax.rem(self.z + j, 4)}

    @property
    def sibling(self):
        return {"ctx": self.lo * 2 + 1 - self.k}

    def in_ring(self, lo, t):
        return {"ctx": lo * 2 + self.k, "tp": t}

    @property
    def others(self):
        return [(self.lo, 1 - self.t), (1 - self.lo, self.t), (1 - self.lo, 1 - self.t)]


def greet(devices):
    barrier = pltpu.get_barrier_semaphore()
    for device in devices:
        pl.semaphore_signal(barrier, inc=1, device_id=device, device_id_type=MESH)
    pl.semaphore_wait(barrier, len(devices))


def describe(source, target, send_sem, recv_sem, device):
    return pltpu.make_async_remote_copy(
        src_ref=source,
        dst_ref=target,
        send_sem=send_sem,
        recv_sem=recv_sem,
        device_id=device,
        device_id_type=MESH,
    )


def send(source, target, send_sem, recv_sem, device):
    copy = describe(source, target, send_sem, recv_sem, device)
    copy.start()
    return copy


def comm_call(body, outs, scratch, collective_id, mib, *args):
    return pl.pallas_call(
        body,
        out_shape=outs,
        in_specs=[VM] * len(args),
        out_specs=[VM] * len(outs),
        scratch_shapes=scratch,
        compiler_params=pltpu.CompilerParams(
            collective_id=collective_id, has_side_effects=True, vmem_limit_bytes=mib << 20
        ),
    )(*args)


def shape(dims, kind):
    return jax.ShapeDtypeStruct(dims, kind)


def over_rows(a, b):
    return lax.dot_general(a, b, (((0,), (0,)), ((), ())), preferred_element_type=F32)


def by_columns(a, b):
    return lax.dot_general(a, b, (((1,), (1,)), ((), ())), preferred_element_type=F32)


def plain(a, b):
    return lax.dot_general(a, b, (((1,), (0,)), ((), ())), preferred_element_type=F32)


def visible_pairs(block, first, start, rows):
    key = block * KEYS + lax.broadcasted_iota(jnp.int32, (KEYS, rows), 0)
    row = first + lax.broadcasted_iota(jnp.int32, (1, rows), 1)
    return (key >= start) & (key <= row)


class RingGather:
    def __init__(self, along, position, pieces, target, source, sems):
        self.along, self.position, self.pieces = along, position, pieces
        self.target, self.source, self.sems = target, source, sems

    def hop(self, i, way):
        s, r = self.sems[:2]
        return describe(
            self.source(i),
            self.target(self.position, i),
            s.at[i, way],
            r.at[i, way],
            self.along(1 if way == 0 else 3),
        )

    def onward(self, i):
        s, r = self.sems[2:]
        way = i // 2
        block = self.target(lax.rem(self.position + (3 if way == 0 else 1), 4), i)
        return describe(block, block, s.at[i], r.at[i], self.along(1 if way == 0 else 3))

    def start(self, i):
        self.hop(i, 0).start()
        self.hop(i, 1).start()

    def forward(self, i):
        self.hop(i, i // 2).wait_recv()
        self.onward(i).start()

    def finish(self):
        for i in range(4):
            self.hop(i, 1 - i // 2).wait_recv()
            self.onward(i).wait()
            self.hop(i, 0).wait_send()
            self.hop(i, 1).wait_send()


class RingSum:
    def __init__(self, along, position, source, passing, got, sems):
        self.along, self.position, self.source = along, position, source
        self.passing, self.got, self.sems = passing, got, sems

    def at(self, offset):
        return lax.rem(self.position + offset, 4)

    def first(self, way):
        s, r = self.sems[:2]
        return describe(
            self.source(self.at(2), 2 * way, 2),
            self.passing.at[way],
            s.at[way],
            r.at[way],
            self.along(1 if way == 0 else 3),
        )

    def second(self, way):
        s, r = self.sems[2:]
        offset = 1 if way == 0 else 3
        return describe(
            self.source(self.at(offset), 0, 4), self.got.at[way], s.at[way], r.at[way], self.along(offset)
        )

    def start(self):
        for way in (0, 1):
            self.first(way).start()

    def middle(self):
        for way in (0, 1):
            self.first(way).wait()
            near = self.source(self.at(1 if way == 0 else 3), 2 * way, 2)
            near[...] = (near[...].astype(F32) + self.passing[way].astype(F32)).astype(BF)
            self.second(way).start()

    def finish(self):
        total = self.source(self.position, 0, 4)[...].astype(F32)
        for way in (0, 1):
            self.second(way).wait()
            total = total + self.got[way].astype(F32)
        return total


def turned(values, cosines, sines):
    return values * cosines - pltpu.roll(values, values.shape[-1] // 2, 1) * sines


def front_kernel(
    heads,
    w, ffn, tok, dy, segments, gain, bias, frequency,
    w_out, halves, dy_all, h1_out, q, kv_out, exact, ob, lse, starts, cosines, sines, part,
    w_all, h1, kv, tok2, top, total, acc,
    s1, r1, wa, wb, wc, wd, s3, r3, ts, tr, ds, dr, fs, fr, ks, kr, cs, cr, ls, os,
):
    me = Place()
    y, z, lo, k, t = me.y, me.z, me.lo, me.k, me.t
    index = z * 2 + lo
    count, model = tok.shape
    rows = 2 * count
    width, size = q.shape[1], exact.shape[1]
    rowed = width + size
    shard = w.shape[0] // 2
    parts = (pl.ds(0, shard), pl.ds(shard, shard))
    near = [me.in_ring(1 - lo, t), me.in_ring(1 - lo, 1 - t)]
    offsets = (1, 3, 2)
    greet(
        [me.along_z(j) for j in (1, 2, 3)]
        + [me.along_y(j) for j in (1, 2, 3)]
        + [me.sibling]
        + near
        + [{"fsdp": y * 4 + lax.rem(z + j, 4), "ctx": (1 - lo) * 2 + k} for j in (1, 2, 3)]
    )

    def attn_place(half, position, i):
        if half == 0:
            return w_all.at[position, lax.rem(z + 4 - i, 4), parts[0]]
        return w_all.at[lax.rem(y + 4 - i, 4), position, parts[1]]

    def attn_source(half, i):
        if i == 0:
            return w.at[parts[half]]
        return attn_place(half, y if half == 0 else z, i)

    def first_hop(half, j):
        along = me.along_z if half == 0 else me.along_y
        return describe(
            w.at[parts[half]],
            w_all.at[y, z, parts[half]],
            s1.at[half, j - 1],
            r1.at[half, j - 1],
            along(j),
        )

    rings = [
        RingGather(
            me.along_y if half == 0 else me.along_z,
            y if half == 0 else z,
            4,
            functools.partial(attn_place, half),
            functools.partial(attn_source, half),
            [sem.at[half] for sem in (wa, wb, wc, wd)],
        )
        for half in (0, 1)
    ]
    for j in offsets:
        for half in (0, 1):
            first_hop(half, j).start()
    for ring in rings:
        ring.start(0)
    tokens_share = send(tok, tok2, ts, tr, me.sibling)
    slab = count // 2
    near_copies = [
        send(dy.at[pl.ds(t * slab, slab)], dy_all.at[lo, t, k], ds.at[i], dr.at[i], near[i])
        for i in (0, 1)
    ]
    rest = [
        send(dy.at[pl.ds(h * slab, slab)], dy_all.at[lo, h, k], fs.at[2 + h], fr.at[2 + h], me.sibling)
        for h in (0, 1)
    ]
    w_all[y, z] = w[...]
    stores = [
        pltpu.make_async_copy(dy.at[pl.ds(h * slab, slab)], dy_all.at[lo, h, k], os.at[h])
        for h in (0, 1)
    ]
    for copy in stores:
        copy.start()

    first = pl.multiple_of(index * rows, rows)
    everyone = segments[pl.ds(y, 1), :]
    mine = segments[pl.ds(y, 1), pl.ds(first, rows)]
    start = jnp.zeros((1, rows), jnp.int32)
    for number in (1, 2, 3):
        begin = jnp.sum(jnp.where(everyone < number, 1.0, 0.0), axis=1, keepdims=True)
        start = jnp.where(mine == number, begin.astype(jnp.int32), start)
    starts[...] = start
    row = first + lax.broadcasted_iota(jnp.int32, (1, rows), 1)
    pos = jnp.broadcast_to((row - start).astype(F32), (8, rows)).T[:, :1]
    angles = pos * frequency[...]
    lane = lax.broadcasted_iota(jnp.int32, (1, size), 1)
    cosines[...] = jnp.cos(angles)
    sines[...] = jnp.sin(angles) * jnp.where(lane < size // 2, 1.0, -1.0)

    for j in offsets:
        for half in (0, 1):
            first_hop(half, j).wait()
            rings[half].start(j)

    def normed(x):
        x = x.astype(F32)
        factor = lax.rsqrt(jnp.mean(x * x, axis=-1, keepdims=True) + epsilon)
        return (x * factor * gain[...]).astype(BF)

    h1[pl.ds(pl.multiple_of(k * count, count), count)] = normed(tok[...])
    tokens_share.wait()
    h1[pl.ds(pl.multiple_of((1 - k) * count, count), count)] = normed(tok2[...])

    for i in (0, 1, 3, 2):
        for ring in rings:
            ring.forward(i)

    def ffn_hop(i, half, j):
        along, here = (me.along_z, z) if half == 0 else (me.along_y, y)
        return describe(
            ffn.at[i, parts[half]],
            halves.at[i, half, here],
            s3.at[i, half, j - 1],
            r3.at[i, half, j - 1],
            along(j),
        )

    def ffn_hops(i):
        for half in (0, 1):
            for j in offsets:
                ffn_hop(i, half, j).start()
            there = halves.at[i, half, z if half == 0 else y]
            copy = pltpu.make_async_copy(ffn.at[i, parts[half]], there, ls.at[i, half])
            copy.start()
            stores.append(copy)

    ffn_hops(0)
    for ring in rings:
        ring.finish()
    for i, (source, there) in enumerate(((w_all, w_out), (h1, h1_out))):
        copy = pltpu.make_async_copy(source, there, os.at[2 + i])
        copy.start()
        stores.append(copy)

    inward = w_all[:, :, :, :rowed].reshape(model, rowed)
    linear = plain(h1[...], inward) + bias[...]
    scale = 1.0 / math.sqrt(size)
    is_key = k == 0
    own = turned(
        linear[:, width:],
        jnp.where(is_key, cosines[...], 1.0),
        jnp.where(is_key, sines[...], 0.0),
    )
    kv[k, index] = own.astype(BF)
    own_keys = kv.at[k, index]

    def keys_copy(i, device):
        return describe(own_keys, own_keys, ks.at[i], kr.at[index], device)

    targets = [(dz, to) for dz in (1, 2, 3) for to in (0, 1)]

    def target(dz, to):
        return {"fsdp": y * 4 + lax.rem(z + dz, 4), "ctx": to * 2 + k}

    for i, (dz, to) in enumerate(targets):

        @pl.when(z + dz < 4)
        def _():
            keys_copy(i, target(dz, to)).start()

    @pl.when(lo == 0)
    def _():
        keys_copy(6, {"ctx": 2 + k}).start()

    def keys_share(b):
        there = kv.at[k, b]
        return describe(there, there, cs.at[b], cr.at[b], me.sibling)

    keys_share(index).start()
    for h in range(heads):
        here = slice(h * size, (h + 1) * size)
        q[:, here] = (turned(linear[:, here], cosines[...], sines[...]) * scale).astype(BF)

    ffn_hops(1)
    ffn_hops(2)
    for i, half in ((0, t), (1, 1 - t)):
        near_copies[i].wait()
        there = dy_all.at[1 - lo, half, k]
        rest.append(send(there, there, fs.at[i], fr.at[i], me.sibling))

    top[...] = jnp.full_like(top, masked_score)
    total[...] = jnp.zeros_like(total)
    acc[...] = jnp.zeros_like(acc)

    def step(i, _):
        b = index - i

        @pl.when(b > 0)
        def _():
            there = kv.at[k, b - 1]
            describe(there, there, ks.at[0], kr.at[b - 1], me.sibling).wait_recv()
            keys_share(b - 1).start()

        keys_share(b).wait_recv()
        keys = kv[0, b]
        values = kv[1, b]
        seen = visible_pairs(b, first, start, rows)
        for h in range(heads):
            s = by_columns(keys, q[:, h * size : (h + 1) * size])
            s = jnp.where(seen, s, masked_score)
            before = top[h : h + 1]
            now = jnp.maximum(before, jnp.max(s, axis=0, keepdims=True))
            p = jnp.exp(s - now)
            shrink = jnp.exp(before - now)
            top[h : h + 1] = now
            total[h : h + 1] = total[h : h + 1] * shrink + jnp.sum(p, axis=0, keepdims=True)
            acc[h] = acc[h] * shrink + over_rows(values, p.astype(BF))
        return 0

    lax.fori_loop(0, index + 1, step, 0)
    copy = pltpu.make_async_copy(kv, kv_out, os.at[4])
    copy.start()
    stores.append(copy)
    lse[...] = jnp.zeros_like(lse)
    for h in range(heads):
        sums = total[h : h + 1]
        lse[h : h + 1] = top[h : h + 1] + jnp.log(sums)
        out = acc[h] / sums
        exact[h] = out
        ob[:, h * size : (h + 1) * size] = out.T.astype(BF)
    outward = w_all[:, :, :, rowed:].reshape(model, width)
    part[...] = by_columns(ob[...], outward).astype(BF).reshape(part.shape)

    for i, (dz, to) in enumerate(targets):

        @pl.when(z + dz < 4)
        def _():
            keys_copy(i, target(dz, to)).wait_send()

    @pl.when(lo == 0)
    def _():
        keys_copy(6, {"ctx": 2 + k}).wait_send()

    def shared(b, _):
        keys_share(b).wait_send()
        return 0

    lax.fori_loop(0, index + 1, shared, 0)
    for i in range(3):
        for half in (0, 1):
            for j in offsets:
                ffn_hop(i, half, j).wait()
    for copy in rest + stores:
        copy.wait()


def front(heads, w, ffn, tok, dy, segments, gain, bias, frequency):
    shard, total = w.shape
    hidden = ffn.shape[2]
    count, model = tok.shape
    rows = 2 * count
    width = bias.shape[1] - frequency.shape[1]
    size = frequency.shape[1]
    far = pl.BlockSpec(memory_space=pl.ANY)
    args = (w, ffn, tok, dy, segments, gain, bias, frequency)
    outs = [
        shape((4, 4, shard, total), BF),
        shape((3, 2, 4, shard // 2, hidden), BF),
        shape((2, 2, 2, count // 2, model), BF),
        shape((rows, model), BF),
        shape((rows, width), BF),
        shape((2, 8, rows, size), BF),
        shape((heads, size, rows), F32),
        shape((rows, width), BF),
        shape((8, rows), F32),
        shape((1, rows), jnp.int32),
        shape((rows, size), F32),
        shape((rows, size), F32),
        shape((2, 2, count // 2, model), BF),
    ]
    return pl.pallas_call(
        functools.partial(front_kernel, heads),
        out_shape=outs,
        in_specs=[VM] * len(args),
        out_specs=[far] * 4 + [VM, far] + [VM] * (len(outs) - 6),
        scratch_shapes=[
            pltpu.VMEM((4, 4, shard, total), BF),
            pltpu.VMEM((rows, model), BF),
            pltpu.VMEM((2, 8, rows, size), BF),
            pltpu.VMEM((count, model), BF),
            pltpu.VMEM((8, rows), F32),
            pltpu.VMEM((8, rows), F32),
            pltpu.VMEM((heads, size, rows), F32),
            DMA((2, 3)),
            DMA((2, 3)),
            DMA((2, 4, 2)),
            DMA((2, 4, 2)),
            DMA((2, 4)),
            DMA((2, 4)),
            DMA((3, 2, 3)),
            DMA((3, 2, 3)),
            DMA,
            DMA,
            DMA((2,)),
            DMA((2,)),
            DMA((4,)),
            DMA((4,)),
            DMA((7,)),
            DMA((8,)),
            DMA((8,)),
            DMA((8,)),
            DMA((3, 2)),
            DMA((5,)),
        ],
        compiler_params=pltpu.CompilerParams(
            collective_id=1, has_side_effects=True, vmem_limit_bytes=56 << 20
        ),
    )(*args)


def norm_back(grad_normed, normed, factor):
    return factor * (grad_normed - normed * jnp.mean(grad_normed * normed, axis=-1, keepdims=True))


def block_kernel(
    part, tok, gain, dy_hbm, halves,
    x1, dx1, dxl, gnf, ysum, gate_sum, down_sum, up_grad,
    w, dy, dy_t, h2, h2_t, hid, gate_back, up_back, whole, pb, s1, r1, r2, ry, passing, got, gx,
    ba, bb, bc, bd, ca, cb, cc, cd, ls, ms, hs, hr, fs, fr, ps, pr, xs, xr, ys, yr, gs, gr,
):
    me = Place()
    y, z, lo, k, t = me.y, me.z, me.lo, me.k, me.t
    rows, model = tok.shape
    both = 2 * rows
    inner = w.shape[-1]
    offsets = (2, 1, 3)

    def chip(i):
        return lax.rem(lo + lax.rem((i + 1) // 2, 2), 2), lax.rem(t + i // 2, 2)

    def columns(i):
        return pl.ds(pl.multiple_of(i * both, both), both)

    loads = [pltpu.make_async_copy(dy_hbm, dy, ls.at[6])]
    for i in range(3):
        loads.append(pltpu.make_async_copy(halves.at[i, 0], w.at[i, y, :, 0], ls.at[2 * i]))
        loads.append(pltpu.make_async_copy(halves.at[i, 1], w.at[i, :, z, 1], ls.at[2 * i + 1]))
    for copy in loads:
        copy.start()
    greet(
        [me.in_ring(*chip(i)) for i in (1, 2, 3)]
        + [me.sibling]
        + [me.along_z(j) for j in (1, 2, 3)]
        + [me.along_y(j) for j in (1, 2, 3)]
    )
    m1, m2, m3 = r1.at[pl.ds(0, 2)], s1.at[0], r2.at[2]
    cores = send(part.at[1 - k], m1, ms.at[0], ms.at[1], me.sibling)

    def weight_place(i, half, position, piece):
        if half == 0:
            return w.at[i, position, lax.rem(z + 4 - piece, 4), 0]
        return w.at[i, lax.rem(y + 4 - piece, 4), position, 1]

    def weight_source(i, half, piece):
        return halves.at[i, half, lax.rem((z if half == 0 else y) + 4 - piece, 4)]

    rings = [
        [
            RingGather(
                me.along_y if half == 0 else me.along_z,
                y if half == 0 else z,
                4,
                functools.partial(weight_place, i, half),
                functools.partial(weight_source, i, half),
                [sem.at[i, half] for sem in (ba, bb, bc, bd)],
            )
            for half in (0, 1)
        ]
        for i in range(3)
    ]

    def gather_start(i):
        for ring in rings[i]:
            for piece in range(4):
                ring.start(piece)

    def gather_forward(i):
        for ring in rings[i]:
            for piece in range(4):
                ring.forward(piece)

    def gather_finish(i):
        for ring in rings[i]:
            ring.finish()
        for copy in loads[2 * i + 1 : 2 * i + 3]:
            copy.wait()

    def weight(i):
        return w[i].reshape(model, inner)

    gather_start(0)
    gather_start(1)
    loads[0].wait()

    def turn_dy(i, _):
        lo_i, t_i = chip(i)
        dy_t[:, columns(i)] = dy[lo_i, t_i].reshape(both, model).T
        return 0

    cores.wait()
    m2[...] = (part[k, 1 - t].astype(F32) + m1[1 - t].astype(F32)).astype(BF)
    across = send(m2, m3, ms.at[2], ms.at[3], me.in_ring(lo, 1 - t))
    lax.fori_loop(0, 4, turn_dy, 0)
    x = tok[...].astype(F32) + part[k, t].astype(F32) + m1[t].astype(F32)
    gather_forward(0)
    across.wait()
    x = x + m3[...].astype(F32)
    x1[...] = x
    factor = lax.rsqrt(jnp.mean(x * x, axis=-1, keepdims=True) + epsilon)
    h2[lo, t, k] = (x * factor * gain[...]).astype(BF)

    def hidden_copy(i):
        block = h2.at[lo, t, k]
        return describe(block, block, hs.at[i - 1], hr.at[i - 1], me.in_ring(*chip(i)))

    def hidden_share(i):
        lo_i, t_i = chip(i)
        block = h2.at[lo_i, t_i, k]
        return describe(block, block, fs.at[i], fr.at[i], me.sibling)

    def part_share(i):
        return describe(pb.at[i], r1.at[i], ps.at[i], pr.at[i], me.sibling)

    def part_copy(i):
        return describe(
            s1.at[i], r2.at[i - 1], xs.at[i - 1], xr.at[i - 1], me.in_ring(*chip(i))
        )

    def result_share(i):
        return describe(pb.at[i], ry.at[i], ys.at[i], yr.at[i], me.sibling)

    for i in (1, 2, 3):
        hidden_copy(i).start()
    hidden_share(0).start()
    gather_forward(1)
    gather_start(2)

    def inward(i, _):
        lo_i, t_i = chip(i)
        hidden_share(i).wait_recv()

        @pl.when(i == 0)
        def _():
            gather_finish(0)

        h = h2[lo_i, t_i].reshape(both, model)
        gate = plain(h, weight(0))
        h2_t[:, columns(i)] = h.T

        @pl.when(i == 0)
        def _():
            gather_finish(1)

        up = plain(h, weight(1))
        sigmoid_gate = jax.nn.sigmoid(gate)
        silu_gate = gate * sigmoid_gate
        hid[i] = (silu_gate * up).astype(BF)
        slope = sigmoid_gate * (1.0 + gate * (1.0 - sigmoid_gate))
        gate_back[i] = (up * slope).astype(BF)
        up_back[i] = silu_gate.astype(BF)

        @pl.when(i < 3)
        def _():
            hidden_copy(i + 1).wait_recv()
            hidden_share(i + 1).start()

        return 0

    def gradient(target, left_t, right):
        flat = right.shape[0] * right.shape[1]
        step_rows = model // 4

        def some(m, _):
            r = pl.ds(pl.multiple_of(m * step_rows, step_rows), step_rows)
            value = plain(left_t[r, :], right[...].reshape(flat, inner))
            target[m] = value.astype(BF).reshape(target.shape[1:])
            return 0

        lax.fori_loop(0, 4, some, 0)

    def ring_sums(n, target):
        def along_z(position, piece, count):
            return target.at[pl.ds(piece, count), position, 0]

        def along_y(position, piece, count):
            return target.at[position, pl.ds(piece, count), 1]

        return [
            RingSum(
                along,
                position,
                source,
                passing.at[n, half],
                got.at[n, half],
                [sem.at[n, half] for sem in (ca, cb, cc, cd)],
            )
            for half, (along, position, source) in enumerate(
                ((me.along_z, z, along_z), (me.along_y, y, along_y))
            )
        ]

    lax.fori_loop(0, 4, inward, 0)
    gather_forward(2)
    down_rings, gate_rings = ring_sums(0, gx), ring_sums(1, w.at[0])
    gradient(gx, dy_t, hid)
    for one in down_rings:
        one.start()
    gather_finish(2)

    def homeward(i):
        part_share(i).wait_recv()
        s1[i] = (s1[i].astype(F32) + r1[i].astype(F32)).astype(BF)

        @pl.when(i > 0)
        def _():
            part_copy(i).start()

    def outward(n, _):
        i = lax.rem(n + 1, 4)
        lo_i, t_i = chip(i)
        grad_inner = plain(dy[lo_i, t_i].reshape(both, model), weight(2))

        @pl.when(n > 0)
        def _():
            homeward(n)

        @pl.when(n == 2)
        def _():
            for one in down_rings:
                one.middle()

        gate_back[i] = (grad_inner * gate_back[i].astype(F32)).astype(BF)
        up_back[i] = (grad_inner * up_back[i].astype(F32)).astype(BF)
        whole[...] = (
            by_columns(gate_back[i], weight(0)) + by_columns(up_back[i], weight(1))
        ).reshape(2, rows, model)
        pb[i] = whole[1 - k].astype(BF)
        s1[i] = whole[k].astype(BF)
        part_share(i).start()
        return 0

    lax.fori_loop(0, 4, outward, 0)
    gradient(w.at[0], h2_t, gate_back)
    for one in gate_rings:
        one.start()

    homeward(0)

    grad = s1[0].astype(F32)
    for i in (1, 2, 3):
        part_copy(i).wait_recv()
        grad = grad + r2[i - 1].astype(F32)
    x = x1[...]
    factor = lax.rsqrt(jnp.mean(x * x, axis=-1, keepdims=True) + epsilon)
    normed = x * factor
    gnf[...] = jnp.sum(grad * normed, axis=0, keepdims=True)
    back = dy[lo, t, k].astype(F32) + norm_back(grad * gain[...], normed, factor)
    dx1[...] = back
    dxl[k, t] = back.astype(BF)
    block = dxl.at[k, t]
    across = send(block, block, gs.at[0], gr.at[0], me.in_ring(lo, 1 - t))
    rest = [send(block, block, gs.at[1], gr.at[1], me.sibling)]
    for one in gate_rings:
        one.middle()

    def result(i, _):
        whole[...] = by_columns(hid[i], weight(2)).reshape(2, rows, model)
        part_share(i).wait_send()
        pb[i] = whole[1 - k].astype(BF)
        ysum[i] = whole[k].astype(BF)
        result_share(i).start()
        return 0

    lax.fori_loop(0, 4, result, 0)

    gradient(w.at[1], h2_t, up_back)
    last = pltpu.make_async_copy(w.at[1], up_grad, ls.at[0])
    last.start()
    rest.append(last)
    across.wait()
    block = dxl.at[k, 1 - t]
    rest.append(send(block, block, gs.at[2], gr.at[2], me.sibling))
    for i in range(4):
        result_share(i).wait()
        ysum[i] = (ysum[i].astype(F32) + ry[i].astype(F32)).astype(BF)
        hidden_share(i).wait_send()
    for i in (1, 2, 3):
        hidden_copy(i).wait_send()
        part_copy(i).wait_send()
    for half in (0, 1):
        down_sum[half] = down_rings[half].finish().astype(BF)
    for half in (0, 1):
        gate_sum[half] = gate_rings[half].finish().astype(BF)
    for copy in rest:
        copy.wait()


def block(part, tok, gain, dy, halves):
    rows, model = tok.shape
    half_rows, hidden = halves.shape[-2:]
    sums = halves.shape[1:]
    weights = (3, 4, 4, 2, half_rows, hidden)
    any_place = pl.BlockSpec(memory_space=pl.ANY)
    quarter = pltpu.VMEM((4, rows, model), BF)
    inner = pltpu.VMEM((4, 2 * rows, hidden), BF)
    flipped = pltpu.VMEM((model, 8 * rows), BF)
    return pl.pallas_call(
        block_kernel,
        out_shape=[
            shape((rows, model), F32),
            shape((rows, model), F32),
            shape((2, 2, rows, model), BF),
            shape((1, model), F32),
            shape((4, rows, model), BF),
            shape(sums, BF),
            shape(sums, BF),
            shape(weights[1:], BF),
        ],
        in_specs=[VM] * 3 + [any_place] * 2,
        out_specs=[VM] * 7 + [any_place],
        scratch_shapes=[
            pltpu.VMEM(weights, BF),
            pltpu.VMEM(dy.shape, BF),
            flipped,
            pltpu.VMEM(dy.shape, BF),
            flipped,
            inner,
            inner,
            inner,
            pltpu.VMEM((2, rows, model), F32),
            quarter,
            quarter,
            quarter,
            pltpu.VMEM((3, rows, model), BF),
            quarter,
            pltpu.VMEM((2, 2, 2, 2, half_rows, hidden), BF),
            pltpu.VMEM((2, 2, 2, 4, half_rows, hidden), BF),
            pltpu.VMEM(weights[1:], BF),
            DMA((3, 2, 4, 2)),
            DMA((3, 2, 4, 2)),
            DMA((3, 2, 4)),
            DMA((3, 2, 4)),
            DMA((2, 2, 2)),
            DMA((2, 2, 2)),
            DMA((2, 2, 2)),
            DMA((2, 2, 2)),
            DMA((7,)),
            DMA((4,)),
            DMA((3,)),
            DMA((3,)),
            DMA((4,)),
            DMA((4,)),
            DMA((4,)),
            DMA((4,)),
            DMA((3,)),
            DMA((3,)),
            DMA((4,)),
            DMA((4,)),
            DMA((3,)),
            DMA((3,)),
        ],
        compiler_params=pltpu.CompilerParams(
            collective_id=3, has_side_effects=True, vmem_limit_bytes=62 << 20
        ),
    )(part, tok, gain, dy, halves)


def rear_kernel(
    heads,
    lse, start_ref, cosines, sines, tok, gain, gnf, *more,
):
    far, outs, near_refs, rest_refs = more[:13], more[13:22], more[22:35], more[35:]
    q_grad, k_grad, v_grad, o_grad, norm_sum, bias_sum, ffn_all, out, grad = outs
    g, gate_sum, down_sum, ysum, dxl, attn, exact, q, kv, x1, ob, h1, dx1 = near_refs
    (
    a_all, ext_all, do, dots, acc, keep, give, arrived, sums, landed, back, part, m1, m2, m3, left_t, ga,
    own, passing, got, p2, q1, sm, q2, fin, fin_w, e0, e1, es, e2, y2,
    ls, d1, d2, d3, d4, ms, ca, cb, cc, cd, fs2, fr2, as1, ar1, as2, ar2, as3, ar3, xs, xr, ss, sr, ts, tr, ys, yr,
    gs, gr,
    ) = rest_refs
    me = Place()
    y, z, lo, k, t = me.y, me.z, me.lo, me.k, me.t
    c = lo * 2 + k
    index = z * 2 + lo
    rows, width = q.shape
    size = width // heads
    slice_rows, model = tok.shape
    rowed = width + size
    offsets = (2, 1, 3)

    def in_x(dt, dc):
        return {"ctx": lax.rem(c + dc, 4), "tp": lax.rem(t + dt, 2)}

    def owner(b):
        return {"fsdp": y * 4 + b // 2, "ctx": lax.rem(b, 2) * 2 + k}

    ring = [(dt, dc) for dt in (0, 1) for dc in range(4) if dt or dc]

    summed_once = (gate_sum, own, down_sum)

    def second_hop(w, half, j):
        if half == 0:
            source, device = summed_once[w].at[0, lax.rem(y + j, 4)], me.along_y(j)
        else:
            source, device = summed_once[w].at[1, lax.rem(z + j, 4)], me.along_z(j)
        return describe(
            source, p2.at[w, half, j - 1], fs2.at[w, half, j - 1], fr2.at[w, half, j - 1], device
        )

    def second_hops(w, half):
        for j in offsets:
            second_hop(w, half, j).start()

    def up_along_z(position, piece, count):
        return g.at[pl.ds(piece, count), position, 0]

    def up_along_y(position, piece, count):
        return g.at[position, pl.ds(piece, count), 1]

    up_rings = [
        RingSum(
            along,
            position,
            source,
            passing.at[half],
            got.at[half],
            [sem.at[half] for sem in (ca, cb, cc, cd)],
        )
        for half, (along, position, source) in enumerate(
            ((me.along_z, z, up_along_z), (me.along_y, y, up_along_y))
        )
    ]

    def up_end(half):
        own[half] = up_rings[half].finish().astype(BF)
        second_hops(1, half)

    def early():
        for one in up_rings:
            one.middle()

    loads = [
        pltpu.make_async_copy(source, target, ls.at[i])
        for i, (source, target) in enumerate(zip(far, near_refs, strict=True))
    ]
    for copy in loads:
        copy.start()
    greet(
        [me.along_z(j) for j in (1, 2, 3)]
        + [me.along_y(j) for j in (1, 2, 3)]
        + [in_x(dt, dc) for dt, dc in ring]
        + [{"fsdp": y * 4 + lax.rem(z + j, 4), "ctx": (1 - lo) * 2 + k} for j in (1, 2, 3)]
    )
    loads[0].wait()
    for one in up_rings:
        one.start()
    for copy in loads[1:4]:
        copy.wait()
    for half in (0, 1):
        second_hops(0, half)
        second_hops(2, half)
    near = [(1 - lo, t), (1 - lo, 1 - t), (lo, 1 - t)]
    results = [
        send(ysum.at[i + 1], y2.at[i], ys.at[i], yr.at[i], me.in_ring(*near[i])) for i in range(3)
    ]

    for copy in loads[4:9]:
        copy.wait()
    do[...] = plain(dxl[...], attn[:, rowed:]).astype(BF)
    for h in range(heads):
        product = exact[h] * do[:, h * size : (h + 1) * size].astype(F32).T
        dots[h : h + 1] = jnp.sum(product, axis=0, keepdims=True)
    acc[...] = jnp.zeros_like(acc)
    start = start_ref[...]
    first = index * rows

    def core_share(b):
        return describe(give.at[b], arrived.at[b], d1.at[b], d2.at[b], me.sibling)

    def home(b):
        return describe(sums.at[b], landed.at[index], d3.at[b], d4.at[index], owner(b))

    def step(b, _):
        keys = kv[0, b]
        values = kv[1, b]
        seen = visible_pairs(b, first, start, rows)
        dk = jnp.zeros((KEYS, size), F32)
        dv = jnp.zeros((KEYS, size), F32)
        for h in range(heads):
            q_h = q[:, h * size : (h + 1) * size]
            do_h = do[:, h * size : (h + 1) * size]
            s = jnp.where(seen, by_columns(keys, q_h), masked_score)
            p = jnp.exp(s - lse[h : h + 1])
            dv = dv + plain(p.astype(BF), do_h)
            dp = by_columns(values, do_h)
            ds = (p * (dp - dots[h : h + 1])).astype(BF)
            dk = dk + plain(ds, q_h)
            acc[h] = acc[h] + over_rows(keys, ds)
        keep[b] = jnp.where(k == 0, dk, dv)
        give[b] = jnp.where(k == 0, dv, dk)
        core_share(b).start()

        @pl.when(b > 0)
        def _():
            @pl.when(b == 1)
            def _():
                early()

            core_share(b - 1).wait_recv()
            sums[b - 1] = (keep[b - 1] + arrived[b - 1]).astype(BF)
            home(b - 1).start()

        return 0

    lax.fori_loop(0, index + 1, step, 0)

    @pl.when(index < 1)
    def _():
        early()


    for copy in loads[9:]:
        copy.wait()
    result = x1[...] + ysum[0].astype(F32)
    for i in range(3):
        results[i].wait()
        result = result + y2[i].astype(F32)
    out[t] = result.astype(BF)
    mine = out.at[t]
    rest = [send(mine, mine, gs.at[1], gr.at[1], me.in_ring(lo, 1 - t))]
    up_end(1)
    up_end(0)

    scale = 1.0 / math.sqrt(size)
    for h in range(heads):
        dq = turned(acc[h].T * scale, cosines[...], -sines[...])
        e0[2:3, h * size : (h + 1) * size] = jnp.sum(dq, axis=0, keepdims=True)
        back[:, h * size : (h + 1) * size] = dq.astype(BF)
    left_t[...] = dxl[...].T
    blocks = ga.shape[:4]

    def spread(value):
        return value.astype(BF).reshape(blocks + (value.shape[1],))

    ga[:, :, :, :, rowed:] = spread(plain(left_t[...], ob[...]))
    left_t[...] = h1[...].T
    ga[:, :, :, :, :width] = spread(plain(left_t[...], back[:, :width]))

    core_share(index).wait_recv()
    dkv = keep[index] + arrived[index]
    keep[index] = dkv
    for b in range(1, 8):

        @pl.when(b > index)
        def _():
            describe(sums.at[0], landed.at[b], d3.at[0], d4.at[b], owner(0)).wait_recv()
            keep[index] = keep[index] + landed[b].astype(F32)

    is_key = k == 0
    dkv = turned(
        keep[index], jnp.where(is_key, cosines[...], 1.0), jnp.where(is_key, -sines[...], 0.0)
    )
    e0[2:3, width:rowed] = jnp.sum(dkv, axis=0, keepdims=True)
    back[:, width:] = dkv.astype(BF)
    part[...] = (
        by_columns(back[...], attn[:, :rowed]).astype(BF).reshape(2, 2, slice_rows, model)
    )
    cores = send(part.at[1 - k], m1, ms.at[0], ms.at[1], me.sibling)
    ga[:, :, :, :, width:rowed] = spread(plain(left_t[...], back[:, width:]))

    large = []
    for j in offsets:
        large.append(
            send(
                ga.at[:, lax.rem(z + j, 4), 0], q1.at[0, j - 1], as1.at[0, j - 1], ar1.at[0, j - 1], me.along_z(j)
            )
        )
        large.append(
            send(
                ga.at[lax.rem(y + j, 4), :, 1], q1.at[1, j - 1], as1.at[1, j - 1], ar1.at[1, j - 1], me.along_y(j)
            )
        )

    cores.wait()
    m2[...] = (part[k, 1 - t].astype(F32) + m1[1 - t].astype(F32)).astype(BF)
    across = send(m2, m3, ms.at[2], ms.at[3], me.in_ring(lo, 1 - t))
    quarter = sm.shape[2] // 2

    def summed(w, half):
        for j in offsets:
            second_hop(w, half, j).wait()
        here = summed_once[w][0, y] if half == 0 else summed_once[w][1, z]
        total = here.astype(F32)
        for j in range(3):
            total = total + p2[w, half, j].astype(F32)
        return total

    def to_owners(w):
        for half in (0, 1):
            total = summed(w, half)
            fin_w[w, 2 * half] = total[:quarter]
            fin_w[w, 2 * half + 1] = total[quarter:]
        width = fin_w.shape[3]
        place = pl.ds(pl.multiple_of(c * width, 128), width)
        ffn_all[w, :, place] = fin_w[w, c]
        return [
            send(
                fin_w.at[w, lax.rem(c + j, 4)], ffn_all.at[w, :, place], ts.at[w, j - 1], tr.at[w, j - 1], in_x(0, j)
            )
            for j in (2, 1, 3)
        ]

    rest += to_owners(2) + to_owners(0) + to_owners(1)

    x = tok[...].astype(F32)
    factor = lax.rsqrt(jnp.mean(x * x, axis=-1, keepdims=True) + epsilon)
    normed = x * factor
    dh1 = part[k, t].astype(F32) + m1[t].astype(F32)
    across.wait()
    dh1 = dh1 + m3[...].astype(F32)
    e0[0:1] = jnp.sum(dh1 * normed, axis=0, keepdims=True)
    e0[1:2] = gnf[...]
    e0[2:3, rowed:] = jnp.zeros((1, model - rowed), F32)
    e0[3:] = jnp.zeros((5, model), F32)
    small = [
        send(e0, e1.at[j - 1], ss.at[0, j - 1], sr.at[0, j - 1], me.along_z(j)) for j in offsets
    ]
    grad[t] = (dx1[...] + norm_back(dh1 * gain[...], normed, factor)).astype(BF)
    mine = grad.at[t]
    rest.append(send(mine, mine, gs.at[0], gr.at[0], me.in_ring(lo, 1 - t)))

    for copy in large:
        copy.wait()
    for half in (0, 1):
        here = ga[:, z, 0] if half == 0 else ga[y, :, 1]
        total = here.astype(F32)
        for j in range(3):
            total = total + q1[half, j].astype(F32)
        sm[half] = total.astype(BF)
    last = []
    for j in offsets:
        last.append(
            send(
                sm.at[0, lax.rem(y + j, 4)], q2.at[0, j - 1], as2.at[0, j - 1], ar2.at[0, j - 1], me.along_y(j)
            )
        )
        last.append(
            send(
                sm.at[1, lax.rem(z + j, 4)], q2.at[1, j - 1], as2.at[1, j - 1], ar2.at[1, j - 1], me.along_z(j)
            )
        )
    for copy in small:
        copy.wait()
    es[...] = (e0[...] + e1[0]) + (e1[1] + e1[2])
    small = [
        send(es, e2.at[j - 1], ss.at[1, j - 1], sr.at[1, j - 1], me.along_y(j)) for j in offsets
    ]

    for copy in last:
        copy.wait()
    for half in (0, 1):
        here = sm[0, y] if half == 0 else sm[1, z]
        total = here.astype(F32)
        for j in range(3):
            total = total + q2[half, j].astype(F32)
        fin[2 * half] = total[:quarter]
        fin[2 * half + 1] = total[quarter:]
    a_all[c] = fin[c]
    rest += [
        send(fin.at[lax.rem(c + j, 4)], a_all.at[c], as3.at[j - 1], ar3.at[j - 1], in_x(0, j))
        for j in (2, 1, 3)
    ]
    for copy in small:
        copy.wait()
    ext_all[t, c] = (es[...] + e2[0]) + (e2[1] + e2[2])
    mine = ext_all.at[t, c]
    rest += [
        send(mine, mine, xs.at[i], xr.at[i], in_x(dt, dc)) for i, (dt, dc) in enumerate(ring)
    ]

    def sent(b, _):
        core_share(b).wait_send()

        @pl.when(b < index)
        def _():
            home(b).wait_send()

        return 0

    lax.fori_loop(0, index + 1, sent, 0)
    for copy in rest:
        copy.wait()
    total = ext_all[0, 0]
    for i in range(1, 8):
        total = total + ext_all[i // 4, i % 4]
    norm_sum[...] = total
    for core in (0, 1):
        bias_sum[core] = ext_all[t, core] + ext_all[t, 2 + core]
        total = a_all[core] + a_all[2 + core]
        place = slice(core * width, (core + 1) * width)
        q_grad[:, place] = total[:, :width]
        (k_grad, v_grad)[core][...] = total[:, width:rowed]
        o_grad[:, place] = total[:, rowed:]


def rear(heads, g, gate_sum, down_sum, dxl, attn, q, kv, exact, lse, start, ob, h1, cosines, sines, ysum, x1, dx1, tok, gain, gnf):
    rows, width = q.shape
    size = width // heads
    slice_rows, model = tok.shape
    hidden = g.shape[-1]
    total = attn.shape[1]
    half_rows = model // 32
    quarter = half_rows // 2
    shared = pltpu.VMEM(kv.shape[1:], F32)
    shared_low = pltpu.VMEM(kv.shape[1:], BF)
    slab = pltpu.VMEM((slice_rows, model), BF)
    args = (lse, start, cosines, sines, tok, gain, gnf)
    far = (g, gate_sum, down_sum, ysum, dxl, attn, exact, q, kv, x1, ob, h1, dx1)
    outs = [
        shape((quarter, 2 * width), F32),
        shape((quarter, size), F32),
        shape((quarter, size), F32),
        shape((quarter, 2 * width), F32),
        shape((8, model), F32),
        shape((2, 8, model), F32),
        shape((3, quarter, 4 * hidden), F32),
        shape((2, slice_rows, model), BF),
        shape((2, slice_rows, model), BF),
    ]
    return pl.pallas_call(
        functools.partial(rear_kernel, heads),
        out_shape=outs,
        in_specs=[VM] * len(args) + [pl.BlockSpec(memory_space=pl.ANY)] * len(far),
        out_specs=[VM] * len(outs),
        scratch_shapes=[pltpu.VMEM(array.shape, array.dtype) for array in far]
        + [
            pltpu.VMEM((4, quarter, total), F32),
            pltpu.VMEM((2, 4, 8, model), F32),
            pltpu.VMEM((rows, width), BF),
            pltpu.VMEM((8, rows), F32),
            pltpu.VMEM((heads, size, rows), F32),
            shared,
            shared,
            shared,
            shared_low,
            shared_low,
            pltpu.VMEM((rows, width + size), BF),
            pltpu.VMEM((2, 2, slice_rows, model), BF),
            pltpu.VMEM((2, slice_rows, model), BF),
            slab,
            slab,
            pltpu.VMEM((model, rows), BF),
            pltpu.VMEM((4, 4, 2, half_rows, total), BF),
            pltpu.VMEM((2, 4, half_rows, hidden), BF),
            pltpu.VMEM((2, 2, 2, half_rows, hidden), BF),
            pltpu.VMEM((2, 2, 4, half_rows, hidden), BF),
            pltpu.VMEM((3, 2, 3, half_rows, hidden), BF),
            pltpu.VMEM((2, 3, 4, half_rows, total), BF),
            pltpu.VMEM((2, 4, half_rows, total), BF),
            pltpu.VMEM((2, 3, half_rows, total), BF),
            pltpu.VMEM((4, quarter, total), F32),
            pltpu.VMEM((3, 4, quarter, hidden), F32),
            pltpu.VMEM((8, model), F32),
            pltpu.VMEM((3, 8, model), F32),
            pltpu.VMEM((8, model), F32),
            pltpu.VMEM((3, 8, model), F32),
            pltpu.VMEM((3, slice_rows, model), BF),
            DMA((13,)),
            DMA((8,)),
            DMA((8,)),
            DMA((8,)),
            DMA((8,)),
            DMA((4,)),
            DMA((2, 2)),
            DMA((2, 2)),
            DMA((2, 2)),
            DMA((2, 2)),
            DMA((3, 2, 3)),
            DMA((3, 2, 3)),
            DMA((2, 3)),
            DMA((2, 3)),
            DMA((2, 3)),
            DMA((2, 3)),
            DMA((3,)),
            DMA((3,)),
            DMA((7,)),
            DMA((7,)),
            DMA((2, 3)),
            DMA((2, 3)),
            DMA((3, 3)),
            DMA((3, 3)),
            DMA((3,)),
            DMA((3,)),
            DMA((2,)),
            DMA((2,)),
        ],
        compiler_params=pltpu.CompilerParams(
            collective_id=7, has_side_effects=True, vmem_limit_bytes=62 << 20
        ),
    )(*args, *far)


def shards(
    tokens,
    segments,
    w_query,
    key_matrix,
    value_matrix,
    b_query,
    key_bias_vector,
    value_bias_vector,
    w_out,
    norm_attn,
    norm_ffn,
    w_gate,
    w_up,
    w_down,
    cotangent,
):
    f = lax.axis_index("fsdp")
    c = lax.axis_index("ctx")
    t = lax.axis_index("tp")
    k = c % 2
    is_key = k == 0
    size = key_matrix.shape[1]
    query_width = w_query.shape[1] // 2
    heads = query_width // size
    own_width = query_width + size
    model = tokens.shape[1]
    count = tokens.shape[0]
    slice_rows = count // 2
    shard_rows = w_query.shape[0]
    hidden = w_gate.shape[1] // 4
    padded = -(-hidden // 128) * 128

    def hidden_slice(w, axis):
        widths = [(0, 0), (0, 0)]
        widths[axis] = (0, 4 * padded - 4 * hidden)
        return lax.dynamic_slice_in_dim(jnp.pad(w, widths), c * padded, padded, axis)

    own_ffn = jnp.stack(
        [
            hidden_slice(w_gate, 1),
            hidden_slice(w_up, 1),
            hidden_slice(w_down, 0).T,
        ]
    )

    own_attn = jnp.concatenate(
        [
            lax.dynamic_slice_in_dim(w_query, k * query_width, query_width, 1),
            jnp.where(is_key, key_matrix, value_matrix),
            lax.dynamic_slice_in_dim(w_out, k * query_width, query_width, 0).T,
        ],
        axis=1,
    )
    own_tokens = lax.dynamic_slice_in_dim(tokens, t * slice_rows, slice_rows, 0)
    rows = 2 * count
    half_size = size // 2
    frequency = np.exp(np.arange(half_size) * (-2.0 * math.log(rope_base) / size))
    frequency = jnp.asarray(np.concatenate([frequency, frequency])[None].astype(np.float32))
    gain_attn = norm_attn.astype(F32)[None]
    gain_ffn = norm_ffn.astype(F32)[None]
    bias = jnp.concatenate(
        [
            lax.dynamic_slice_in_dim(b_query, k * query_width, query_width, 0),
            jnp.where(is_key, key_bias_vector, value_bias_vector),
        ]
    ).astype(F32)[None]
    (
        attn_all,
        halves,
        dy_all,
        h1,
        q,
        kv,
        exact,
        ob,
        lse,
        starts,
        cosines,
        sines,
        part,
    ) = front(heads, own_attn, own_ffn, tokens, cotangent, segments, gain_attn, bias, frequency)
    x1, dx1, dxl, grad_norm_two, ysum, gate_sum, down_sum, up_grad = block(
        part, own_tokens, gain_ffn, dy_all, halves
    )
    q_grad, k_grad, v_grad, o_grad, norm_sum, bias_sum, ffn_all, output, grad_tokens = rear(
        heads,
        up_grad,
        gate_sum,
        down_sum,
        dxl.reshape(rows, model),
        attn_all.reshape(model, own_width + query_width),
        q,
        kv,
        exact,
        lse,
        starts,
        ob,
        h1,
        cosines,
        sines,
        ysum,
        x1,
        dx1,
        own_tokens,
        gain_attn,
        grad_norm_two,
    )
    owner_rows = shard_rows // 4

    owner = f * 4 + c
    norms = lax.dynamic_slice_in_dim(norm_sum[:2], owner * owner_rows, owner_rows, 1)
    biases = bias_sum[:, 2, :own_width].reshape(2, heads + 1, size)
    biases = lax.dynamic_slice_in_dim(biases, owner * 2, 2, 2)
    return (
        output.reshape(count, model),
        grad_tokens.reshape(count, model).astype(F32),
        q_grad,
        k_grad,
        v_grad,
        biases[:, :heads].reshape(2 * heads, 2),
        biases[0, heads:],
        biases[1, heads:],
        o_grad.T,
        norms[0],
        norms[1],
        ffn_all[0, :, : 4 * hidden],
        ffn_all[1, :, : 4 * hidden],
        ffn_all[2, :, : 4 * hidden].T,
    )


def solution(mesh):
    both = ("fsdp", "ctx")
    in_specs = (
        P(both, None),
        P(),
        P("fsdp", "tp"),
        P("fsdp", "tp"),
        P("fsdp", "tp"),
        P("tp"),
        P("tp"),
        P("tp"),
        P("tp", "fsdp"),
        P(),
        P(),
        P("fsdp", "tp"),
        P("fsdp", "tp"),
        P("tp", "fsdp"),
        P(both, None),
    )
    out_specs = (
        P(both, None),
        P(both, None),
        P(both, "tp"),
        P(both, "tp"),
        P(both, "tp"),
        P("tp", both),
        P("tp", both),
        P("tp", both),
        P("tp", both),
        P(both),
        P(both),
        P(both, "tp"),
        P(both, "tp"),
        P("tp", both),
    )
    return jax.shard_map(shards, mesh=mesh, in_specs=in_specs, out_specs=out_specs, check_vma=False)
```
